32 devices in a mesh: gx: 8 (over z, x), gy: 4 (over y, core).
Axes of the slice: x: 2, y: 2, z: 4, core: 2. Of those that a mesh axis runs over, the one named last changes fastest.
Arguments:
- checkpoint: float32 [27, 8, 32, 512], P(None, None, 'gx', 'gy'), may hold values from 0.0027 to 0.415, as said below
- rates: float32 [27], replicated, may hold values from 0.8 to 1.7
- wall_mask: int32 [8, 32, 512], P(None, 'gx', 'gy'), may hold values 0 or 1
- cotangent: float32 [27, 8, 32, 512], P(None, None, 'gx', 'gy'), may hold values from -6 to 6
Outputs:
- grad_checkpoint: float32 [27, 8, 32, 512], P(None, None, 'gx', 'gy')
The draws below stay inside these ranges and needn't reach their ends.
Inputs may be any that keep to these rules, and one draw needn't show every extreme that they name: `checkpoint`: each population lies between 0.6 and 1.4 times its lattice weight.
All inputs are finite; a program needn't handle non-finite values. No bound on the sum of `wall_mask` on one device may be relied on, other than what follows from the above.
Results may differ from the reference program's by a relative error of at most 0.00009.
Values sent between devices are 32-bit elements; how exact they have to be, the bound alone decides.
No kernel may reach another device: no remote copies, remote signals or barrier semaphores. Data moves between devices by JAX's collectives and lax.ppermute only.
A program may use at most 64 MiB of HBM per device.

```python
import math
import jax
import jax.numpy as jnp
import numpy as np
from jax import lax

NZ = 8
NX = 32
NY = 512


def lattice_weights():
    signs = (-1, 0, 1)
    table = [8.0 / 27.0, 2.0 / 27.0, 1.0 / 54.0, 1.0 / 216.0]
    return [table[abs(a) + abs(b) + abs(c)] for a in signs for b in signs for c in signs]


def draw_checkpoint(key, part):
    weights = jnp.asarray(lattice_weights(), jnp.float32).reshape(27, 1, 1, 1)
    random_part = jax.random.uniform(key, (27, NZ, NX, NY), jnp.float32)
    factor = 0.6 + 0.8 * random_part
    return weights * factor


def with_ends(entries, rng, smallest, top_value):
    index_at = [jax.random.randint(jax.random.fold_in(rng, axis), (), 0, length) for axis, length in enumerate(entries.shape)]
    longest = entries.shape.index(max(entries.shape))
    neighbour = index_at[:longest] + [(index_at[longest] + 1) % entries.shape[longest]] + index_at[longest + 1:]
    return entries.at[tuple(index_at)].set(smallest).at[tuple(neighbour)].set(top_value)


def level_of(rng, extent, cuts, least, high):
    level = 1.0
    for dim, blocks in cuts:
        steps = jax.random.uniform(jax.random.fold_in(jax.random.fold_in(rng, 6), dim), (blocks,), jnp.float32, least / len(cuts), high / len(cuts))
        level = level * jnp.repeat(jnp.exp(steps), extent[dim] // blocks).reshape((-1,) + (1,) * (len(extent) - 1 - dim))
    return level


def noise(key, dims, deviation, limit, split=(), held_as=jnp.bfloat16):
    values = deviation * jax.random.normal(key, dims, jnp.float32)
    if split:
        values = values * level_of(key, dims, split, -0.22, 0.18)
    return jnp.clip(values, -limit, limit).astype(held_as)


def setup_inputs(seed: int = 0) -> dict:
    arg_keys = jax.random.split(jax.random.key(seed), 5)
    checkpoint = draw_checkpoint(jax.random.fold_in(arg_keys[4], 71), 0)
    rates = jnp.clip(jnp.exp(jax.random.uniform(arg_keys[1], (27,), jnp.float32, math.log(0.8), math.log(1.7))), 0.8, 1.7)
    wall_mask = with_ends((jax.random.randint(arg_keys[2], (NZ, NX, NY), 0, 6) < 1).astype(jnp.int32), jax.random.fold_in(arg_keys[2], 1), 0, 1)
    cotangent = noise(arg_keys[3], (27, NZ, NX, NY), 1.0, 6.0, ((2, 8), (3, 4)), jnp.float32)
    return dict(checkpoint=checkpoint, rates=rates, wall_mask=wall_mask, cotangent=cotangent)


def lattice_tables():
    signs = (-1, 0, 1)
    velocity = [[a, b, c] for a in signs for b in signs for c in signs]
    table = [8.0 / 27.0, 2.0 / 27.0, 1.0 / 54.0, 1.0 / 216.0]
    weights = [table[abs(a) + abs(b) + abs(c)] for a in signs for b in signs for c in signs]
    powers = [[1.0, 1.0, 1.0], [-1.0, 0.0, 1.0], [1.0, 0.0, 1.0]]
    undo = [[0.0, -0.5, 0.5], [1.0, 0.0, -1.0], [0.0, 0.5, 0.5]]
    moment = np.kron(np.kron(powers, powers), powers)
    inverse = np.kron(np.kron(undo, undo), undo)
    return (velocity, weights, moment, inverse)

def collide(incoming, rates, wall_cells):
    velocity, weights, moment, inverse = lattice_tables()
    velocity = jnp.asarray(velocity, jnp.float32)
    weights = jnp.asarray(weights, jnp.float32)
    moment = jnp.asarray(moment, jnp.float32)
    inverse = jnp.asarray(inverse, jnp.float32)
    high = lax.Precision.HIGHEST
    populations = incoming.reshape(27, -1)
    density = lax.optimization_barrier(jnp.sum(populations, axis=0))
    momentum = jnp.dot(velocity.T, populations, precision=high)
    speeds = momentum / density
    projected = jnp.dot(velocity, speeds, precision=high)
    speed_sq = lax.optimization_barrier(jnp.sum(speeds * speeds, axis=0))
    equilibrium = weights[:, None] * density * (1.0 + 3.0 * projected + 4.5 * projected * projected - 1.5 * speed_sq)
    relaxation = jnp.dot(inverse, rates[:, None] * moment, precision=high)
    collided = populations - jnp.dot(relaxation, populations - equilibrium, precision=high)
    reflected = populations[::-1]
    solid = wall_cells.reshape(1, -1)
    return (collided + solid * (reflected - collided)).reshape(incoming.shape)

def wall_field(wall_mask):
    height = lax.broadcasted_iota(jnp.int32, wall_mask.shape, 0)
    boundary = (height == 0) | (height == wall_mask.shape[0] - 1)
    return jnp.where(boundary, 1, wall_mask).astype(jnp.float32)

def stream(field, direction):
    pieces = []
    for slot in range(27):
        step_x = direction * (slot // 9 - 1)
        step_y = direction * (slot // 3 % 3 - 1)
        step_z = direction * (slot % 3 - 1)
        pieces.append(jnp.roll(field[slot], (step_z, step_x, step_y), axis=(0, 1, 2)))
    return jnp.stack(pieces)

def reference(checkpoint, rates, wall_mask, cotangent):
    wall_cells = wall_field(wall_mask)
    collided = collide(checkpoint, rates, wall_cells)
    next_state = stream(collided, 1)
    back_one = stream(cotangent, -1)
    _, pullback = jax.vjp(lambda value: collide(value, rates, wall_cells), next_state)
    grad_next = pullback(back_one)[0]
    back_two = stream(grad_next, -1)
    _, pullback_first = jax.vjp(lambda value: collide(value, rates, wall_cells), checkpoint)
    return pullback_first(back_two)[0]
```

```python
import functools
import jax
import jax.numpy as jnp
from jax import lax
from jax.experimental import pallas as pl
from jax.experimental.pallas import tpu as pltpu
from jax.sharding import PartitionSpec as P

F32 = jnp.float32
SIGNS = (-1, 0, 1)
Q = [(a, b, c) for a in SIGNS for b in SIGNS for c in SIGNS]


def qi(a, b, c):
    return 9 * (a + 1) + 3 * (b + 1) + (c + 1)


def mi(i, j, k):
    return 9 * i + 3 * j + k


NNZ = [(i > 0) + (j > 0) + (k > 0) for i in range(3) for j in range(3) for k in range(3)]


def slots(rows):
    first, second, sums = [], [], []
    for q, (a, b, c) in enumerate(Q):
        for x in range(rows):
            left = (a >= 0 and x == 0) or (a == 1 and x == 1)
            right = (a <= 0 and x == rows - 1) or (a == -1 and x == rows - 2)
            (first if left or right else second).append((("v", q, x), b))
    for x in range(rows):
        second.append((("w", x), 0))
    for a in SIGNS:
        for b in SIGNS:
            for s in range(2):
                for x in range(rows):
                    sums.append((("s", a, b, s, x), -b))
    table = {}
    groups = [first + sums[64:], second, sums[:64]]
    for g, group in enumerate(groups):
        for i, (key, kind) in enumerate(group):
            table[key] = (g, 2 * i, kind)
    return table, 2 * len(first)


def turn(v, shift, axis):
    shift = shift % v.shape[axis]
    return v if shift == 0 else pltpu.roll(v, shift, axis)


def lanes():
    return lax.broadcasted_iota(jnp.int32, (8, 128), 1)


def outgoing(block, lane, kind):
    return turn(block, {0: lane + 1, 1: lane, -1: lane + 2}[kind], 1)


def incoming(packed, lane, kind):
    return turn(packed, {0: 127, 1: 0, -1: 126}[kind] - lane, 1)


def shift_y(main, outer, b, lane):
    if b == 0:
        return main, outer
    edge = lane == (127 if b == 1 else 0)
    rm, ro = turn(main, -b, 1), turn(outer, -b, 1)
    return jnp.where(edge, ro, rm), jnp.where(edge, rm, ro)


def along(values, pass_):
    values = list(values)
    for step in (1, 3, 9):
        for start in range(27):
            if (start // step) % 3 == 0:
                at = (start, start + step, start + 2 * step)
                for i, new in zip(at, pass_(*[values[j] for j in at])):
                    values[i] = new
    return values


def moments(values):
    def pass_(lo, mid, hi):
        both = lo + hi
        return both + mid, hi - lo, both
    return along(values, pass_)


def dual_moments(values):
    return along(values, lambda lo, mid, hi: (mid, hi - lo, (hi - mid) + (lo - mid)))


def from_moments(values):
    return along(values, lambda m0, m1, m2: (m2 - m1, m0 - (m2 + m2), m2 + m1))


def from_dual(values):
    def pass_(z0, z1, z2):
        both = z0 + z2
        return both - z1, z0, both + z1
    return along(values, pass_)


def collide(f, solid, scale):
    m = moments(f)
    rho = m[0]
    inverse = 1.0 / rho
    jx, jy, jz = m[mi(1, 0, 0)], m[mi(0, 1, 0)], m[mi(0, 0, 1)]
    ux, uy, uz = jx * inverse, jy * inverse, jz * inverse
    xx, yy, zz = jx * ux, jy * uy, jz * uz
    third = rho * (1.0 / 3.0)
    ninth = rho * (1.0 / 9.0)
    e = [None] * 27
    e[mi(2, 0, 0)], e[mi(0, 2, 0)], e[mi(0, 0, 2)] = third + xx, third + yy, third + zz
    e[mi(1, 1, 0)], e[mi(1, 0, 1)], e[mi(0, 1, 1)] = jx * uy, jx * uz, jy * uz
    jx3, jy3, jz3 = jx * (1.0 / 3.0), jy * (1.0 / 3.0), jz * (1.0 / 3.0)
    e[mi(1, 2, 0)] = e[mi(1, 0, 2)] = jx3
    e[mi(2, 1, 0)] = e[mi(0, 1, 2)] = jy3
    e[mi(2, 0, 1)] = e[mi(0, 2, 1)] = jz3
    e[mi(2, 2, 0)] = ninth + (xx + yy) * (1.0 / 3.0)
    e[mi(2, 0, 2)] = ninth + (xx + zz) * (1.0 / 3.0)
    e[mi(0, 2, 2)] = ninth + (yy + zz) * (1.0 / 3.0)
    e[mi(2, 1, 1)] = e[mi(0, 1, 1)] * (1.0 / 3.0)
    e[mi(1, 2, 1)] = e[mi(1, 0, 1)] * (1.0 / 3.0)
    e[mi(1, 1, 2)] = e[mi(1, 1, 0)] * (1.0 / 3.0)
    e[mi(1, 2, 2)], e[mi(2, 1, 2)], e[mi(2, 2, 1)] = jx * (1.0 / 9.0), jy * (1.0 / 9.0), jz * (1.0 / 9.0)
    e[mi(2, 2, 2)] = (third + (xx + yy + zz)) * (1.0 / 9.0)
    z = []
    for i in range(27):
        if i in (0, 1, 3, 9):
            z.append(jnp.zeros_like(rho))
        else:
            z.append((m[i] if e[i] is None else m[i] - e[i]) * scale[i])
    h = from_moments(z)
    out = [jnp.where(solid, f[26 - q], f[q] - h[q]) for q in range(27)]
    return out, (ux, uy, uz)


def pull_back(v, u, solid, scale):
    ux, uy, uz = u
    z = [y * s for y, s in zip(dual_moments(v), scale)]

    def at(i, j, k):
        return z[mi(i, j, k)]

    third = 1.0 / 3.0
    top = at(2, 2, 2) * third
    d_xy, d_xz, d_yz = at(2, 2, 0) + top, at(2, 0, 2) + top, at(0, 2, 2) + top
    q_xx = at(2, 0, 0) + (at(2, 2, 0) + d_xz) * third
    q_yy = at(0, 2, 0) + (at(0, 2, 2) + d_xy) * third
    q_zz = at(0, 0, 2) + (at(2, 0, 2) + d_yz) * third
    base = at(0, 0, 0) + (q_xx + (at(0, 2, 0) + at(0, 0, 2) + at(0, 2, 2) * third)) * third
    b_x = at(1, 0, 0) + (at(1, 2, 0) + at(1, 0, 2) + at(1, 2, 2) * third) * third
    b_y = at(0, 1, 0) + (at(2, 1, 0) + at(0, 1, 2) + at(2, 1, 2) * third) * third
    b_z = at(0, 0, 1) + (at(2, 0, 1) + at(0, 2, 1) + at(2, 2, 1) * third) * third
    q_xy = at(1, 1, 0) + at(1, 1, 2) * third
    q_xz = at(1, 0, 1) + at(1, 2, 1) * third
    q_yz = at(0, 1, 1) + at(2, 1, 1) * third
    p_x = (q_xx + q_xx) * ux + q_xy * uy + q_xz * uz
    p_y = q_xy * ux + (q_yy + q_yy) * uy + q_yz * uz
    p_z = q_xz * ux + q_yz * uy + (q_zz + q_zz) * uz
    quad = (p_x * ux + p_y * uy + p_z * uz) * 0.5
    z[0] = z[0] - (base - quad)
    z[mi(1, 0, 0)] = z[mi(1, 0, 0)] - (b_x + p_x)
    z[mi(0, 1, 0)] = z[mi(0, 1, 0)] - (b_y + p_y)
    z[mi(0, 0, 1)] = z[mi(0, 0, 1)] - (b_z + p_z)
    h = from_dual(z)
    return [jnp.where(solid, v[26 - q], v[q] - h[q]) for q in range(27)]


def scales(rates_ref):
    return [rates_ref[i] * (0.5 ** NNZ[i]) for i in range(27)]


def first_kernel(rows, rates, f, wall, cot, sums, speed, solid_out, packed):
    scale = scales(rates)
    plane = lax.broadcasted_iota(jnp.int32, (8, 128), 0)
    boundary = (plane == 0) | (plane == 7)
    lane = lanes()
    table, _ = slots(rows)
    for x in range(rows):
        at = pl.ds(x, 8, stride=rows)
        solid = boundary | (wall[at, :] == 1)
        solid_out[x] = jnp.where(solid, 1.0, 0.0)
        out, u = collide([f[q, at, :] for q in range(27)], solid, scale)
        for k in range(3):
            speed[k, x] = u[k]
        for a in SIGNS:
            for b in SIGNS:
                low = turn(out[qi(a, b, -1)], -1, 0)
                high = turn(out[qi(a, b, 1)], 1, 0)
                i = 2 * (3 * (a + 1) + b + 1)
                sums[i, x] = out[qi(a, b, 0)] + (low + high)
                sums[i + 1, x] = high - low
    pieces = [jnp.zeros((8, 128), F32) for _ in range(3)]
    for key, (g, i, kind) in table.items():
        if key[0] == "v":
            block = cot[key[1], pl.ds(key[2], 8, stride=rows), :]
        elif key[0] == "w":
            block = solid_out[key[1]]
        else:
            block = sums[2 * (3 * (key[1] + 1) + key[2] + 1) + key[3], key[4]]
        mine = (lane == i) | (lane == i + 1)
        pieces[g] = jnp.where(mine, outgoing(block, i, kind), pieces[g])
    for g in range(3):
        packed[g] = pieces[g]


def edge_rows(rows, side):
    near, far = (0, 1) if side == 1 else (rows - 1, rows - 2)
    keys = [(q, near) for q, c in enumerate(Q) if c[0] == 0]
    keys += [(q, near) for q, c in enumerate(Q) if c[0] == side]
    return keys + [(q, far) for q, c in enumerate(Q) if c[0] == side]


def second_kernel(rows, cot, sums, solid_in, from_left, from_right, to_left, to_right, own, merged):
    lane = lanes()
    table, used = slots(rows)
    halo = []
    for g in range(3):
        takes_left = jnp.zeros((8, 128), jnp.bool_)
        for key, (h, i, kind) in table.items():
            if h == g and kind <= 0:
                takes_left = takes_left | (lane == i)
            if h == g and kind == -1:
                takes_left = takes_left | (lane == i + 1)
        halo.append(jnp.where(takes_left, from_left[g], from_right[g]))
        merged[g] = halo[g]

    def outer(key):
        g, i, kind = table[key]
        return incoming(halo[g], i, kind)

    def both(a, x):
        parts = {}
        for b in SIGNS:
            for s in range(2):
                i = 2 * (3 * (a + 1) + b + 1) + s
                parts[b, s] = shift_y(sums[i, x], outer(("s", a, b, s, x)), -b, lane)
        result = []
        for n in range(2):
            result.append((
                parts[0, 0][n] + (parts[-1, 0][n] + parts[1, 0][n]),
                parts[1, 0][n] - parts[-1, 0][n],
                parts[0, 1][n] + (parts[-1, 1][n] + parts[1, 1][n]),
            ))
        return result

    t = {(a, x): both(a, x) for a in SIGNS for x in range(rows)}

    def total(x, n):
        terms = [(a, t[a, x - a][n]) for a in SIGNS if 0 <= x - a < rows]
        density = functools.reduce(jnp.add, [v[0] for _, v in terms])
        along_y = functools.reduce(jnp.add, [v[1] for _, v in terms])
        along_z = functools.reduce(jnp.add, [v[2] for _, v in terms])
        moving = [(a, v[0]) for a, v in terms if a]
        along_x = jnp.zeros((8, 128), F32)
        for a, v in moving:
            along_x = along_x + v if a == 1 else along_x - v
        return density, along_x, along_y, along_z

    for x in range(-1, rows + 1):
        for n in range(2):
            for k, v in enumerate(total(x, n)):
                own[k, 2 * (x + 1) + n] = v

    for side, message in ((1, to_left), (-1, to_right)):
        near, far = (0, 1) if side == 1 else (rows - 1, rows - 2)
        for k, (q, x) in enumerate(edge_rows(rows, side)):
            message[k] = cot[q, pl.ds(x, 8, stride=rows), :]
        extra = []
        for n in range(2):
            row = list(t[-side, near][n])
            still, moved = t[0, near][n], t[-side, far][n]
            row += [still[0] + moved[0], moved[0] if side == -1 else -moved[0]]
            row += [still[1] + moved[1], still[2] + moved[2]]
            row.append(solid_in[near] if n == 0 else outer(("w", near)))
            extra.append(row)
        columns = halo[0]
        for k in range(8):
            message[27 + k] = extra[0][k]
            i = used + 2 * k
            columns = jnp.where((lane == i) | (lane == i + 1), turn(extra[1][k], i + 1, 1), columns)
        message[35] = columns


def third_kernel(rows, rates, cot, speed, solid_in, own, merged, from_low, from_high, out, v1, g1, extra):
    scale = scales(rates)
    lane = lanes()
    table, used = slots(rows)
    ring = rows + 2
    remote = {}
    for side, message in ((1, from_high), (-1, from_low)):
        for k, (q, x) in enumerate(edge_rows(rows, side)):
            g, i, kind = table["v", q, x]
            remote[q, x + side * rows] = (message, k, i, kind)
    for q, (a, b, c) in enumerate(Q):
        for x in range(-1, rows + 1):
            source = x + a
            if 0 <= source < rows:
                main = cot[q, pl.ds(source, 8, stride=rows), :]
                g, i, kind = table["v", q, source]
                outer = incoming(merged[g], i, kind)
            else:
                message, k, i, kind = remote[q, source]
                main = message[k]
                outer = incoming(message[35], i, kind)
            main, outer = turn(main, -c, 0), turn(outer, -c, 0)
            main, outer = shift_y(main, outer, b, lane)
            v1[q, 2 * (x + 1)] = main
            v1[q, 2 * (x + 1) + 1] = outer
    for x in range(-1, rows + 1):
        for n in range(2):
            total = [own[k, 2 * (x + 1) + n] for k in range(4)]
            for side, message in ((1, from_high), (-1, from_low)):
                near = rows - 1 if side == 1 else 0

                def got(k):
                    if n == 0:
                        return message[27 + k]
                    return incoming(message[35], used + 2 * k, 0)

                if x == near:
                    total = [total[0] + got(0), total[1] - got(0) if side == 1 else total[1] + got(0),
                             total[2] + got(1), total[3] + got(2)]
                if x == near + side:
                    total = [total[k] + got(3 + k) for k in range(4)]
                    wall = got(7)
            if 0 <= x < rows:
                if n == 0:
                    wall = solid_in[x]
                else:
                    g, i, kind = table["w", x]
                    wall = incoming(merged[g], i, kind)
            inverse = 1.0 / total[0]
            for k in range(3):
                extra[k, 2 * (x + 1) + n] = total[k + 1] * inverse
            extra[3, 2 * (x + 1) + n] = wall

    def one(r, _):
        v = [v1[q, r] for q in range(27)]
        u = [extra[k, r] for k in range(3)]
        g = pull_back(v, u, extra[3, r] > 0.5, scale)
        for q in range(27):
            g1[q, r] = g[q]
        return 0

    lax.fori_loop(0, 2 * ring, one, 0)
    for x in range(rows):
        v = []
        for q, (a, b, c) in enumerate(Q):
            r = 2 * (x + a + 1)
            main = g1[q, r]
            if b:
                main = shift_y(main, g1[q, r + 1], b, lane)[0]
            v.append(turn(main, -c, 0))
        result = pull_back(v, [speed[k, x] for k in range(3)], solid_in[x] > 0.5, scale)
        for q in range(27):
            out[q, pl.ds(x, 8, stride=rows), :] = result[q]


def call(kernel, name, out_shapes, scratch, operands, smem_first):
    vmem = pl.BlockSpec(memory_space=pltpu.VMEM)
    specs = [vmem] * len(operands)
    if smem_first:
        specs[0] = pl.BlockSpec(memory_space=pltpu.SMEM)
    return pl.pallas_call(
        kernel,
        out_shape=[jax.ShapeDtypeStruct(s, F32) for s in out_shapes],
        in_specs=specs,
        out_specs=[vmem] * len(out_shapes),
        scratch_shapes=[pltpu.VMEM(s, F32) for s in scratch],
        compiler_params=pltpu.CompilerParams(vmem_limit_bytes=32 * 1024 * 1024),
        name=name,
    )(*operands)


def ring(block, axis, step):
    size = lax.axis_size(axis)
    return lax.ppermute(block, axis, [(i, (i + step) % size) for i in range(size)])


def shards(checkpoint, rates, wall_mask, cotangent):
    planes, rows, width = checkpoint.shape[1:]
    f = checkpoint.reshape(27, planes * rows, width)
    cot = cotangent.reshape(27, planes * rows, width)
    wall = wall_mask.reshape(planes * rows, width)
    tile = (planes, width)
    sums, speed, solid, packed = call(
        functools.partial(first_kernel, rows), "collide",
        [(18, rows) + tile, (3, rows) + tile, (rows,) + tile, (3,) + tile], [],
        (rates, f, wall, cot), True)
    from_right = ring(packed, "gy", -1)
    from_left = ring(packed, "gy", 1)
    to_left, to_right, own, merged = call(
        functools.partial(second_kernel, rows), "pack",
        [(36,) + tile, (36,) + tile, (4, 2 * rows + 4) + tile, (3,) + tile], [],
        (cot, sums, solid, from_left, from_right), False)
    from_high = ring(to_left, "gx", -1)
    from_low = ring(to_right, "gx", 1)
    (out,) = call(
        functools.partial(third_kernel, rows), "gradient",
        [(27, planes * rows, width)],
        [(27, 2 * rows + 4) + tile, (27, 2 * rows + 4) + tile, (4, 2 * rows + 4) + tile],
        (rates, cot, speed, solid, own, merged, from_low, from_high), True)
    return out.reshape(checkpoint.shape)


def solution(mesh):
    in_specs = (P(None, None, "gx", "gy"), P(), P(None, "gx", "gy"), P(None, None, "gx", "gy"))
    out_specs = P(None, None, "gx", "gy")
    return jax.shard_map(shards, mesh=mesh, in_specs=in_specs, out_specs=out_specs, check_vma=False)
```

```python
import functools
import jax
import jax.numpy as jnp
from jax import lax
from jax.experimental import pallas as pl
from jax.experimental.pallas import tpu as pltpu
from jax.sharding import PartitionSpec as P

F32 = jnp.float32
SIGNS = (-1, 0, 1)
Q = [(a, b, c) for a in SIGNS for b in SIGNS for c in SIGNS]


def qi(a, b, c):
    return 9 * (a + 1) + 3 * (b + 1) + (c + 1)


def mi(i, j, k):
    return 9 * i + 3 * j + k


NNZ = [(i > 0) + (j > 0) + (k > 0) for i in range(3) for j in range(3) for k in range(3)]


def slots(rows):
    first, second, sums = [], [], []
    for q, (a, b, c) in enumerate(Q):
        for x in range(rows):
            left = (a >= 0 and x == 0) or (a == 1 and x == 1)
            right = (a <= 0 and x == rows - 1) or (a == -1 and x == rows - 2)
            (first if left or right else second).append((("v", q, x), b))
    for x in range(rows):
        second.append((("w", x), 0))
    for a in SIGNS:
        for b in SIGNS:
            for s in range(2):
                for x in range(rows):
                    sums.append((("s", a, b, s, x), -b))
    table = {}
    groups = [first + sums[64:], second, sums[:64]]
    for g, group in enumerate(groups):
        for i, (key, kind) in enumerate(group):
            table[key] = (g, 2 * i, kind)
    return table, 2 * len(first)


def turn(v, shift, axis):
    shift = shift % v.shape[axis]
    return v if shift == 0 else pltpu.roll(v, shift, axis)


def lanes():
    return lax.broadcasted_iota(jnp.int32, (8, 128), 1)


def outgoing(block, lane, kind):
    return turn(block, {0: lane + 1, 1: lane, -1: lane + 2}[kind], 1)


def incoming(packed, lane, kind, b=0):
    return turn(packed, {0: 127, 1: 0, -1: 126}[kind] - lane - b, 1)


def shift_y(main, rolled_outer, b, lane):
    if b == 0:
        return main, rolled_outer
    edge = lane == (127 if b == 1 else 0)
    rolled = turn(main, -b, 1)
    return jnp.where(edge, rolled_outer, rolled), jnp.where(edge, rolled, rolled_outer)


def along(values, pass_):
    values = list(values)
    for step in (1, 3, 9):
        for start in range(27):
            if (start // step) % 3 == 0:
                at = (start, start + step, start + 2 * step)
                for i, new in zip(at, pass_(*[values[j] for j in at])):
                    values[i] = new
    return values


def moments(values):
    def pass_(lo, mid, hi):
        both = lo + hi
        return both + mid, hi - lo, both
    return along(values, pass_)


def dual_moments(values):
    return along(values, lambda lo, mid, hi: (mid, hi - lo, (hi - mid) + (lo - mid)))


def from_moments(values):
    return along(values, lambda m0, m1, m2: (m2 - m1, m0 - (m2 + m2), m2 + m1))


def from_dual(values):
    def pass_(z0, z1, z2):
        both = z0 + z2
        return both - z1, z0, both + z1
    return along(values, pass_)


def collide(f, solid, scale):
    m = moments(f)
    rho = m[0]
    inverse = 1.0 / rho
    jx, jy, jz = m[mi(1, 0, 0)], m[mi(0, 1, 0)], m[mi(0, 0, 1)]
    ux, uy, uz = jx * inverse, jy * inverse, jz * inverse
    xx, yy, zz = jx * ux, jy * uy, jz * uz
    third = rho * (1.0 / 3.0)
    ninth = rho * (1.0 / 9.0)
    e = [None] * 27
    e[mi(2, 0, 0)], e[mi(0, 2, 0)], e[mi(0, 0, 2)] = third + xx, third + yy, third + zz
    e[mi(1, 1, 0)], e[mi(1, 0, 1)], e[mi(0, 1, 1)] = jx * uy, jx * uz, jy * uz
    jx3, jy3, jz3 = jx * (1.0 / 3.0), jy * (1.0 / 3.0), jz * (1.0 / 3.0)
    e[mi(1, 2, 0)] = e[mi(1, 0, 2)] = jx3
    e[mi(2, 1, 0)] = e[mi(0, 1, 2)] = jy3
    e[mi(2, 0, 1)] = e[mi(0, 2, 1)] = jz3
    e[mi(2, 2, 0)] = ninth + (xx + yy) * (1.0 / 3.0)
    e[mi(2, 0, 2)] = ninth + (xx + zz) * (1.0 / 3.0)
    e[mi(0, 2, 2)] = ninth + (yy + zz) * (1.0 / 3.0)
    e[mi(2, 1, 1)] = e[mi(0, 1, 1)] * (1.0 / 3.0)
    e[mi(1, 2, 1)] = e[mi(1, 0, 1)] * (1.0 / 3.0)
    e[mi(1, 1, 2)] = e[mi(1, 1, 0)] * (1.0 / 3.0)
    e[mi(1, 2, 2)], e[mi(2, 1, 2)], e[mi(2, 2, 1)] = jx * (1.0 / 9.0), jy * (1.0 / 9.0), jz * (1.0 / 9.0)
    e[mi(2, 2, 2)] = (third + (xx + yy + zz)) * (1.0 / 9.0)
    z = []
    for i in range(27):
        if i in (0, 1, 3, 9):
            z.append(jnp.zeros_like(rho))
        else:
            z.append((m[i] if e[i] is None else m[i] - e[i]) * scale[i])
    h = from_moments(z)
    out = [jnp.where(solid, f[26 - q], f[q] - h[q]) for q in range(27)]
    return out, (ux, uy, uz)


def pull_back(v, u, solid, scale):
    ux, uy, uz = u
    z = [y * s for y, s in zip(dual_moments(v), scale)]

    def at(i, j, k):
        return z[mi(i, j, k)]

    third = 1.0 / 3.0
    top = at(2, 2, 2) * third
    d_xy, d_xz, d_yz = at(2, 2, 0) + top, at(2, 0, 2) + top, at(0, 2, 2) + top
    q_xx = at(2, 0, 0) + (at(2, 2, 0) + d_xz) * third
    q_yy = at(0, 2, 0) + (at(0, 2, 2) + d_xy) * third
    q_zz = at(0, 0, 2) + (at(2, 0, 2) + d_yz) * third
    base = at(0, 0, 0) + (q_xx + (at(0, 2, 0) + at(0, 0, 2) + at(0, 2, 2) * third)) * third
    b_x = at(1, 0, 0) + (at(1, 2, 0) + at(1, 0, 2) + at(1, 2, 2) * third) * third
    b_y = at(0, 1, 0) + (at(2, 1, 0) + at(0, 1, 2) + at(2, 1, 2) * third) * third
    b_z = at(0, 0, 1) + (at(2, 0, 1) + at(0, 2, 1) + at(2, 2, 1) * third) * third
    q_xy = at(1, 1, 0) + at(1, 1, 2) * third
    q_xz = at(1, 0, 1) + at(1, 2, 1) * third
    q_yz = at(0, 1, 1) + at(2, 1, 1) * third
    p_x = (q_xx + q_xx) * ux + q_xy * uy + q_xz * uz
    p_y = q_xy * ux + (q_yy + q_yy) * uy + q_yz * uz
    p_z = q_xz * ux + q_yz * uy + (q_zz + q_zz) * uz
    quad = (p_x * ux + p_y * uy + p_z * uz) * 0.5
    z[0] = z[0] - (base - quad)
    z[mi(1, 0, 0)] = z[mi(1, 0, 0)] - (b_x + p_x)
    z[mi(0, 1, 0)] = z[mi(0, 1, 0)] - (b_y + p_y)
    z[mi(0, 0, 1)] = z[mi(0, 0, 1)] - (b_z + p_z)
    h = from_dual(z)
    return [jnp.where(solid, v[26 - q], v[q] - h[q]) for q in range(27)]


PIECES = 3


def first_kernel(rows, rates_in, f_in, wall_in, cot_in, cot, scale_out, sums, speed, solid_out, packed,
                 rates, f, wall, sems):
    copies = [pltpu.make_async_copy(rates_in, rates, sems.at[0]), pltpu.make_async_copy(wall_in, wall, sems.at[1])]
    for array, (source, target) in enumerate(((f_in, f), (cot_in, cot))):
        for piece in range(PIECES):
            part = pl.ds(27 // PIECES * piece, 27 // PIECES)
            copies.append(pltpu.make_async_copy(
                source.at[part], target.at[part], sems.at[2 + PIECES * array + piece]))
    for copy in copies:
        copy.start()
    for copy in copies[:2 + PIECES]:
        copy.wait()
    for i in range(27):
        scale_out[i] = jnp.full((8, 128), rates[i] * (0.5 ** NNZ[i]), F32)
    scale = [rates[i] * (0.5 ** NNZ[i]) for i in range(27)]
    plane = lax.broadcasted_iota(jnp.int32, (8, 128), 0)
    boundary = (plane == 0) | (plane == 7)
    lane = lanes()
    table, _ = slots(rows)
    for x in range(rows):
        at = pl.ds(x, 8, stride=rows)
        solid = boundary | (wall[at, :] == 1)
        solid_out[x] = jnp.where(solid, 1.0, 0.0)
        out, u = collide([f[q, at, :] for q in range(27)], solid, scale)
        for k in range(3):
            speed[k, x] = u[k]
        for a in SIGNS:
            for b in SIGNS:
                low = turn(out[qi(a, b, -1)], -1, 0)
                high = turn(out[qi(a, b, 1)], 1, 0)
                i = 2 * (3 * (a + 1) + b + 1)
                sums[i, x] = out[qi(a, b, 0)] + (low + high)
                sums[i + 1, x] = high - low
    for copy in copies[2 + PIECES:]:
        copy.wait()
    pieces = [jnp.zeros((8, 128), F32) for _ in range(3)]
    for key, (g, i, kind) in table.items():
        if key[0] == "v":
            block = cot[key[1], pl.ds(key[2], 8, stride=rows), :]
        elif key[0] == "w":
            block = solid_out[key[1]]
        else:
            block = sums[2 * (3 * (key[1] + 1) + key[2] + 1) + key[3], key[4]]
        mine = (lane == i) | (lane == i + 1)
        pieces[g] = jnp.where(mine, outgoing(block, i, kind), pieces[g])
    for g in range(3):
        packed[g] = pieces[g]


def edge_rows(rows, side):
    near, far = (0, 1) if side == 1 else (rows - 1, rows - 2)
    keys = [(q, near) for q, c in enumerate(Q) if c[0] == 0]
    keys += [(q, near) for q, c in enumerate(Q) if c[0] == side]
    return keys + [(q, far) for q, c in enumerate(Q) if c[0] == side]


def second_kernel(rows, cot, sums, solid_in, from_left, from_right, to_left, to_right, own, merged):
    lane = lanes()
    table, used = slots(rows)
    halo = []
    for g in range(3):
        takes_left = jnp.zeros((8, 128), jnp.bool_)
        for key, (h, i, kind) in table.items():
            if h == g and kind <= 0:
                takes_left = takes_left | (lane == i)
            if h == g and kind == -1:
                takes_left = takes_left | (lane == i + 1)
        halo.append(jnp.where(takes_left, from_left[g], from_right[g]))
        merged[g] = halo[g]

    def outer(key, b=0):
        g, i, kind = table[key]
        return incoming(halo[g], i, kind, b)

    def both(a, x):
        parts = {}
        for b in SIGNS:
            for s in range(2):
                i = 2 * (3 * (a + 1) + b + 1) + s
                parts[b, s] = shift_y(sums[i, x], outer(("s", a, b, s, x), -b), -b, lane)
        result = []
        for n in range(2):
            result.append((
                parts[0, 0][n] + (parts[-1, 0][n] + parts[1, 0][n]),
                parts[1, 0][n] - parts[-1, 0][n],
                parts[0, 1][n] + (parts[-1, 1][n] + parts[1, 1][n]),
            ))
        return result

    t = {(a, x): both(a, x) for a in SIGNS for x in range(rows)}

    def total(x, n):
        terms = [(a, t[a, x - a][n]) for a in SIGNS if 0 <= x - a < rows]
        density = functools.reduce(jnp.add, [v[0] for _, v in terms])
        along_y = functools.reduce(jnp.add, [v[1] for _, v in terms])
        along_z = functools.reduce(jnp.add, [v[2] for _, v in terms])
        moving = [(a, v[0]) for a, v in terms if a]
        along_x = jnp.zeros((8, 128), F32)
        for a, v in moving:
            along_x = along_x + v if a == 1 else along_x - v
        return density, along_x, along_y, along_z

    for x in range(-1, rows + 1):
        for n in range(2):
            for k, v in enumerate(total(x, n)):
                own[k, 2 * (x + 1) + n] = v

    for side, message in ((1, to_left), (-1, to_right)):
        near, far = (0, 1) if side == 1 else (rows - 1, rows - 2)
        for k, (q, x) in enumerate(edge_rows(rows, side)):
            message[k] = cot[q, pl.ds(x, 8, stride=rows), :]
        extra = []
        for n in range(2):
            row = list(t[-side, near][n])
            still, moved = t[0, near][n], t[-side, far][n]
            row += [still[0] + moved[0], moved[0] if side == -1 else -moved[0]]
            row += [still[1] + moved[1], still[2] + moved[2]]
            row.append(solid_in[near] if n == 0 else outer(("w", near)))
            extra.append(row)
        columns = halo[0]
        for k in range(8):
            message[27 + k] = extra[0][k]
            i = used + 2 * k
            columns = jnp.where((lane == i) | (lane == i + 1), turn(extra[1][k], i + 1, 1), columns)
        message[35] = columns


def third_kernel(rows, rates, cot, speed, solid_in, own, merged, from_low, from_high, out, v1, g1, extra):
    scale = [rates[i] for i in range(27)]
    lane = lanes()
    table, used = slots(rows)
    ring = rows + 2
    remote = {}
    for side, message, group in ((1, from_high, "high"), (-1, from_low, "low")):
        for k, (q, x) in enumerate(edge_rows(rows, side)):
            _, i, kind = table["v", q, x]
            remote[q, x + side * rows] = (message, group, k, i, kind)
    turned = {}
    for c in SIGNS:
        for g in range(2):
            turned[g, c] = turn(merged[g], -c, 0)
        turned["low", c] = turn(from_low[35], -c, 0)
        turned["high", c] = turn(from_high[35], -c, 0)
    for q, (a, b, c) in enumerate(Q):
        for x in range(-1, rows + 1):
            source = x + a
            if 0 <= source < rows:
                main = cot[q, pl.ds(source, 8, stride=rows), :]
                group, i, kind = table["v", q, source]
            else:
                message, group, k, i, kind = remote[q, source]
                main = message[k]
            outer = incoming(turned[group, c], i, kind, b)
            main, outer = shift_y(turn(main, -c, 0), outer, b, lane)
            v1[q, 2 * (x + 1)] = main
            v1[q, 2 * (x + 1) + 1] = outer
    for x in range(-1, rows + 1):
        for n in range(2):
            total = [own[k, 2 * (x + 1) + n] for k in range(4)]
            for side, message in ((1, from_high), (-1, from_low)):
                near = rows - 1 if side == 1 else 0

                def got(k):
                    if n == 0:
                        return message[27 + k]
                    return incoming(message[35], used + 2 * k, 0)

                if x == near:
                    total = [total[0] + got(0), total[1] - got(0) if side == 1 else total[1] + got(0),
                             total[2] + got(1), total[3] + got(2)]
                if x == near + side:
                    total = [total[k] + got(3 + k) for k in range(4)]
                    wall = got(7)
            if 0 <= x < rows:
                if n == 0:
                    wall = solid_in[x]
                else:
                    g, i, kind = table["w", x]
                    wall = incoming(merged[g], i, kind)
            inverse = 1.0 / total[0]
            for k in range(3):
                extra[k, 2 * (x + 1) + n] = total[k + 1] * inverse
            extra[3, 2 * (x + 1) + n] = wall

    def one(r, _):
        v = [v1[q, r] for q in range(27)]
        u = [extra[k, r] for k in range(3)]
        g = pull_back(v, u, extra[3, r] > 0.5, scale)
        for q in range(27):
            g1[q, r] = g[q]
        return 0

    lax.fori_loop(0, 2 * ring, one, 0)
    for x in range(rows):
        v = []
        for q, (a, b, c) in enumerate(Q):
            r = 2 * (x + a + 1)
            main = g1[q, r]
            if b:
                main = shift_y(main, turn(g1[q, r + 1], -b, 1), b, lane)[0]
            v.append(turn(main, -c, 0))
        result = pull_back(v, [speed[k, x] for k in range(3)], solid_in[x] > 0.5, scale)
        for q in range(27):
            out[q, pl.ds(x, 8, stride=rows), :] = result[q]


def call(kernel, name, out_shapes, scratch, operands, space=pltpu.VMEM):
    return pl.pallas_call(
        kernel,
        out_shape=[jax.ShapeDtypeStruct(s, F32) for s in out_shapes],
        in_specs=[pl.BlockSpec(memory_space=space)] * len(operands),
        out_specs=[pl.BlockSpec(memory_space=pltpu.VMEM)] * len(out_shapes),
        scratch_shapes=scratch,
        compiler_params=pltpu.CompilerParams(vmem_limit_bytes=32 * 1024 * 1024),
        name=name,
    )(*operands)


def ring(block, axis, step):
    size = lax.axis_size(axis)
    return lax.ppermute(block, axis, [(i, (i + step) % size) for i in range(size)])


def shards(checkpoint, rates, wall_mask, cotangent):
    planes, rows, width = checkpoint.shape[1:]
    f = checkpoint.reshape(27, planes * rows, width)
    cot = cotangent.reshape(27, planes * rows, width)
    wall = wall_mask.reshape(planes * rows, width)
    tile = (planes, width)
    lattice = (27, planes * rows, width)
    cot, scale, sums, speed, solid, packed = call(
        functools.partial(first_kernel, rows), "collide",
        [lattice, (27,) + tile, (18, rows) + tile, (3, rows) + tile, (rows,) + tile, (3,) + tile],
        [pltpu.SMEM((27,), F32), pltpu.VMEM(lattice, F32), pltpu.VMEM(lattice[1:], jnp.int32),
         pltpu.SemaphoreType.DMA((2 + 2 * PIECES,))],
        (rates, f, wall, cot), pltpu.HBM)
    from_right = ring(packed, "gy", -1)
    from_left = ring(packed, "gy", 1)
    to_left, to_right, own, merged = call(
        functools.partial(second_kernel, rows), "pack",
        [(36,) + tile, (36,) + tile, (4, 2 * rows + 4) + tile, (3,) + tile], [],
        (cot, sums, solid, from_left, from_right))
    from_high = ring(to_left, "gx", -1)
    from_low = ring(to_right, "gx", 1)
    (out,) = call(
        functools.partial(third_kernel, rows), "gradient",
        [lattice],
        [pltpu.VMEM((27, 2 * rows + 4) + tile, F32), pltpu.VMEM((27, 2 * rows + 4) + tile, F32),
         pltpu.VMEM((4, 2 * rows + 4) + tile, F32)],
        (scale, cot, speed, solid, own, merged, from_low, from_high))
    return out.reshape(checkpoint.shape)


def solution(mesh):
    in_specs = (P(None, None, "gx", "gy"), P(), P(None, "gx", "gy"), P(None, None, "gx", "gy"))
    out_specs = P(None, None, "gx", "gy")
    return jax.shard_map(shards, mesh=mesh, in_specs=in_specs, out_specs=out_specs, check_vma=False)
```

```python
import functools
import jax
import jax.numpy as jnp
from jax import lax
from jax.experimental import pallas as pl
from jax.experimental.pallas import tpu as pltpu
from jax.sharding import PartitionSpec as P

F32 = jnp.float32
SIGNS = (-1, 0, 1)
Q = [(a, b, c) for a in SIGNS for b in SIGNS for c in SIGNS]


def qi(a, b, c):
    return 9 * (a + 1) + 3 * (b + 1) + (c + 1)


def mi(i, j, k):
    return 9 * i + 3 * j + k


NNZ = [(i > 0) + (j > 0) + (k > 0) for i in range(3) for j in range(3) for k in range(3)]


def slots(rows):
    first, second, sums = [], [], []
    for q, (a, b, c) in enumerate(Q):
        for x in range(rows):
            left = (a >= 0 and x == 0) or (a == 1 and x == 1)
            right = (a <= 0 and x == rows - 1) or (a == -1 and x == rows - 2)
            (first if left or right else second).append((("v", q, x), b))
    for x in range(rows):
        second.append((("w", x), 0))
    for a in SIGNS:
        for b in SIGNS:
            for s in range(2):
                for x in range(rows):
                    sums.append((("s", a, b, s, x), -b))
    table = {}
    groups = [first + sums[64:], second, sums[:64]]
    for g, group in enumerate(groups):
        for i, (key, kind) in enumerate(group):
            table[key] = (g, 2 * i, kind)
    return table, 2 * len(first)


def turn(v, shift, axis):
    shift = shift % v.shape[axis]
    return v if shift == 0 else pltpu.roll(v, shift, axis)


def lanes():
    return lax.broadcasted_iota(jnp.int32, (8, 128), 1)


def outgoing(block, lane, kind):
    return turn(block, {0: lane + 1, 1: lane, -1: lane + 2}[kind], 1)


def incoming(packed, lane, kind, b=0):
    return turn(packed, {0: 127, 1: 0, -1: 126}[kind] - lane - b, 1)


def shift_y(main, rolled_outer, b, lane):
    if b == 0:
        return main, rolled_outer
    edge = lane == (127 if b == 1 else 0)
    rolled = turn(main, -b, 1)
    return jnp.where(edge, rolled_outer, rolled), jnp.where(edge, rolled, rolled_outer)


def along(values, pass_):
    values = list(values)
    for step in (1, 3, 9):
        for start in range(27):
            if (start // step) % 3 == 0:
                at = (start, start + step, start + 2 * step)
                for i, new in zip(at, pass_(*[values[j] for j in at])):
                    values[i] = new
    return values


def moments(values):
    def pass_(lo, mid, hi):
        both = lo + hi
        return both + mid, hi - lo, both
    return along(values, pass_)


def dual_moments(values):
    return along(values, lambda lo, mid, hi: (mid, hi - lo, (hi - mid) + (lo - mid)))


def from_moments(values):
    return along(values, lambda m0, m1, m2: (m2 - m1, m0 - (m2 + m2), m2 + m1))


def from_dual(values):
    def pass_(z0, z1, z2):
        both = z0 + z2
        return both - z1, z0, both + z1
    return along(values, pass_)


def collide(f, solid, scale):
    m = moments(f)
    rho = m[0]
    inverse = 1.0 / rho
    jx, jy, jz = m[mi(1, 0, 0)], m[mi(0, 1, 0)], m[mi(0, 0, 1)]
    ux, uy, uz = jx * inverse, jy * inverse, jz * inverse
    xx, yy, zz = jx * ux, jy * uy, jz * uz
    third = rho * (1.0 / 3.0)
    ninth = rho * (1.0 / 9.0)
    e = [None] * 27
    e[mi(2, 0, 0)], e[mi(0, 2, 0)], e[mi(0, 0, 2)] = third + xx, third + yy, third + zz
    e[mi(1, 1, 0)], e[mi(1, 0, 1)], e[mi(0, 1, 1)] = jx * uy, jx * uz, jy * uz
    jx3, jy3, jz3 = jx * (1.0 / 3.0), jy * (1.0 / 3.0), jz * (1.0 / 3.0)
    e[mi(1, 2, 0)] = e[mi(1, 0, 2)] = jx3
    e[mi(2, 1, 0)] = e[mi(0, 1, 2)] = jy3
    e[mi(2, 0, 1)] = e[mi(0, 2, 1)] = jz3
    e[mi(2, 2, 0)] = ninth + (xx + yy) * (1.0 / 3.0)
    e[mi(2, 0, 2)] = ninth + (xx + zz) * (1.0 / 3.0)
    e[mi(0, 2, 2)] = ninth + (yy + zz) * (1.0 / 3.0)
    e[mi(2, 1, 1)] = e[mi(0, 1, 1)] * (1.0 / 3.0)
    e[mi(1, 2, 1)] = e[mi(1, 0, 1)] * (1.0 / 3.0)
    e[mi(1, 1, 2)] = e[mi(1, 1, 0)] * (1.0 / 3.0)
    e[mi(1, 2, 2)], e[mi(2, 1, 2)], e[mi(2, 2, 1)] = jx * (1.0 / 9.0), jy * (1.0 / 9.0), jz * (1.0 / 9.0)
    e[mi(2, 2, 2)] = (third + (xx + yy + zz)) * (1.0 / 9.0)
    z = []
    for i in range(27):
        if i in (0, 1, 3, 9):
            z.append(jnp.zeros_like(rho))
        else:
            z.append((m[i] if e[i] is None else m[i] - e[i]) * scale[i])
    h = from_moments(z)
    out = [jnp.where(solid, f[26 - q], f[q] - h[q]) for q in range(27)]
    return out, (ux, uy, uz)


def pull_back(v, u, solid, scale):
    ux, uy, uz = u
    z = [y * s for y, s in zip(dual_moments(v), scale)]

    def at(i, j, k):
        return z[mi(i, j, k)]

    third = 1.0 / 3.0
    top = at(2, 2, 2) * third
    d_xy, d_xz, d_yz = at(2, 2, 0) + top, at(2, 0, 2) + top, at(0, 2, 2) + top
    q_xx = at(2, 0, 0) + (at(2, 2, 0) + d_xz) * third
    q_yy = at(0, 2, 0) + (at(0, 2, 2) + d_xy) * third
    q_zz = at(0, 0, 2) + (at(2, 0, 2) + d_yz) * third
    base = at(0, 0, 0) + (q_xx + (at(0, 2, 0) + at(0, 0, 2) + at(0, 2, 2) * third)) * third
    b_x = at(1, 0, 0) + (at(1, 2, 0) + at(1, 0, 2) + at(1, 2, 2) * third) * third
    b_y = at(0, 1, 0) + (at(2, 1, 0) + at(0, 1, 2) + at(2, 1, 2) * third) * third
    b_z = at(0, 0, 1) + (at(2, 0, 1) + at(0, 2, 1) + at(2, 2, 1) * third) * third
    q_xy = at(1, 1, 0) + at(1, 1, 2) * third
    q_xz = at(1, 0, 1) + at(1, 2, 1) * third
    q_yz = at(0, 1, 1) + at(2, 1, 1) * third
    p_x = (q_xx + q_xx) * ux + q_xy * uy + q_xz * uz
    p_y = q_xy * ux + (q_yy + q_yy) * uy + q_yz * uz
    p_z = q_xz * ux + q_yz * uy + (q_zz + q_zz) * uz
    quad = (p_x * ux + p_y * uy + p_z * uz) * 0.5
    z[0] = z[0] - (base - quad)
    z[mi(1, 0, 0)] = z[mi(1, 0, 0)] - (b_x + p_x)
    z[mi(0, 1, 0)] = z[mi(0, 1, 0)] - (b_y + p_y)
    z[mi(0, 0, 1)] = z[mi(0, 0, 1)] - (b_z + p_z)
    h = from_dual(z)
    return [jnp.where(solid, v[26 - q], v[q] - h[q]) for q in range(27)]


PIECES = 3


def first_kernel(rows, rates_in, f_in, wall_in, cot_in, cot, scale_out, sums, speed, solid_out, packed,
                 rates, f, wall, sems):
    copies = [pltpu.make_async_copy(rates_in, rates, sems.at[0]), pltpu.make_async_copy(wall_in, wall, sems.at[1])]
    for array, (source, target) in enumerate(((f_in, f), (cot_in, cot))):
        for piece in range(PIECES):
            part = pl.ds(27 // PIECES * piece, 27 // PIECES)
            copies.append(pltpu.make_async_copy(
                source.at[part], target.at[part], sems.at[2 + PIECES * array + piece]))
    for copy in copies:
        copy.start()
    for copy in copies[:2 + PIECES]:
        copy.wait()
    for i in range(27):
        scale_out[i] = jnp.full((8, 128), rates[i] * (0.5 ** NNZ[i]), F32)
    scale = [rates[i] * (0.5 ** NNZ[i]) for i in range(27)]
    plane = lax.broadcasted_iota(jnp.int32, (8, 128), 0)
    boundary = (plane == 0) | (plane == 7)
    lane = lanes()
    table, _ = slots(rows)
    for x in range(rows):
        at = pl.ds(x, 8, stride=rows)
        solid = boundary | (wall[at, :] == 1)
        solid_out[x] = jnp.where(solid, 1.0, 0.0)
        out, u = collide([f[q, at, :] for q in range(27)], solid, scale)
        for k in range(3):
            speed[k, x] = u[k]
        for a in SIGNS:
            for b in SIGNS:
                low = turn(out[qi(a, b, -1)], -1, 0)
                high = turn(out[qi(a, b, 1)], 1, 0)
                i = 2 * (3 * (a + 1) + b + 1)
                sums[i, x] = out[qi(a, b, 0)] + (low + high)
                sums[i + 1, x] = high - low
    for copy in copies[2 + PIECES:]:
        copy.wait()
    pieces = [jnp.zeros((8, 128), F32) for _ in range(3)]
    for key, (g, i, kind) in table.items():
        if key[0] == "v":
            block = cot[key[1], pl.ds(key[2], 8, stride=rows), :]
        elif key[0] == "w":
            block = solid_out[key[1]]
        else:
            block = sums[2 * (3 * (key[1] + 1) + key[2] + 1) + key[3], key[4]]
        mine = (lane == i) | (lane == i + 1)
        pieces[g] = jnp.where(mine, outgoing(block, i, kind), pieces[g])
    for g in range(3):
        packed[g] = pieces[g]


def edge_rows(rows, side):
    near, far = (0, 1) if side == 1 else (rows - 1, rows - 2)
    keys = [(q, near) for q, c in enumerate(Q) if c[0] == 0]
    keys += [(q, near) for q, c in enumerate(Q) if c[0] == side]
    return keys + [(q, far) for q, c in enumerate(Q) if c[0] == side]


def second_kernel(rows, cot, sums, solid_in, from_left, from_right, to_left, to_right, own, merged):
    lane = lanes()
    table, used = slots(rows)
    halo = []
    for g in range(3):
        takes_left = jnp.zeros((8, 128), jnp.bool_)
        for key, (h, i, kind) in table.items():
            if h == g and kind <= 0:
                takes_left = takes_left | (lane == i)
            if h == g and kind == -1:
                takes_left = takes_left | (lane == i + 1)
        halo.append(jnp.where(takes_left, from_left[g], from_right[g]))
        merged[g] = halo[g]

    def outer(key, b=0):
        g, i, kind = table[key]
        return incoming(halo[g], i, kind, b)

    def both(a, x):
        parts = {}
        for b in SIGNS:
            for s in range(2):
                i = 2 * (3 * (a + 1) + b + 1) + s
                parts[b, s] = shift_y(sums[i, x], outer(("s", a, b, s, x), -b), -b, lane)
        result = []
        for n in range(2):
            result.append((
                parts[0, 0][n] + (parts[-1, 0][n] + parts[1, 0][n]),
                parts[1, 0][n] - parts[-1, 0][n],
                parts[0, 1][n] + (parts[-1, 1][n] + parts[1, 1][n]),
            ))
        return result

    t = {(a, x): both(a, x) for a in SIGNS for x in range(rows)}

    def total(x, n):
        terms = [(a, t[a, x - a][n]) for a in SIGNS if 0 <= x - a < rows]
        density = functools.reduce(jnp.add, [v[0] for _, v in terms])
        along_y = functools.reduce(jnp.add, [v[1] for _, v in terms])
        along_z = functools.reduce(jnp.add, [v[2] for _, v in terms])
        moving = [(a, v[0]) for a, v in terms if a]
        along_x = jnp.zeros((8, 128), F32)
        for a, v in moving:
            along_x = along_x + v if a == 1 else along_x - v
        return density, along_x, along_y, along_z

    for x in range(-1, rows + 1):
        for n in range(2):
            for k, v in enumerate(total(x, n)):
                own[k, 2 * (x + 1) + n] = v

    for side, message in ((1, to_left), (-1, to_right)):
        near, far = (0, 1) if side == 1 else (rows - 1, rows - 2)
        for k, (q, x) in enumerate(edge_rows(rows, side)):
            message[k] = cot[q, pl.ds(x, 8, stride=rows), :]
        extra = []
        for n in range(2):
            row = list(t[-side, near][n])
            still, moved = t[0, near][n], t[-side, far][n]
            row += [still[0] + moved[0], moved[0] if side == -1 else -moved[0]]
            row += [still[1] + moved[1], still[2] + moved[2]]
            row.append(solid_in[near] if n == 0 else outer(("w", near)))
            extra.append(row)
        columns = halo[0]
        for k in range(8):
            message[27 + k] = extra[0][k]
            i = used + 2 * k
            columns = jnp.where((lane == i) | (lane == i + 1), turn(extra[1][k], i + 1, 1), columns)
        message[35] = columns


def third_kernel(rows, rates, cot, speed, solid_in, own, merged, from_low, from_high, out, v1, g1, extra):
    scale = [rates[i] for i in range(27)]
    lane = lanes()
    table, used = slots(rows)
    ring = rows + 2
    remote = {}
    for side, message, group in ((1, from_high, "high"), (-1, from_low, "low")):
        for k, (q, x) in enumerate(edge_rows(rows, side)):
            _, i, kind = table["v", q, x]
            remote[q, x + side * rows] = (message, group, k, i, kind)
    turned = {}
    for c in SIGNS:
        for g in range(2):
            turned[g, c] = turn(merged[g], -c, 0)
        turned["low", c] = turn(from_low[35], -c, 0)
        turned["high", c] = turn(from_high[35], -c, 0)
    for q, (a, b, c) in enumerate(Q):
        for x in range(-1, rows + 1):
            source = x + a
            if 0 <= source < rows:
                main = cot[q, pl.ds(source, 8, stride=rows), :]
                group, i, kind = table["v", q, source]
            else:
                message, group, k, i, kind = remote[q, source]
                main = message[k]
            outer = incoming(turned[group, c], i, kind, b)
            main, outer = shift_y(turn(main, -c, 0), outer, b, lane)
            v1[q, 2 * (x + 1)] = main
            v1[q, 2 * (x + 1) + 1] = outer
    for x in range(-1, rows + 1):
        for n in range(2):
            total = [own[k, 2 * (x + 1) + n] for k in range(4)]
            for side, message in ((1, from_high), (-1, from_low)):
                near = rows - 1 if side == 1 else 0

                def got(k):
                    if n == 0:
                        return message[27 + k]
                    return incoming(message[35], used + 2 * k, 0)

                if x == near:
                    total = [total[0] + got(0), total[1] - got(0) if side == 1 else total[1] + got(0),
                             total[2] + got(1), total[3] + got(2)]
                if x == near + side:
                    total = [total[k] + got(3 + k) for k in range(4)]
                    wall = got(7)
            if 0 <= x < rows:
                if n == 0:
                    wall = solid_in[x]
                else:
                    g, i, kind = table["w", x]
                    wall = incoming(merged[g], i, kind)
            inverse = 1.0 / total[0]
            for k in range(3):
                extra[k, 2 * (x + 1) + n] = total[k + 1] * inverse
            extra[3, 2 * (x + 1) + n] = wall

    def one(r, _):
        v = [v1[q, r] for q in range(27)]
        u = [extra[k, r] for k in range(3)]
        g = pull_back(v, u, extra[3, r] > 0.5, scale)
        for q in range(27):
            g1[q, r] = g[q]
        return 0

    lax.fori_loop(0, 2 * ring, one, 0)
    for x in range(rows):
        v = []
        for q, (a, b, c) in enumerate(Q):
            r = 2 * (x + a + 1)
            main = g1[q, r]
            if b:
                main = shift_y(main, turn(g1[q, r + 1], -b, 1), b, lane)[0]
            v.append(turn(main, -c, 0))
        result = pull_back(v, [speed[k, x] for k in range(3)], solid_in[x] > 0.5, scale)
        for q in range(27):
            out[q, pl.ds(x, 8, stride=rows), :] = result[q]


def call(kernel, name, out_shapes, scratch, operands, space=pltpu.VMEM):
    return pl.pallas_call(
        kernel,
        out_shape=[jax.ShapeDtypeStruct(s, F32) for s in out_shapes],
        in_specs=[pl.BlockSpec(memory_space=space)] * len(operands),
        out_specs=[pl.BlockSpec(memory_space=pltpu.VMEM)] * len(out_shapes),
        scratch_shapes=scratch,
        compiler_params=pltpu.CompilerParams(vmem_limit_bytes=32 * 1024 * 1024),
        name=name,
    )(*operands)


def ring(block, axis, step):
    size = lax.axis_size(axis)
    return lax.ppermute(block, axis, [(i, (i + step) % size) for i in range(size)])


def shards(checkpoint, rates, wall_mask, cotangent):
    planes, rows, width = checkpoint.shape[1:]
    f = checkpoint.reshape(27, planes * rows, width)
    cot = cotangent.reshape(27, planes * rows, width)
    wall = wall_mask.reshape(planes * rows, width)
    tile = (planes, width)
    lattice = (27, planes * rows, width)
    cot, scale, sums, speed, solid, packed = call(
        functools.partial(first_kernel, rows), "collide",
        [lattice, (27,) + tile, (18, rows) + tile, (3, rows) + tile, (rows,) + tile, (3,) + tile],
        [pltpu.SMEM((27,), F32), pltpu.VMEM(lattice, F32), pltpu.VMEM(lattice[1:], jnp.int32),
         pltpu.SemaphoreType.DMA((2 + 2 * PIECES,))],
        tuple(pltpu.with_memory_space_constraint(v, pltpu.HBM) for v in (rates, f, wall, cot)), pltpu.HBM)
    from_right = ring(packed, "gy", -1)
    from_left = ring(packed, "gy", 1)
    to_left, to_right, own, merged = call(
        functools.partial(second_kernel, rows), "pack",
        [(36,) + tile, (36,) + tile, (4, 2 * rows + 4) + tile, (3,) + tile], [],
        (cot, sums, solid, from_left, from_right))
    from_high = ring(to_left, "gx", -1)
    from_low = ring(to_right, "gx", 1)
    (out,) = call(
        functools.partial(third_kernel, rows), "gradient",
        [lattice],
        [pltpu.VMEM((27, 2 * rows + 4) + tile, F32), pltpu.VMEM((27, 2 * rows + 4) + tile, F32),
         pltpu.VMEM((4, 2 * rows + 4) + tile, F32)],
        (scale, cot, speed, solid, own, merged, from_low, from_high))
    return out.reshape(checkpoint.shape)


def solution(mesh):
    in_specs = (P(None, None, "gx", "gy"), P(), P(None, "gx", "gy"), P(None, None, "gx", "gy"))
    out_specs = P(None, None, "gx", "gy")
    return jax.shard_map(shards, mesh=mesh, in_specs=in_specs, out_specs=out_specs, check_vma=False)
```

```python
import functools
import jax
import jax.numpy as jnp
from jax import lax
from jax.experimental import pallas as pl
from jax.experimental.pallas import tpu as pltpu
from jax.sharding import PartitionSpec as P

F32 = jnp.float32
SIGNS = (-1, 0, 1)
Q = [(a, b, c) for a in SIGNS for b in SIGNS for c in SIGNS]


def qi(a, b, c):
    return 9 * (a + 1) + 3 * (b + 1) + (c + 1)


def mi(i, j, k):
    return 9 * i + 3 * j + k


NNZ = [(i > 0) + (j > 0) + (k > 0) for i in range(3) for j in range(3) for k in range(3)]


def slots(rows):
    first, second, sums = [], [], []
    for q, (a, b, c) in enumerate(Q):
        for x in range(rows):
            left = (a >= 0 and x == 0) or (a == 1 and x == 1)
            right = (a <= 0 and x == rows - 1) or (a == -1 and x == rows - 2)
            (first if left or right else second).append((("v", q, x), b))
    for x in range(rows):
        second.append((("w", x), 0))
    for a in SIGNS:
        for b in SIGNS:
            for s in range(2):
                for x in range(rows):
                    sums.append((("s", a, b, s, x), -b))
    table = {}
    groups = [first + sums[64:], second, sums[:64]]
    for g, group in enumerate(groups):
        for i, (key, kind) in enumerate(group):
            table[key] = (g, 2 * i, kind)
    return table, 2 * len(first)


def turn(v, shift, axis):
    shift = shift % v.shape[axis]
    return v if shift == 0 else pltpu.roll(v, shift, axis)


def lanes():
    return lax.broadcasted_iota(jnp.int32, (8, 128), 1)


def outgoing(block, lane, kind):
    return turn(block, {0: lane + 1, 1: lane, -1: lane + 2}[kind], 1)


def incoming(packed, lane, kind, b=0):
    return turn(packed, {0: 127, 1: 0, -1: 126}[kind] - lane - b, 1)


def shift_y(main, rolled_outer, b, lane):
    if b == 0:
        return main, rolled_outer
    edge = lane == (127 if b == 1 else 0)
    rolled = turn(main, -b, 1)
    return jnp.where(edge, rolled_outer, rolled), jnp.where(edge, rolled, rolled_outer)


def along(values, pass_):
    values = list(values)
    for step in (1, 3, 9):
        for start in range(27):
            if (start // step) % 3 == 0:
                at = (start, start + step, start + 2 * step)
                for i, new in zip(at, pass_(*[values[j] for j in at])):
                    values[i] = new
    return values


def moments(values):
    def pass_(lo, mid, hi):
        both = lo + hi
        return both + mid, hi - lo, both
    return along(values, pass_)


def dual_moments(values):
    return along(values, lambda lo, mid, hi: (mid, hi - lo, (hi - mid) + (lo - mid)))


def from_moments(values):
    return along(values, lambda m0, m1, m2: (m2 - m1, m0 - (m2 + m2), m2 + m1))


def from_dual(values):
    def pass_(z0, z1, z2):
        both = z0 + z2
        return both - z1, z0, both + z1
    return along(values, pass_)


def collide(f, solid, scale):
    m = moments(f)
    rho = m[0]
    inverse = 1.0 / rho
    jx, jy, jz = m[mi(1, 0, 0)], m[mi(0, 1, 0)], m[mi(0, 0, 1)]
    ux, uy, uz = jx * inverse, jy * inverse, jz * inverse
    xx, yy, zz = jx * ux, jy * uy, jz * uz
    third = rho * (1.0 / 3.0)
    ninth = rho * (1.0 / 9.0)
    e = [None] * 27
    e[mi(2, 0, 0)], e[mi(0, 2, 0)], e[mi(0, 0, 2)] = third + xx, third + yy, third + zz
    e[mi(1, 1, 0)], e[mi(1, 0, 1)], e[mi(0, 1, 1)] = jx * uy, jx * uz, jy * uz
    jx3, jy3, jz3 = jx * (1.0 / 3.0), jy * (1.0 / 3.0), jz * (1.0 / 3.0)
    e[mi(1, 2, 0)] = e[mi(1, 0, 2)] = jx3
    e[mi(2, 1, 0)] = e[mi(0, 1, 2)] = jy3
    e[mi(2, 0, 1)] = e[mi(0, 2, 1)] = jz3
    e[mi(2, 2, 0)] = ninth + (xx + yy) * (1.0 / 3.0)
    e[mi(2, 0, 2)] = ninth + (xx + zz) * (1.0 / 3.0)
    e[mi(0, 2, 2)] = ninth + (yy + zz) * (1.0 / 3.0)
    e[mi(2, 1, 1)] = e[mi(0, 1, 1)] * (1.0 / 3.0)
    e[mi(1, 2, 1)] = e[mi(1, 0, 1)] * (1.0 / 3.0)
    e[mi(1, 1, 2)] = e[mi(1, 1, 0)] * (1.0 / 3.0)
    e[mi(1, 2, 2)], e[mi(2, 1, 2)], e[mi(2, 2, 1)] = jx * (1.0 / 9.0), jy * (1.0 / 9.0), jz * (1.0 / 9.0)
    e[mi(2, 2, 2)] = (third + (xx + yy + zz)) * (1.0 / 9.0)
    z = []
    for i in range(27):
        if i in (0, 1, 3, 9):
            z.append(jnp.zeros_like(rho))
        else:
            z.append((m[i] if e[i] is None else m[i] - e[i]) * scale[i])
    h = from_moments(z)
    out = [jnp.where(solid, f[26 - q], f[q] - h[q]) for q in range(27)]
    return out, (ux, uy, uz)


def pull_back(v, u, solid, scale):
    ux, uy, uz = u
    z = [y * s for y, s in zip(dual_moments(v), scale)]

    def at(i, j, k):
        return z[mi(i, j, k)]

    third = 1.0 / 3.0
    top = at(2, 2, 2) * third
    d_xy, d_xz, d_yz = at(2, 2, 0) + top, at(2, 0, 2) + top, at(0, 2, 2) + top
    q_xx = at(2, 0, 0) + (at(2, 2, 0) + d_xz) * third
    q_yy = at(0, 2, 0) + (at(0, 2, 2) + d_xy) * third
    q_zz = at(0, 0, 2) + (at(2, 0, 2) + d_yz) * third
    base = at(0, 0, 0) + (q_xx + (at(0, 2, 0) + at(0, 0, 2) + at(0, 2, 2) * third)) * third
    b_x = at(1, 0, 0) + (at(1, 2, 0) + at(1, 0, 2) + at(1, 2, 2) * third) * third
    b_y = at(0, 1, 0) + (at(2, 1, 0) + at(0, 1, 2) + at(2, 1, 2) * third) * third
    b_z = at(0, 0, 1) + (at(2, 0, 1) + at(0, 2, 1) + at(2, 2, 1) * third) * third
    q_xy = at(1, 1, 0) + at(1, 1, 2) * third
    q_xz = at(1, 0, 1) + at(1, 2, 1) * third
    q_yz = at(0, 1, 1) + at(2, 1, 1) * third
    p_x = (q_xx + q_xx) * ux + q_xy * uy + q_xz * uz
    p_y = q_xy * ux + (q_yy + q_yy) * uy + q_yz * uz
    p_z = q_xz * ux + q_yz * uy + (q_zz + q_zz) * uz
    quad = (p_x * ux + p_y * uy + p_z * uz) * 0.5
    z[0] = z[0] - (base - quad)
    z[mi(1, 0, 0)] = z[mi(1, 0, 0)] - (b_x + p_x)
    z[mi(0, 1, 0)] = z[mi(0, 1, 0)] - (b_y + p_y)
    z[mi(0, 0, 1)] = z[mi(0, 0, 1)] - (b_z + p_z)
    h = from_dual(z)
    return [jnp.where(solid, v[26 - q], v[q] - h[q]) for q in range(27)]


PIECES = 3


def first_kernel(rows, rates_in, f_in, wall_in, cot_in, cot, scale_out, sums, speed, solid_out, packed,
                 raw_right,
                 rates, f, wall, sems):
    copies = [pltpu.make_async_copy(rates_in, rates, sems.at[0]), pltpu.make_async_copy(wall_in, wall, sems.at[1])]
    for array, (source, target) in enumerate(((f_in, f), (cot_in, cot))):
        for piece in range(PIECES):
            part = pl.ds(27 // PIECES * piece, 27 // PIECES)
            copies.append(pltpu.make_async_copy(
                source.at[part], target.at[part], sems.at[2 + PIECES * array + piece]))
    for copy in copies:
        copy.start()
    for copy in copies[:2 + PIECES]:
        copy.wait()
    for i in range(27):
        scale_out[i] = jnp.full((8, 128), rates[i] * (0.5 ** NNZ[i]), F32)
    scale = [rates[i] * (0.5 ** NNZ[i]) for i in range(27)]
    plane = lax.broadcasted_iota(jnp.int32, (8, 128), 0)
    boundary = (plane == 0) | (plane == 7)
    lane = lanes()
    table, _ = slots(rows)
    for x in range(rows):
        at = pl.ds(x, 8, stride=rows)
        solid = boundary | (wall[at, :] == 1)
        solid_out[x] = jnp.where(solid, 1.0, 0.0)
        out, u = collide([f[q, at, :] for q in range(27)], solid, scale)
        for k in range(3):
            speed[k, x] = u[k]
        for a in SIGNS:
            for b in SIGNS:
                low = turn(out[qi(a, b, -1)], -1, 0)
                high = turn(out[qi(a, b, 1)], 1, 0)
                i = 2 * (3 * (a + 1) + b + 1)
                sums[i, x] = out[qi(a, b, 0)] + (low + high)
                sums[i + 1, x] = high - low
    for copy in copies[2 + PIECES:]:
        copy.wait()
    raw_rows(rows, -1, cot, raw_right)
    pieces = [jnp.zeros((8, 128), F32) for _ in range(3)]
    for key, (g, i, kind) in table.items():
        if key[0] == "v":
            block = cot[key[1], pl.ds(key[2], 8, stride=rows), :]
        elif key[0] == "w":
            block = solid_out[key[1]]
        else:
            block = sums[2 * (3 * (key[1] + 1) + key[2] + 1) + key[3], key[4]]
        mine = (lane == i) | (lane == i + 1)
        pieces[g] = jnp.where(mine, outgoing(block, i, kind), pieces[g])
    for g in range(3):
        packed[g] = pieces[g]


def edge_rows(rows, side):
    near, far = (0, 1) if side == 1 else (rows - 1, rows - 2)
    keys = [(q, near) for q, c in enumerate(Q) if c[0] == 0]
    keys += [(q, near) for q, c in enumerate(Q) if c[0] == side]
    return keys + [(q, far) for q, c in enumerate(Q) if c[0] == side]


def raw_rows(rows, side, cot, message):
    for k, (q, x) in enumerate(edge_rows(rows, side)):
        message[k] = cot[q, pl.ds(x, 8, stride=rows), :]


def second_kernel(rows, cot, sums, solid_in, from_left, from_right, to_left, to_right, own, merged):
    lane = lanes()
    table, used = slots(rows)
    halo = []
    for g in range(3):
        takes_left = jnp.zeros((8, 128), jnp.bool_)
        for key, (h, i, kind) in table.items():
            if h == g and kind <= 0:
                takes_left = takes_left | (lane == i)
            if h == g and kind == -1:
                takes_left = takes_left | (lane == i + 1)
        halo.append(jnp.where(takes_left, from_left[g], from_right[g]))
        merged[g] = halo[g]

    def outer(key, b=0):
        g, i, kind = table[key]
        return incoming(halo[g], i, kind, b)

    def both(a, x):
        parts = {}
        for b in SIGNS:
            for s in range(2):
                i = 2 * (3 * (a + 1) + b + 1) + s
                parts[b, s] = shift_y(sums[i, x], outer(("s", a, b, s, x), -b), -b, lane)
        result = []
        for n in range(2):
            result.append((
                parts[0, 0][n] + (parts[-1, 0][n] + parts[1, 0][n]),
                parts[1, 0][n] - parts[-1, 0][n],
                parts[0, 1][n] + (parts[-1, 1][n] + parts[1, 1][n]),
            ))
        return result

    t = {(a, x): both(a, x) for a in SIGNS for x in range(rows)}

    def total(x, n):
        terms = [(a, t[a, x - a][n]) for a in SIGNS if 0 <= x - a < rows]
        density = functools.reduce(jnp.add, [v[0] for _, v in terms])
        along_y = functools.reduce(jnp.add, [v[1] for _, v in terms])
        along_z = functools.reduce(jnp.add, [v[2] for _, v in terms])
        moving = [(a, v[0]) for a, v in terms if a]
        along_x = jnp.zeros((8, 128), F32)
        for a, v in moving:
            along_x = along_x + v if a == 1 else along_x - v
        return density, along_x, along_y, along_z

    for x in range(-1, rows + 1):
        for n in range(2):
            for k, v in enumerate(total(x, n)):
                own[k, 2 * (x + 1) + n] = v

    for side, message in ((1, to_left), (-1, to_right)):
        near, far = (0, 1) if side == 1 else (rows - 1, rows - 2)
        first = message.shape[0] - 9
        if first:
            raw_rows(rows, side, cot, message)
        extra = []
        for n in range(2):
            row = list(t[-side, near][n])
            still, moved = t[0, near][n], t[-side, far][n]
            row += [still[0] + moved[0], moved[0] if side == -1 else -moved[0]]
            row += [still[1] + moved[1], still[2] + moved[2]]
            row.append(solid_in[near] if n == 0 else outer(("w", near)))
            extra.append(row)
        columns = halo[0]
        for k in range(8):
            message[first + k] = extra[0][k]
            i = used + 2 * k
            columns = jnp.where((lane == i) | (lane == i + 1), turn(extra[1][k], i + 1, 1), columns)
        message[first + 8] = columns


def outer_rows(rows):
    return [x for x in range(-1, rows + 1) if not 0 < x < rows - 1]


def gathered(rows, x, q, cot, turned, lane, remote=None):
    table, _ = slots(rows)
    a, b, c = Q[q]
    source = x + a
    if 0 <= source < rows:
        main = cot[q, pl.ds(source, 8, stride=rows), :]
        group, i, kind = table["v", q, source]
    else:
        message, group, k, i, kind = remote[q, source]
        main = message[k]
    outer = incoming(turned[group, c], i, kind, b)
    return shift_y(turn(main, -c, 0), outer, b, lane)


def middle_kernel(rows, scale_in, cot, solid_in, own, merged, inner, known):
    scale = [scale_in[i] for i in range(27)]
    lane = lanes()
    table, _ = slots(rows)
    turned = {(g, c): turn(merged[g], -c, 0) for g in range(2) for c in SIGNS}
    for x in range(1, rows - 1):
        v = [gathered(rows, x, q, cot, turned, lane) for q in range(27)]
        for n in range(2):
            total = [own[k, 2 * (x + 1) + n] for k in range(4)]
            inverse = 1.0 / total[0]
            if n == 0:
                wall = solid_in[x]
            else:
                g, i, kind = table["w", x]
                wall = incoming(merged[g], i, kind)
            out = pull_back([t[n] for t in v], [t * inverse for t in total[1:]], wall > 0.5, scale)
            for q in range(27):
                inner[q, 2 * (x - 1) + n] = out[q]
    for j, x in enumerate(outer_rows(rows)):
        for q in range(27):
            if 0 <= x + Q[q][0] < rows:
                known[q, 2 * j], known[q, 2 * j + 1] = gathered(rows, x, q, cot, turned, lane)


def outer_gradient(rows, side, scale, solid_in, own, merged, known, raw, extra, g1):
    lane = lanes()
    table, used = slots(rows)
    remote = {}
    for k, (q, x) in enumerate(edge_rows(rows, side)):
        _, i, kind = table["v", q, x]
        remote[q, x + side * rows] = (raw, "far", k, i, kind)
    turned = {("far", c): turn(extra[8], -c, 0) for c in SIGNS}
    near = rows - 1 if side == 1 else 0
    for j, x in enumerate(outer_rows(rows)):
        if x not in (near, near + side):
            continue
        v = []
        for q in range(27):
            if 0 <= x + Q[q][0] < rows:
                v.append((known[q, 2 * j], known[q, 2 * j + 1]))
            else:
                v.append(gathered(rows, x, q, None, turned, lane, remote))
        for n in range(2):
            def got(k):
                return extra[k] if n == 0 else incoming(extra[8], used + 2 * k, 0)

            total = [own[k, 2 * (x + 1) + n] for k in range(4)]
            if x == near:
                total = [total[0] + got(0), total[1] - got(0) if side == 1 else total[1] + got(0),
                         total[2] + got(1), total[3] + got(2)]
                if n == 0:
                    wall = solid_in[x]
                else:
                    g, i, kind = table["w", x]
                    wall = incoming(merged[g], i, kind)
            else:
                total = [total[k] + got(3 + k) for k in range(4)]
                wall = got(7)
            inverse = 1.0 / total[0]
            g = pull_back([t[n] for t in v], [t * inverse for t in total[1:]], wall > 0.5, scale)
            for q in range(27):
                if 0 <= x - Q[q][0] < rows:
                    g1[q, 2 * (j % 2) + n] = g[q]


def pulled_row(rows, x, arrays, speed, solid_in, scale, lane):
    v = []
    for q, (a, b, c) in enumerate(Q):
        array, r = arrays(x + a)
        main = array[q, r]
        if b:
            main = shift_y(main, turn(array[q, r + 1], -b, 1), b, lane)[0]
        v.append(turn(main, -c, 0))
    return pull_back(v, [speed[k, x] for k in range(3)], solid_in[x] > 0.5, scale)


def low_kernel(rows, scale_in, speed, solid_in, own, merged, inner, known, raw, extra, done, g1):
    scale = [scale_in[i] for i in range(27)]
    lane = lanes()
    outer_gradient(rows, -1, scale, solid_in, own, merged, known, raw, extra, g1)

    def arrays(x):
        return (g1, 2 * (x + 1)) if x < 1 else (inner, 2 * (x - 1))

    for x in range(rows - 2):
        result = pulled_row(rows, x, arrays, speed, solid_in, scale, lane)
        for q in range(27):
            done[q, x] = result[q]


def last_kernel(rows, scale_in, speed, solid_in, own, merged, inner, known, done, from_high, out_hbm, high, out, sems):
    scale = [scale_in[i] for i in range(27)]
    lane = lanes()
    outer_gradient(rows, 1, scale, solid_in, own, merged, known, from_high.at[0:27], from_high.at[27:36], high)

    def arrays(x):
        return (inner, 2 * (x - 1)) if x < rows - 1 else (high, 2 * (x - rows + 1))

    for x in range(rows):
        if x < rows - 2:
            result = [done[q, x] for q in range(27)]
        else:
            result = pulled_row(rows, x, arrays, speed, solid_in, scale, lane)
        for q in range(27):
            out[q, pl.ds(x, 8, stride=rows), :] = result[q]
    copies = []
    for piece in range(PIECES):
        part = pl.ds(27 // PIECES * piece, 27 // PIECES)
        copies.append(pltpu.make_async_copy(out.at[part], out_hbm.at[part], sems.at[piece]))
    for copy in copies:
        copy.start()
    for copy in copies:
        copy.wait()


def call(kernel, name, out_shapes, scratch, operands, space=pltpu.VMEM, work=0, out_space=pltpu.VMEM):
    return pl.pallas_call(
        kernel,
        out_shape=[jax.ShapeDtypeStruct(s, F32) for s in out_shapes],
        in_specs=[pl.BlockSpec(memory_space=space)] * len(operands),
        out_specs=[pl.BlockSpec(memory_space=out_space)] * len(out_shapes),
        scratch_shapes=scratch,
        compiler_params=pltpu.CompilerParams(vmem_limit_bytes=32 * 1024 * 1024),
        cost_estimate=pl.CostEstimate(flops=work, bytes_accessed=0 if work else 0, transcendentals=0) if work else None,
        name=name,
    )(*operands)


def ring(block, axis, step):
    size = lax.axis_size(axis)
    return lax.ppermute(block, axis, [(i, (i + step) % size) for i in range(size)])


def swap(block, axis, first):
    size = lax.axis_size(axis)
    route = []
    for i in range(first, size + first, 2):
        route += [(i % size, (i + 1) % size), ((i + 1) % size, i % size)]
    return lax.ppermute(block, axis, route)


def shards(checkpoint, rates, wall_mask, cotangent):
    planes, rows, width = checkpoint.shape[1:]
    f = checkpoint.reshape(27, planes * rows, width)
    cot = cotangent.reshape(27, planes * rows, width)
    wall = wall_mask.reshape(planes * rows, width)
    tile = (planes, width)
    lattice = (27, planes * rows, width)
    cot, scale, sums, speed, solid, packed, raw_right = call(
        functools.partial(first_kernel, rows), "collide",
        [lattice, (27,) + tile, (18, rows) + tile, (3, rows) + tile, (rows,) + tile, (3,) + tile, (27,) + tile],
        [pltpu.SMEM((27,), F32), pltpu.VMEM(lattice, F32), pltpu.VMEM(lattice[1:], jnp.int32),
         pltpu.SemaphoreType.DMA((2 + 2 * PIECES,))],
        tuple(pltpu.with_memory_space_constraint(v, pltpu.HBM) for v in (rates, f, wall, cot)), pltpu.HBM)
    raw_low = ring(raw_right, "gx", 1)
    pairs = [swap(packed, "gy", first) for first in (0, 1)]
    even = lax.axis_index("gy") % 2 == 0
    from_right = jnp.where(even, pairs[0], pairs[1])
    from_left = jnp.where(even, pairs[1], pairs[0])
    to_left, small_right, own, merged = call(
        functools.partial(second_kernel, rows), "pack",
        [(36,) + tile, (9,) + tile, (4, 2 * rows + 4) + tile, (3,) + tile], [],
        (cot, sums, solid, from_left, from_right))
    small_low = ring(small_right, "gx", 1)
    from_high = ring(to_left, "gx", -1)
    inner, known = call(
        functools.partial(middle_kernel, rows), "inner_rows",
        [(27, 2 * rows - 4) + tile, (27, 8) + tile], [],
        (scale, cot, solid, own, merged))
    (done,) = call(
        functools.partial(low_kernel, rows), "low_rows",
        [(27, rows - 2) + tile], [pltpu.VMEM((27, 4) + tile, F32)],
        (scale, speed, solid, own, merged, inner, known, raw_low, small_low), work=2000000000)
    (out,) = call(
        functools.partial(last_kernel, rows), "gradient",
        [lattice],
        [pltpu.VMEM((27, 4) + tile, F32), pltpu.VMEM(lattice, F32), pltpu.SemaphoreType.DMA((PIECES,))],
        (scale, speed, solid, own, merged, inner, known, done, from_high), out_space=pltpu.HBM)
    return out.reshape(checkpoint.shape)


def solution(mesh):
    in_specs = (P(None, None, "gx", "gy"), P(), P(None, "gx", "gy"), P(None, None, "gx", "gy"))
    out_specs = P(None, None, "gx", "gy")
    return jax.shard_map(shards, mesh=mesh, in_specs=in_specs, out_specs=out_specs, check_vma=False)
```

```python
import functools
import jax
import jax.numpy as jnp
from jax import lax
from jax.experimental import pallas as pl
from jax.experimental.pallas import tpu as pltpu
from jax.sharding import PartitionSpec as P

F32 = jnp.float32
SIGNS = (-1, 0, 1)
Q = [(a, b, c) for a in SIGNS for b in SIGNS for c in SIGNS]


def qi(a, b, c):
    return 9 * (a + 1) + 3 * (b + 1) + (c + 1)


def mi(i, j, k):
    return 9 * i + 3 * j + k


NNZ = [(i > 0) + (j > 0) + (k > 0) for i in range(3) for j in range(3) for k in range(3)]


def slots(rows):
    first, second, sums = [], [], []
    for q, (a, b, c) in enumerate(Q):
        for x in range(rows):
            left = (a >= 0 and x == 0) or (a == 1 and x == 1)
            right = (a <= 0 and x == rows - 1) or (a == -1 and x == rows - 2)
            (first if left or right else second).append((("v", q, x), b))
    for x in range(rows):
        second.append((("w", x), 0))
    for a in SIGNS:
        for b in SIGNS:
            for s in range(2):
                for x in range(rows):
                    sums.append((("s", a, b, s, x), -b))
    table = {}
    groups = [first + sums[64:], second, sums[:64]]
    for g, group in enumerate(groups):
        for i, (key, kind) in enumerate(group):
            table[key] = (g, 2 * i, kind)
    return table, 2 * len(first)


def turn(v, shift, axis):
    shift = shift % v.shape[axis]
    return v if shift == 0 else pltpu.roll(v, shift, axis)


def lanes():
    return lax.broadcasted_iota(jnp.int32, (8, 128), 1)


def outgoing(block, lane, kind):
    return turn(block, {0: lane + 1, 1: lane, -1: lane + 2}[kind], 1)


def incoming(packed, lane, kind, b=0):
    return turn(packed, {0: 127, 1: 0, -1: 126}[kind] - lane - b, 1)


def shift_y(main, rolled_outer, b, lane):
    if b == 0:
        return main, rolled_outer
    edge = lane == (127 if b == 1 else 0)
    rolled = turn(main, -b, 1)
    return jnp.where(edge, rolled_outer, rolled), jnp.where(edge, rolled, rolled_outer)


def along(values, pass_):
    values = list(values)
    for step in (1, 3, 9):
        for start in range(27):
            if (start // step) % 3 == 0:
                at = (start, start + step, start + 2 * step)
                for i, new in zip(at, pass_(*[values[j] for j in at])):
                    values[i] = new
    return values


def moments(values):
    def pass_(lo, mid, hi):
        both = lo + hi
        return both + mid, hi - lo, both
    return along(values, pass_)


def dual_moments(values):
    return along(values, lambda lo, mid, hi: (mid, hi - lo, (hi - mid) + (lo - mid)))


def from_moments(values):
    return along(values, lambda m0, m1, m2: (m2 - m1, m0 - (m2 + m2), m2 + m1))


def from_dual(values):
    def pass_(z0, z1, z2):
        both = z0 + z2
        return both - z1, z0, both + z1
    return along(values, pass_)


def collide(f, solid, scale):
    m = moments(f)
    rho = m[0]
    inverse = 1.0 / rho
    jx, jy, jz = m[mi(1, 0, 0)], m[mi(0, 1, 0)], m[mi(0, 0, 1)]
    ux, uy, uz = jx * inverse, jy * inverse, jz * inverse
    xx, yy, zz = jx * ux, jy * uy, jz * uz
    third = rho * (1.0 / 3.0)
    ninth = rho * (1.0 / 9.0)
    e = [None] * 27
    e[mi(2, 0, 0)], e[mi(0, 2, 0)], e[mi(0, 0, 2)] = third + xx, third + yy, third + zz
    e[mi(1, 1, 0)], e[mi(1, 0, 1)], e[mi(0, 1, 1)] = jx * uy, jx * uz, jy * uz
    jx3, jy3, jz3 = jx * (1.0 / 3.0), jy * (1.0 / 3.0), jz * (1.0 / 3.0)
    e[mi(1, 2, 0)] = e[mi(1, 0, 2)] = jx3
    e[mi(2, 1, 0)] = e[mi(0, 1, 2)] = jy3
    e[mi(2, 0, 1)] = e[mi(0, 2, 1)] = jz3
    e[mi(2, 2, 0)] = ninth + (xx + yy) * (1.0 / 3.0)
    e[mi(2, 0, 2)] = ninth + (xx + zz) * (1.0 / 3.0)
    e[mi(0, 2, 2)] = ninth + (yy + zz) * (1.0 / 3.0)
    e[mi(2, 1, 1)] = e[mi(0, 1, 1)] * (1.0 / 3.0)
    e[mi(1, 2, 1)] = e[mi(1, 0, 1)] * (1.0 / 3.0)
    e[mi(1, 1, 2)] = e[mi(1, 1, 0)] * (1.0 / 3.0)
    e[mi(1, 2, 2)], e[mi(2, 1, 2)], e[mi(2, 2, 1)] = jx * (1.0 / 9.0), jy * (1.0 / 9.0), jz * (1.0 / 9.0)
    e[mi(2, 2, 2)] = (third + (xx + yy + zz)) * (1.0 / 9.0)
    z = []
    for i in range(27):
        if i in (0, 1, 3, 9):
            z.append(jnp.zeros_like(rho))
        else:
            z.append((m[i] if e[i] is None else m[i] - e[i]) * scale[i])
    h = from_moments(z)
    out = [jnp.where(solid, f[26 - q], f[q] - h[q]) for q in range(27)]
    return out, (ux, uy, uz)


def pull_back(v, u, solid, scale):
    ux, uy, uz = u
    z = [y * s for y, s in zip(dual_moments(v), scale)]

    def at(i, j, k):
        return z[mi(i, j, k)]

    third = 1.0 / 3.0
    top = at(2, 2, 2) * third
    d_xy, d_xz, d_yz = at(2, 2, 0) + top, at(2, 0, 2) + top, at(0, 2, 2) + top
    q_xx = at(2, 0, 0) + (at(2, 2, 0) + d_xz) * third
    q_yy = at(0, 2, 0) + (at(0, 2, 2) + d_xy) * third
    q_zz = at(0, 0, 2) + (at(2, 0, 2) + d_yz) * third
    base = at(0, 0, 0) + (q_xx + (at(0, 2, 0) + at(0, 0, 2) + at(0, 2, 2) * third)) * third
    b_x = at(1, 0, 0) + (at(1, 2, 0) + at(1, 0, 2) + at(1, 2, 2) * third) * third
    b_y = at(0, 1, 0) + (at(2, 1, 0) + at(0, 1, 2) + at(2, 1, 2) * third) * third
    b_z = at(0, 0, 1) + (at(2, 0, 1) + at(0, 2, 1) + at(2, 2, 1) * third) * third
    q_xy = at(1, 1, 0) + at(1, 1, 2) * third
    q_xz = at(1, 0, 1) + at(1, 2, 1) * third
    q_yz = at(0, 1, 1) + at(2, 1, 1) * third
    p_x = (q_xx + q_xx) * ux + q_xy * uy + q_xz * uz
    p_y = q_xy * ux + (q_yy + q_yy) * uy + q_yz * uz
    p_z = q_xz * ux + q_yz * uy + (q_zz + q_zz) * uz
    quad = (p_x * ux + p_y * uy + p_z * uz) * 0.5
    z[0] = z[0] - (base - quad)
    z[mi(1, 0, 0)] = z[mi(1, 0, 0)] - (b_x + p_x)
    z[mi(0, 1, 0)] = z[mi(0, 1, 0)] - (b_y + p_y)
    z[mi(0, 0, 1)] = z[mi(0, 0, 1)] - (b_z + p_z)
    h = from_dual(z)
    return [jnp.where(solid, v[26 - q], v[q] - h[q]) for q in range(27)]


PIECES = 3


def first_kernel(rows, rates_in, f_in, wall_in, cot_in, cot, scale_out, sums, speed, solid_out, packed,
                 raw_right,
                 rates, f, wall, sems):
    copies = [pltpu.make_async_copy(rates_in, rates, sems.at[0]), pltpu.make_async_copy(wall_in, wall, sems.at[1])]
    for array, (source, target) in enumerate(((f_in, f), (cot_in, cot))):
        for piece in range(PIECES):
            part = pl.ds(27 // PIECES * piece, 27 // PIECES)
            copies.append(pltpu.make_async_copy(
                source.at[part], target.at[part], sems.at[2 + PIECES * array + piece]))
    for copy in copies:
        copy.start()
    for copy in copies[:2 + PIECES]:
        copy.wait()
    for i in range(27):
        scale_out[i] = jnp.full((8, 128), rates[i] * (0.5 ** NNZ[i]), F32)
    scale = [rates[i] * (0.5 ** NNZ[i]) for i in range(27)]
    plane = lax.broadcasted_iota(jnp.int32, (8, 128), 0)
    boundary = (plane == 0) | (plane == 7)
    lane = lanes()
    table, _ = slots(rows)
    for x in range(rows):
        at = pl.ds(x, 8, stride=rows)
        solid = boundary | (wall[at, :] == 1)
        solid_out[x] = jnp.where(solid, 1.0, 0.0)
        out, u = collide([f[q, at, :] for q in range(27)], solid, scale)
        for k in range(3):
            speed[k, x] = u[k]
        for a in SIGNS:
            for b in SIGNS:
                low = turn(out[qi(a, b, -1)], -1, 0)
                high = turn(out[qi(a, b, 1)], 1, 0)
                i = 2 * (3 * (a + 1) + b + 1)
                sums[i, x] = out[qi(a, b, 0)] + (low + high)
                sums[i + 1, x] = high - low
    for copy in copies[2 + PIECES:]:
        copy.wait()
    raw_rows(rows, -1, cot, raw_right, 0)
    raw_right[RAW_ROWS:] = jnp.zeros((padded(RAW_ROWS) - RAW_ROWS, 128), F32)
    pieces = [jnp.zeros((8, 128), F32) for _ in range(3)]
    for key, (g, i, kind) in table.items():
        if key[0] == "v":
            block = cot[key[1], pl.ds(key[2], 8, stride=rows), :]
        elif key[0] == "w":
            block = solid_out[key[1]]
        else:
            block = sums[2 * (3 * (key[1] + 1) + key[2] + 1) + key[3], key[4]]
        mine = (lane == i) | (lane == i + 1)
        pieces[g] = jnp.where(mine, outgoing(block, i, kind), pieces[g])
    for g in range(3):
        packed[g] = pieces[g]


FULL = 9


def edge_rows(rows, side):
    near, far = (0, 1) if side == 1 else (rows - 1, rows - 2)
    keys = [(q, near) for q, c in enumerate(Q) if c[0] == side]
    keys += [(q, near) for q, c in enumerate(Q) if c[0] == 0]
    return keys + [(q, far) for q, c in enumerate(Q) if c[0] == side]


def raw_at(k, gap):
    return 8 * k if k < FULL else 8 * FULL + gap + 6 * (k - FULL)


RAW_ROWS = 8 * FULL + 6 * 18
SMALL_ROWS = 8 + 6 * 8


def padded(count):
    return (count + 7) // 8 * 8


def raw_rows(rows, side, cot, message, gap):
    for k, (q, x) in enumerate(edge_rows(rows, side)):
        at = raw_at(k, gap)
        if k < FULL:
            message[at:at + 8] = cot[q, pl.ds(x, 8, stride=rows), :]
        else:
            message[at:at + 6] = cot[q, pl.ds(x + rows * (1 + Q[q][2]), 6, stride=rows), :]


def planes(ref, at):
    start = min(at - 1, ref.shape[0] - 8)
    return turn(ref[start:start + 8], 1 - (at - start), 0)


def second_kernel(rows, cot, sums, solid_in, from_left, from_right, to_left, to_right, own, merged):
    lane = lanes()
    table, used = slots(rows)
    halo = []
    for g in range(3):
        takes_left = jnp.zeros((8, 128), jnp.bool_)
        for key, (h, i, kind) in table.items():
            if h == g and kind <= 0:
                takes_left = takes_left | (lane == i)
            if h == g and kind == -1:
                takes_left = takes_left | (lane == i + 1)
        halo.append(jnp.where(takes_left, from_left[g], from_right[g]))
        merged[g] = halo[g]

    def outer(key, b=0):
        g, i, kind = table[key]
        return incoming(halo[g], i, kind, b)

    def both(a, x):
        parts = {}
        for b in SIGNS:
            for s in range(2):
                i = 2 * (3 * (a + 1) + b + 1) + s
                parts[b, s] = shift_y(sums[i, x], outer(("s", a, b, s, x), -b), -b, lane)
        result = []
        for n in range(2):
            result.append((
                parts[0, 0][n] + (parts[-1, 0][n] + parts[1, 0][n]),
                parts[1, 0][n] - parts[-1, 0][n],
                parts[0, 1][n] + (parts[-1, 1][n] + parts[1, 1][n]),
            ))
        return result

    t = {(a, x): both(a, x) for a in SIGNS for x in range(rows)}

    def total(x, n):
        terms = [(a, t[a, x - a][n]) for a in SIGNS if 0 <= x - a < rows]
        density = functools.reduce(jnp.add, [v[0] for _, v in terms])
        along_y = functools.reduce(jnp.add, [v[1] for _, v in terms])
        along_z = functools.reduce(jnp.add, [v[2] for _, v in terms])
        moving = [(a, v[0]) for a, v in terms if a]
        along_x = jnp.zeros((8, 128), F32)
        for a, v in moving:
            along_x = along_x + v if a == 1 else along_x - v
        return density, along_x, along_y, along_z

    for x in range(-1, rows + 1):
        for n in range(2):
            for k, v in enumerate(total(x, n)):
                own[k, 2 * (x + 1) + n] = v

    for side, message in ((1, to_left), (-1, to_right)):
        near, far = (0, 1) if side == 1 else (rows - 1, rows - 2)
        both_parts = message.shape[0] > SMALL_ROWS
        at = 8 * FULL if both_parts else 0
        items = RAW_ROWS + 8 if both_parts else 8
        if both_parts:
            raw_rows(rows, side, cot, message, 8)
            end = RAW_ROWS + SMALL_ROWS
            message[end:] = jnp.zeros((padded(end) - end, 128), F32)
        extra = []
        for n in range(2):
            row = list(t[-side, near][n])
            still, moved = t[0, near][n], t[-side, far][n]
            row += [still[0] + moved[0], moved[0] if side == -1 else -moved[0]]
            row += [still[1] + moved[1], still[2] + moved[2]]
            row.append(solid_in[near] if n == 0 else outer(("w", near)))
            extra.append(row)
        columns = halo[0]
        for k in range(8):
            message[items + 6 * k:items + 6 * k + 6] = extra[0][k][1:7]
            i = used + 2 * k
            columns = jnp.where((lane == i) | (lane == i + 1), turn(extra[1][k], i + 1, 1), columns)
        message[at:at + 8] = columns


def outer_rows(rows):
    return [x for x in range(-1, rows + 1) if not 0 < x < rows - 1]


def gathered(rows, x, q, cot, turned, lane, remote=None):
    table, _ = slots(rows)
    a, b, c = Q[q]
    source = x + a
    if 0 <= source < rows:
        main = turn(cot[q, pl.ds(source, 8, stride=rows), :], -c, 0)
        group, i, kind = table["v", q, source]
    else:
        load, group, i, kind = remote[q, source]
        main = load()
    outer = incoming(turned[group, c], i, kind, b)
    return shift_y(main, outer, b, lane)


def middle_kernel(rows, scale_in, cot, solid_in, own, merged, inner, known):
    scale = [scale_in[i] for i in range(27)]
    lane = lanes()
    table, _ = slots(rows)
    turned = {(g, c): turn(merged[g], -c, 0) for g in range(2) for c in SIGNS}
    for x in range(1, rows - 1):
        v = [gathered(rows, x, q, cot, turned, lane) for q in range(27)]
        for n in range(2):
            total = [own[k, 2 * (x + 1) + n] for k in range(4)]
            inverse = 1.0 / total[0]
            if n == 0:
                wall = solid_in[x]
            else:
                g, i, kind = table["w", x]
                wall = incoming(merged[g], i, kind)
            out = pull_back([t[n] for t in v], [t * inverse for t in total[1:]], wall > 0.5, scale)
            for q in range(27):
                inner[q, 2 * (x - 1) + n] = out[q]
    for j, x in enumerate(outer_rows(rows)):
        for q in range(27):
            if 0 <= x + Q[q][0] < rows:
                known[q, 2 * j], known[q, 2 * j + 1] = gathered(rows, x, q, cot, turned, lane)


def outer_gradient(rows, side, scale, solid_in, own, merged, known, raw, gap, extra, columns_at, items_at, g1):
    lane = lanes()
    table, used = slots(rows)
    remote = {}
    def load(k, c):
        at = raw_at(k, gap)
        return turn(raw[at:at + 8], -c, 0) if k < FULL else planes(raw, at)

    for k, (q, x) in enumerate(edge_rows(rows, side)):
        _, i, kind = table["v", q, x]
        remote[q, x + side * rows] = (functools.partial(load, k, Q[q][2]), "far", i, kind)
    columns = extra[columns_at:columns_at + 8]
    turned = {("far", c): turn(columns, -c, 0) for c in SIGNS}
    plane = lax.broadcasted_iota(jnp.int32, (8, 128), 0)
    boundary = (plane == 0) | (plane == 7)
    near = rows - 1 if side == 1 else 0
    for j, x in enumerate(outer_rows(rows)):
        if x not in (near, near + side):
            continue
        v = []
        for q in range(27):
            if 0 <= x + Q[q][0] < rows:
                v.append((known[q, 2 * j], known[q, 2 * j + 1]))
            else:
                v.append(gathered(rows, x, q, None, turned, lane, remote))
        for n in range(2):
            def got(k):
                return planes(extra, items_at + 6 * k) if n == 0 else incoming(columns, used + 2 * k, 0)

            total = [own[k, 2 * (x + 1) + n] for k in range(4)]
            if x == near:
                total = [total[0] + got(0), total[1] - got(0) if side == 1 else total[1] + got(0),
                         total[2] + got(1), total[3] + got(2)]
                if n == 0:
                    wall = solid_in[x]
                else:
                    g, i, kind = table["w", x]
                    wall = incoming(merged[g], i, kind)
            else:
                total = [total[k] + got(3 + k) for k in range(4)]
                wall = got(7)
            inverse = 1.0 / total[0]
            g = pull_back([t[n] for t in v], [t * inverse for t in total[1:]], boundary | (wall > 0.5), scale)
            for q in range(27):
                if 0 <= x - Q[q][0] < rows:
                    g1[q, 2 * (j % 2) + n] = g[q]


def pulled_row(rows, x, arrays, speed, solid_in, scale, lane):
    v = []
    for q, (a, b, c) in enumerate(Q):
        array, r = arrays(x + a)
        main = array[q, r]
        if b:
            main = shift_y(main, turn(array[q, r + 1], -b, 1), b, lane)[0]
        v.append(turn(main, -c, 0))
    return pull_back(v, [speed[k, x] for k in range(3)], solid_in[x] > 0.5, scale)


def low_kernel(rows, scale_in, speed, solid_in, own, merged, inner, known, raw, extra, done, g1):
    scale = [scale_in[i] for i in range(27)]
    lane = lanes()
    outer_gradient(rows, -1, scale, solid_in, own, merged, known, raw, 0, extra, 0, 8, g1)

    def arrays(x):
        return (g1, 2 * (x + 1)) if x < 1 else (inner, 2 * (x - 1))

    for x in range(rows - 2):
        result = pulled_row(rows, x, arrays, speed, solid_in, scale, lane)
        for q in range(27):
            done[q, x] = result[q]


def last_kernel(rows, scale_in, speed, solid_in, own, merged, inner, known, done, from_high, out_hbm, high, out, sems):
    scale = [scale_in[i] for i in range(27)]
    lane = lanes()
    outer_gradient(rows, 1, scale, solid_in, own, merged, known, from_high, 8, from_high, 8 * FULL, RAW_ROWS + 8, high)

    def arrays(x):
        return (inner, 2 * (x - 1)) if x < rows - 1 else (high, 2 * (x - rows + 1))

    for x in range(rows):
        if x < rows - 2:
            result = [done[q, x] for q in range(27)]
        else:
            result = pulled_row(rows, x, arrays, speed, solid_in, scale, lane)
        for q in range(27):
            out[q, pl.ds(x, 8, stride=rows), :] = result[q]
    copies = []
    for piece in range(PIECES):
        part = pl.ds(27 // PIECES * piece, 27 // PIECES)
        copies.append(pltpu.make_async_copy(out.at[part], out_hbm.at[part], sems.at[piece]))
    for copy in copies:
        copy.start()
    for copy in copies:
        copy.wait()


def call(kernel, name, out_shapes, scratch, operands, space=pltpu.VMEM, work=0, out_space=pltpu.VMEM):
    return pl.pallas_call(
        kernel,
        out_shape=[jax.ShapeDtypeStruct(s, F32) for s in out_shapes],
        in_specs=[pl.BlockSpec(memory_space=space)] * len(operands),
        out_specs=[pl.BlockSpec(memory_space=out_space)] * len(out_shapes),
        scratch_shapes=scratch,
        compiler_params=pltpu.CompilerParams(vmem_limit_bytes=32 * 1024 * 1024),
        cost_estimate=pl.CostEstimate(flops=work, bytes_accessed=0 if work else 0, transcendentals=0) if work else None,
        name=name,
    )(*operands)


def ring(block, axis, step):
    size = lax.axis_size(axis)
    return lax.ppermute(block, axis, [(i, (i + step) % size) for i in range(size)])


def swap(block, axis, first):
    size = lax.axis_size(axis)
    route = []
    for i in range(first, size + first, 2):
        route += [(i % size, (i + 1) % size), ((i + 1) % size, i % size)]
    return lax.ppermute(block, axis, route)


def shards(checkpoint, rates, wall_mask, cotangent):
    planes, rows, width = checkpoint.shape[1:]
    f = checkpoint.reshape(27, planes * rows, width)
    cot = cotangent.reshape(27, planes * rows, width)
    wall = wall_mask.reshape(planes * rows, width)
    tile = (planes, width)
    lattice = (27, planes * rows, width)
    cot, scale, sums, speed, solid, packed, raw_right = call(
        functools.partial(first_kernel, rows), "collide",
        [lattice, (27,) + tile, (18, rows) + tile, (3, rows) + tile, (rows,) + tile, (3,) + tile,
         (padded(RAW_ROWS), width)],
        [pltpu.SMEM((27,), F32), pltpu.VMEM(lattice, F32), pltpu.VMEM(lattice[1:], jnp.int32),
         pltpu.SemaphoreType.DMA((2 + 2 * PIECES,))],
        tuple(pltpu.with_memory_space_constraint(v, pltpu.HBM) for v in (rates, f, wall, cot)), pltpu.HBM)
    raw_low = ring(raw_right, "gx", 1)
    pairs = [swap(packed, "gy", first) for first in (0, 1)]
    even = lax.axis_index("gy") % 2 == 0
    from_right = jnp.where(even, pairs[0], pairs[1])
    from_left = jnp.where(even, pairs[1], pairs[0])
    to_left, small_right, own, merged = call(
        functools.partial(second_kernel, rows), "pack",
        [(padded(RAW_ROWS + SMALL_ROWS), width), (SMALL_ROWS, width), (4, 2 * rows + 4) + tile, (3,) + tile], [],
        (cot, sums, solid, from_left, from_right))
    small_low = ring(small_right, "gx", 1)
    from_high = ring(to_left, "gx", -1)
    inner, known = call(
        functools.partial(middle_kernel, rows), "inner_rows",
        [(27, 2 * rows - 4) + tile, (27, 8) + tile], [],
        (scale, cot, solid, own, merged))
    (done,) = call(
        functools.partial(low_kernel, rows), "low_rows",
        [(27, rows - 2) + tile], [pltpu.VMEM((27, 4) + tile, F32)],
        (scale, speed, solid, own, merged, inner, known, raw_low, small_low), work=2000000000)
    (out,) = call(
        functools.partial(last_kernel, rows), "gradient",
        [lattice],
        [pltpu.VMEM((27, 4) + tile, F32), pltpu.VMEM(lattice, F32), pltpu.SemaphoreType.DMA((PIECES,))],
        (scale, speed, solid, own, merged, inner, known, done, from_high), out_space=pltpu.HBM)
    return out.reshape(checkpoint.shape)


def solution(mesh):
    in_specs = (P(None, None, "gx", "gy"), P(), P(None, "gx", "gy"), P(None, None, "gx", "gy"))
    out_specs = P(None, None, "gx", "gy")
    return jax.shard_map(shards, mesh=mesh, in_specs=in_specs, out_specs=out_specs, check_vma=False)
```

```python
import functools
import jax
import jax.numpy as jnp
from jax import lax
from jax.experimental import pallas as pl
from jax.experimental.pallas import tpu as pltpu
from jax.sharding import PartitionSpec as P

F32 = jnp.float32
SIGNS = (-1, 0, 1)
Q = [(a, b, c) for a in SIGNS for b in SIGNS for c in SIGNS]


def qi(a, b, c):
    return 9 * (a + 1) + 3 * (b + 1) + (c + 1)


def mi(i, j, k):
    return 9 * i + 3 * j + k


NNZ = [(i > 0) + (j > 0) + (k > 0) for i in range(3) for j in range(3) for k in range(3)]


def slots(rows):
    first, second, sums = [], [], []
    for q, (a, b, c) in enumerate(Q):
        for x in range(rows):
            left = (a >= 0 and x == 0) or (a == 1 and x == 1)
            right = (a <= 0 and x == rows - 1) or (a == -1 and x == rows - 2)
            (first if left or right else second).append((("v", q, x), b))
    for x in range(rows):
        second.append((("w", x), 0))
    for a in SIGNS:
        for b in SIGNS:
            for s in range(2):
                for x in range(rows):
                    sums.append((("s", a, b, s, x), -b))
    table = {}
    groups = [first + sums[64:], second, sums[:64]]
    for g, group in enumerate(groups):
        for i, (key, kind) in enumerate(group):
            table[key] = (g, 2 * i, kind)
    return table, 2 * len(first)


def turn(v, shift, axis):
    shift = shift % v.shape[axis]
    return v if shift == 0 else pltpu.roll(v, shift, axis)


def lanes():
    return lax.broadcasted_iota(jnp.int32, (8, 128), 1)


def outgoing(block, lane, kind):
    return turn(block, {0: lane + 1, 1: lane, -1: lane + 2}[kind], 1)


def incoming(packed, lane, kind, b=0):
    return turn(packed, {0: 127, 1: 0, -1: 126}[kind] - lane - b, 1)


def shift_y(main, rolled_outer, b, lane):
    if b == 0:
        return main, rolled_outer
    edge = lane == (127 if b == 1 else 0)
    rolled = turn(main, -b, 1)
    return jnp.where(edge, rolled_outer, rolled), jnp.where(edge, rolled, rolled_outer)


def along(values, pass_):
    values = list(values)
    for step in (1, 3, 9):
        for start in range(27):
            if (start // step) % 3 == 0:
                at = (start, start + step, start + 2 * step)
                for i, new in zip(at, pass_(*[values[j] for j in at])):
                    values[i] = new
    return values


def moments(values):
    def pass_(lo, mid, hi):
        both = lo + hi
        return both + mid, hi - lo, both
    return along(values, pass_)


def dual_moments(values):
    return along(values, lambda lo, mid, hi: (mid, hi - lo, (hi - mid) + (lo - mid)))


def from_moments(values):
    return along(values, lambda m0, m1, m2: (m2 - m1, m0 - (m2 + m2), m2 + m1))


def from_dual(values):
    def pass_(z0, z1, z2):
        both = z0 + z2
        return both - z1, z0, both + z1
    return along(values, pass_)


def collide(f, solid, scale):
    m = moments(f)
    rho = m[0]
    inverse = 1.0 / rho
    jx, jy, jz = m[mi(1, 0, 0)], m[mi(0, 1, 0)], m[mi(0, 0, 1)]
    ux, uy, uz = jx * inverse, jy * inverse, jz * inverse
    xx, yy, zz = jx * ux, jy * uy, jz * uz
    third = rho * (1.0 / 3.0)
    ninth = rho * (1.0 / 9.0)
    e = [None] * 27
    e[mi(2, 0, 0)], e[mi(0, 2, 0)], e[mi(0, 0, 2)] = third + xx, third + yy, third + zz
    e[mi(1, 1, 0)], e[mi(1, 0, 1)], e[mi(0, 1, 1)] = jx * uy, jx * uz, jy * uz
    jx3, jy3, jz3 = jx * (1.0 / 3.0), jy * (1.0 / 3.0), jz * (1.0 / 3.0)
    e[mi(1, 2, 0)] = e[mi(1, 0, 2)] = jx3
    e[mi(2, 1, 0)] = e[mi(0, 1, 2)] = jy3
    e[mi(2, 0, 1)] = e[mi(0, 2, 1)] = jz3
    e[mi(2, 2, 0)] = ninth + (xx + yy) * (1.0 / 3.0)
    e[mi(2, 0, 2)] = ninth + (xx + zz) * (1.0 / 3.0)
    e[mi(0, 2, 2)] = ninth + (yy + zz) * (1.0 / 3.0)
    e[mi(2, 1, 1)] = e[mi(0, 1, 1)] * (1.0 / 3.0)
    e[mi(1, 2, 1)] = e[mi(1, 0, 1)] * (1.0 / 3.0)
    e[mi(1, 1, 2)] = e[mi(1, 1, 0)] * (1.0 / 3.0)
    e[mi(1, 2, 2)], e[mi(2, 1, 2)], e[mi(2, 2, 1)] = jx * (1.0 / 9.0), jy * (1.0 / 9.0), jz * (1.0 / 9.0)
    e[mi(2, 2, 2)] = (third + (xx + yy + zz)) * (1.0 / 9.0)
    z = []
    for i in range(27):
        if i in (0, 1, 3, 9):
            z.append(jnp.zeros_like(rho))
        else:
            z.append((m[i] if e[i] is None else m[i] - e[i]) * scale[i])
    h = from_moments(z)
    out = [jnp.where(solid, f[26 - q], f[q] - h[q]) for q in range(27)]
    return out, (ux, uy, uz)


def pull_back(v, u, solid, scale):
    ux, uy, uz = u
    z = [y * s for y, s in zip(dual_moments(v), scale)]

    def at(i, j, k):
        return z[mi(i, j, k)]

    third = 1.0 / 3.0
    top = at(2, 2, 2) * third
    d_xy, d_xz, d_yz = at(2, 2, 0) + top, at(2, 0, 2) + top, at(0, 2, 2) + top
    q_xx = at(2, 0, 0) + (at(2, 2, 0) + d_xz) * third
    q_yy = at(0, 2, 0) + (at(0, 2, 2) + d_xy) * third
    q_zz = at(0, 0, 2) + (at(2, 0, 2) + d_yz) * third
    base = at(0, 0, 0) + (q_xx + (at(0, 2, 0) + at(0, 0, 2) + at(0, 2, 2) * third)) * third
    b_x = at(1, 0, 0) + (at(1, 2, 0) + at(1, 0, 2) + at(1, 2, 2) * third) * third
    b_y = at(0, 1, 0) + (at(2, 1, 0) + at(0, 1, 2) + at(2, 1, 2) * third) * third
    b_z = at(0, 0, 1) + (at(2, 0, 1) + at(0, 2, 1) + at(2, 2, 1) * third) * third
    q_xy = at(1, 1, 0) + at(1, 1, 2) * third
    q_xz = at(1, 0, 1) + at(1, 2, 1) * third
    q_yz = at(0, 1, 1) + at(2, 1, 1) * third
    p_x = (q_xx + q_xx) * ux + q_xy * uy + q_xz * uz
    p_y = q_xy * ux + (q_yy + q_yy) * uy + q_yz * uz
    p_z = q_xz * ux + q_yz * uy + (q_zz + q_zz) * uz
    quad = (p_x * ux + p_y * uy + p_z * uz) * 0.5
    z[0] = z[0] - (base - quad)
    z[mi(1, 0, 0)] = z[mi(1, 0, 0)] - (b_x + p_x)
    z[mi(0, 1, 0)] = z[mi(0, 1, 0)] - (b_y + p_y)
    z[mi(0, 0, 1)] = z[mi(0, 0, 1)] - (b_z + p_z)
    h = from_dual(z)
    return [jnp.where(solid, v[26 - q], v[q] - h[q]) for q in range(27)]


PIECES = 1


def first_kernel(rows, rates_in, f_in, wall_in, cot_in, cot, scale_out, sums, speed, solid_out, packed,
                 raw_right,
                 rates, f, wall, sems):
    copies = [pltpu.make_async_copy(rates_in, rates, sems.at[0]), pltpu.make_async_copy(wall_in, wall, sems.at[1])]
    for array, (source, target) in enumerate(((f_in, f), (cot_in, cot))):
        for piece in range(PIECES):
            part = pl.ds(27 // PIECES * piece, 27 // PIECES)
            copies.append(pltpu.make_async_copy(
                source.at[part], target.at[part], sems.at[2 + PIECES * array + piece]))
    for copy in copies:
        copy.start()
    for copy in copies[:2 + PIECES]:
        copy.wait()
    for i in range(27):
        scale_out[i] = jnp.full((8, 128), rates[i] * (0.5 ** NNZ[i]), F32)
    scale = [rates[i] * (0.5 ** NNZ[i]) for i in range(27)]
    plane = lax.broadcasted_iota(jnp.int32, (8, 128), 0)
    boundary = (plane == 0) | (plane == 7)
    lane = lanes()
    table, _ = slots(rows)
    for x in range(rows):
        at = pl.ds(x, 8, stride=rows)
        solid = boundary | (wall[at, :] == 1)
        solid_out[x] = jnp.where(solid, 1.0, 0.0)
        out, u = collide([f[q, at, :] for q in range(27)], solid, scale)
        for k in range(3):
            speed[k, x] = u[k]
        for a in SIGNS:
            for b in SIGNS:
                low = turn(out[qi(a, b, -1)], -1, 0)
                high = turn(out[qi(a, b, 1)], 1, 0)
                i = 2 * (3 * (a + 1) + b + 1)
                sums[i, x] = out[qi(a, b, 0)] + (low + high)
                sums[i + 1, x] = high - low
    for copy in copies[2 + PIECES:]:
        copy.wait()
    raw_rows(rows, -1, cot, raw_right, 0)
    raw_right[RAW_ROWS:] = jnp.zeros((padded(RAW_ROWS) - RAW_ROWS, 128), F32)
    pieces = [jnp.zeros((8, 128), F32) for _ in range(3)]
    for key, (g, i, kind) in table.items():
        if key[0] == "v":
            block = cot[key[1], pl.ds(key[2], 8, stride=rows), :]
        elif key[0] == "w":
            block = solid_out[key[1]]
        else:
            block = sums[2 * (3 * (key[1] + 1) + key[2] + 1) + key[3], key[4]]
        mine = (lane == i) | (lane == i + 1)
        pieces[g] = jnp.where(mine, outgoing(block, i, kind), pieces[g])
    for g in range(3):
        packed[g] = pieces[g]


FULL = 9


def edge_rows(rows, side):
    near, far = (0, 1) if side == 1 else (rows - 1, rows - 2)
    keys = [(q, near) for q, c in enumerate(Q) if c[0] == side]
    keys += [(q, near) for q, c in enumerate(Q) if c[0] == 0]
    return keys + [(q, far) for q, c in enumerate(Q) if c[0] == side]


def raw_at(k, gap):
    return 8 * k if k < FULL else 8 * FULL + gap + 6 * (k - FULL)


RAW_ROWS = 8 * FULL + 6 * 18
SMALL_ROWS = 8 + 6 * 8


def padded(count):
    return (count + 7) // 8 * 8


def raw_rows(rows, side, cot, message, gap):
    for k, (q, x) in enumerate(edge_rows(rows, side)):
        at = raw_at(k, gap)
        if k < FULL:
            message[at:at + 8] = cot[q, pl.ds(x, 8, stride=rows), :]
        else:
            message[at:at + 6] = cot[q, pl.ds(x + rows * (1 + Q[q][2]), 6, stride=rows), :]


def planes(ref, at):
    start = min(at - 1, ref.shape[0] - 8)
    return turn(ref[start:start + 8], 1 - (at - start), 0)


def second_kernel(rows, cot, sums, solid_in, from_left, from_right, to_left, to_right, own, merged):
    lane = lanes()
    table, used = slots(rows)
    halo = []
    for g in range(3):
        takes_left = jnp.zeros((8, 128), jnp.bool_)
        for key, (h, i, kind) in table.items():
            if h == g and kind <= 0:
                takes_left = takes_left | (lane == i)
            if h == g and kind == -1:
                takes_left = takes_left | (lane == i + 1)
        halo.append(jnp.where(takes_left, from_left[g], from_right[g]))
        merged[g] = halo[g]

    def outer(key, b=0):
        g, i, kind = table[key]
        return incoming(halo[g], i, kind, b)

    def both(a, x):
        parts = {}
        for b in SIGNS:
            for s in range(2):
                i = 2 * (3 * (a + 1) + b + 1) + s
                parts[b, s] = shift_y(sums[i, x], outer(("s", a, b, s, x), -b), -b, lane)
        result = []
        for n in range(2):
            result.append((
                parts[0, 0][n] + (parts[-1, 0][n] + parts[1, 0][n]),
                parts[1, 0][n] - parts[-1, 0][n],
                parts[0, 1][n] + (parts[-1, 1][n] + parts[1, 1][n]),
            ))
        return result

    t = {(a, x): both(a, x) for a in SIGNS for x in range(rows)}

    def total(x, n):
        terms = [(a, t[a, x - a][n]) for a in SIGNS if 0 <= x - a < rows]
        density = functools.reduce(jnp.add, [v[0] for _, v in terms])
        along_y = functools.reduce(jnp.add, [v[1] for _, v in terms])
        along_z = functools.reduce(jnp.add, [v[2] for _, v in terms])
        moving = [(a, v[0]) for a, v in terms if a]
        along_x = jnp.zeros((8, 128), F32)
        for a, v in moving:
            along_x = along_x + v if a == 1 else along_x - v
        return density, along_x, along_y, along_z

    for x in range(-1, rows + 1):
        for n in range(2):
            for k, v in enumerate(total(x, n)):
                own[k, 2 * (x + 1) + n] = v

    for side, message in ((1, to_left), (-1, to_right)):
        near, far = (0, 1) if side == 1 else (rows - 1, rows - 2)
        both_parts = message.shape[0] > SMALL_ROWS
        at = 8 * FULL if both_parts else 0
        items = RAW_ROWS + 8 if both_parts else 8
        if both_parts:
            raw_rows(rows, side, cot, message, 8)
            end = RAW_ROWS + SMALL_ROWS
            message[end:] = jnp.zeros((padded(end) - end, 128), F32)
        extra = []
        for n in range(2):
            row = list(t[-side, near][n])
            still, moved = t[0, near][n], t[-side, far][n]
            row += [still[0] + moved[0], moved[0] if side == -1 else -moved[0]]
            row += [still[1] + moved[1], still[2] + moved[2]]
            row.append(solid_in[near] if n == 0 else outer(("w", near)))
            extra.append(row)
        columns = halo[0]
        for k in range(8):
            message[items + 6 * k:items + 6 * k + 6] = extra[0][k][1:7]
            i = used + 2 * k
            columns = jnp.where((lane == i) | (lane == i + 1), turn(extra[1][k], i + 1, 1), columns)
        message[at:at + 8] = columns


def outer_rows(rows):
    return [x for x in range(-1, rows + 1) if not 0 < x < rows - 1]


def gathered(rows, x, q, cot, turned, lane, remote=None):
    table, _ = slots(rows)
    a, b, c = Q[q]
    source = x + a
    if 0 <= source < rows:
        main = turn(cot[q, pl.ds(source, 8, stride=rows), :], -c, 0)
        group, i, kind = table["v", q, source]
    else:
        load, group, i, kind = remote[q, source]
        main = load()
    outer = incoming(turned[group, c], i, kind, b)
    return shift_y(main, outer, b, lane)


def middle_kernel(rows, scale_in, cot, solid_in, own, merged, inner, known):
    scale = [scale_in[i] for i in range(27)]
    lane = lanes()
    table, _ = slots(rows)
    turned = {(g, c): turn(merged[g], -c, 0) for g in range(2) for c in SIGNS}
    for x in range(1, rows - 1):
        v = [gathered(rows, x, q, cot, turned, lane) for q in range(27)]
        for n in range(2):
            total = [own[k, 2 * (x + 1) + n] for k in range(4)]
            inverse = 1.0 / total[0]
            if n == 0:
                wall = solid_in[x]
            else:
                g, i, kind = table["w", x]
                wall = incoming(merged[g], i, kind)
            out = pull_back([t[n] for t in v], [t * inverse for t in total[1:]], wall > 0.5, scale)
            for q in range(27):
                inner[q, 2 * (x - 1) + n] = out[q]
    for j, x in enumerate(outer_rows(rows)):
        for q in range(27):
            if 0 <= x + Q[q][0] < rows:
                known[q, 2 * j], known[q, 2 * j + 1] = gathered(rows, x, q, cot, turned, lane)


def outer_gradient(rows, side, scale, solid_in, own, merged, known, raw, gap, extra, columns_at, items_at, g1):
    lane = lanes()
    table, used = slots(rows)
    remote = {}
    def load(k, c):
        at = raw_at(k, gap)
        return turn(raw[at:at + 8], -c, 0) if k < FULL else planes(raw, at)

    for k, (q, x) in enumerate(edge_rows(rows, side)):
        _, i, kind = table["v", q, x]
        remote[q, x + side * rows] = (functools.partial(load, k, Q[q][2]), "far", i, kind)
    columns = extra[columns_at:columns_at + 8]
    turned = {("far", c): turn(columns, -c, 0) for c in SIGNS}
    plane = lax.broadcasted_iota(jnp.int32, (8, 128), 0)
    boundary = (plane == 0) | (plane == 7)
    near = rows - 1 if side == 1 else 0
    for j, x in enumerate(outer_rows(rows)):
        if x not in (near, near + side):
            continue
        v = []
        for q in range(27):
            if 0 <= x + Q[q][0] < rows:
                v.append((known[q, 2 * j], known[q, 2 * j + 1]))
            else:
                v.append(gathered(rows, x, q, None, turned, lane, remote))
        for n in range(2):
            def got(k):
                return planes(extra, items_at + 6 * k) if n == 0 else incoming(columns, used + 2 * k, 0)

            total = [own[k, 2 * (x + 1) + n] for k in range(4)]
            if x == near:
                total = [total[0] + got(0), total[1] - got(0) if side == 1 else total[1] + got(0),
                         total[2] + got(1), total[3] + got(2)]
                if n == 0:
                    wall = solid_in[x]
                else:
                    g, i, kind = table["w", x]
                    wall = incoming(merged[g], i, kind)
            else:
                total = [total[k] + got(3 + k) for k in range(4)]
                wall = got(7)
            inverse = 1.0 / total[0]
            g = pull_back([t[n] for t in v], [t * inverse for t in total[1:]], boundary | (wall > 0.5), scale)
            for q in range(27):
                if 0 <= x - Q[q][0] < rows:
                    g1[q, 2 * (j % 2) + n] = g[q]


def pulled_row(rows, x, arrays, speed, solid_in, scale, lane):
    v = []
    for q, (a, b, c) in enumerate(Q):
        array, r = arrays(x + a)
        main = array[q, r]
        if b:
            main = shift_y(main, turn(array[q, r + 1], -b, 1), b, lane)[0]
        v.append(turn(main, -c, 0))
    return pull_back(v, [speed[k, x] for k in range(3)], solid_in[x] > 0.5, scale)


def low_kernel(rows, scale_in, speed, solid_in, own, merged, inner, known, raw, extra, done, g1):
    scale = [scale_in[i] for i in range(27)]
    lane = lanes()
    outer_gradient(rows, -1, scale, solid_in, own, merged, known, raw, 0, extra, 0, 8, g1)

    def arrays(x):
        return (g1, 2 * (x + 1)) if x < 1 else (inner, 2 * (x - 1))

    for x in range(rows - 2):
        result = pulled_row(rows, x, arrays, speed, solid_in, scale, lane)
        for q in range(27):
            done[q, x] = result[q]


def last_kernel(rows, scale_in, speed, solid_in, own, merged, inner, known, done, from_high, out_hbm, high, out, sems):
    scale = [scale_in[i] for i in range(27)]
    lane = lanes()
    outer_gradient(rows, 1, scale, solid_in, own, merged, known, from_high, 8, from_high, 8 * FULL, RAW_ROWS + 8, high)

    def arrays(x):
        return (inner, 2 * (x - 1)) if x < rows - 1 else (high, 2 * (x - rows + 1))

    for x in range(rows):
        if x < rows - 2:
            result = [done[q, x] for q in range(27)]
        else:
            result = pulled_row(rows, x, arrays, speed, solid_in, scale, lane)
        for q in range(27):
            out[q, pl.ds(x, 8, stride=rows), :] = result[q]
    copies = []
    for piece in range(PIECES):
        part = pl.ds(27 // PIECES * piece, 27 // PIECES)
        copies.append(pltpu.make_async_copy(out.at[part], out_hbm.at[part], sems.at[piece]))
    for copy in copies:
        copy.start()
    for copy in copies:
        copy.wait()


def call(kernel, name, out_shapes, scratch, operands, space=pltpu.VMEM, work=0, out_space=pltpu.VMEM):
    return pl.pallas_call(
        kernel,
        out_shape=[jax.ShapeDtypeStruct(s, F32) for s in out_shapes],
        in_specs=[pl.BlockSpec(memory_space=space)] * len(operands),
        out_specs=[pl.BlockSpec(memory_space=out_space)] * len(out_shapes),
        scratch_shapes=scratch,
        compiler_params=pltpu.CompilerParams(vmem_limit_bytes=32 * 1024 * 1024),
        cost_estimate=pl.CostEstimate(flops=work, bytes_accessed=0 if work else 0, transcendentals=0) if work else None,
        name=name,
    )(*operands)


def ring(block, axis, step):
    size = lax.axis_size(axis)
    return lax.ppermute(block, axis, [(i, (i + step) % size) for i in range(size)])


def swap(block, axis, first):
    size = lax.axis_size(axis)
    route = []
    for i in range(first, size + first, 2):
        route += [(i % size, (i + 1) % size), ((i + 1) % size, i % size)]
    return lax.ppermute(block, axis, route)


def shards(checkpoint, rates, wall_mask, cotangent):
    planes, rows, width = checkpoint.shape[1:]
    f = checkpoint.reshape(27, planes * rows, width)
    cot = cotangent.reshape(27, planes * rows, width)
    wall = wall_mask.reshape(planes * rows, width)
    tile = (planes, width)
    lattice = (27, planes * rows, width)
    cot, scale, sums, speed, solid, packed, raw_right = call(
        functools.partial(first_kernel, rows), "collide",
        [lattice, (27,) + tile, (18, rows) + tile, (3, rows) + tile, (rows,) + tile, (3,) + tile,
         (padded(RAW_ROWS), width)],
        [pltpu.SMEM((27,), F32), pltpu.VMEM(lattice, F32), pltpu.VMEM(lattice[1:], jnp.int32),
         pltpu.SemaphoreType.DMA((2 + 2 * PIECES,))],
        tuple(pltpu.with_memory_space_constraint(v, pltpu.HBM) for v in (rates, f, wall, cot)), pltpu.HBM)
    raw_low = ring(raw_right, "gx", 1)
    across, inside = swap(packed, "gy", 1), swap(packed, "gy", 0)
    odd = lax.axis_index("gy") % 2 == 1
    from_left = jnp.where(odd, inside, across)
    from_right = jnp.where(odd, across, inside)
    to_left, small_right, own, merged = call(
        functools.partial(second_kernel, rows), "pack",
        [(padded(RAW_ROWS + SMALL_ROWS), width), (SMALL_ROWS, width), (4, 2 * rows + 4) + tile, (3,) + tile], [],
        (cot, sums, solid, from_left, from_right))
    small_low = ring(small_right, "gx", 1)
    from_high = ring(to_left, "gx", -1)
    inner, known = call(
        functools.partial(middle_kernel, rows), "inner_rows",
        [(27, 2 * rows - 4) + tile, (27, 8) + tile], [],
        (scale, cot, solid, own, merged))
    (done,) = call(
        functools.partial(low_kernel, rows), "low_rows",
        [(27, rows - 2) + tile], [pltpu.VMEM((27, 4) + tile, F32)],
        (scale, speed, solid, own, merged, inner, known, raw_low, small_low), work=2000000000)
    (out,) = call(
        functools.partial(last_kernel, rows), "gradient",
        [lattice],
        [pltpu.VMEM((27, 4) + tile, F32), pltpu.VMEM(lattice, F32), pltpu.SemaphoreType.DMA((PIECES,))],
        (scale, speed, solid, own, merged, inner, known, done, from_high), out_space=pltpu.HBM)
    return out.reshape(checkpoint.shape)


def solution(mesh):
    in_specs = (P(None, None, "gx", "gy"), P(), P(None, "gx", "gy"), P(None, None, "gx", "gy"))
    out_specs = P(None, None, "gx", "gy")
    return jax.shard_map(shards, mesh=mesh, in_specs=in_specs, out_specs=out_specs, check_vma=False)
```

```python
import functools
import jax
import jax.numpy as jnp
from jax import lax
from jax.experimental import pallas as pl
from jax.experimental.pallas import tpu as pltpu
from jax.sharding import PartitionSpec as P

F32 = jnp.float32
SIGNS = (-1, 0, 1)
Q = [(a, b, c) for a in SIGNS for b in SIGNS for c in SIGNS]


def qi(a, b, c):
    return 9 * (a + 1) + 3 * (b + 1) + (c + 1)


def mi(i, j, k):
    return 9 * i + 3 * j + k


NNZ = [(i > 0) + (j > 0) + (k > 0) for i in range(3) for j in range(3) for k in range(3)]


def slots(rows):
    first, second, sums = [], [], []
    for q, (a, b, c) in enumerate(Q):
        for x in range(rows):
            left = (a >= 0 and x == 0) or (a == 1 and x == 1)
            right = (a <= 0 and x == rows - 1) or (a == -1 and x == rows - 2)
            (first if left or right else second).append((("v", q, x), b))
    for x in range(rows):
        second.append((("w", x), 0))
    for a in SIGNS:
        for b in SIGNS:
            for s in range(2):
                for x in range(rows):
                    sums.append((("s", a, b, s, x), -b))
    table = {}
    groups = [first + sums[64:], second, sums[:64]]
    for g, group in enumerate(groups):
        for i, (key, kind) in enumerate(group):
            table[key] = (g, 2 * i, kind)
    return table, 2 * len(first)


def turn(v, shift, axis):
    shift = shift % v.shape[axis]
    return v if shift == 0 else pltpu.roll(v, shift, axis)


def lanes():
    return lax.broadcasted_iota(jnp.int32, (8, 128), 1)


def outgoing(block, lane, kind):
    return turn(block, {0: lane + 1, 1: lane, -1: lane + 2}[kind], 1)


def incoming(packed, lane, kind, b=0):
    return turn(packed, {0: 127, 1: 0, -1: 126}[kind] - lane - b, 1)


def shift_y(main, rolled_outer, b, lane):
    if b == 0:
        return main, rolled_outer
    edge = lane == (127 if b == 1 else 0)
    rolled = turn(main, -b, 1)
    return jnp.where(edge, rolled_outer, rolled), jnp.where(edge, rolled, rolled_outer)


def along(values, pass_, steps=(1, 3, 9)):
    values = list(values)
    for step in steps:
        for start in range(len(values)):
            if (start // step) % 3 == 0:
                at = (start, start + step, start + 2 * step)
                for i, new in zip(at, pass_(*[values[j] for j in at])):
                    values[i] = new
    return values


def moments(values):
    def pass_(lo, mid, hi):
        both = lo + hi
        return both + mid, hi - lo, both
    return along(values, pass_)


def dual_moments(values):
    return along(values, lambda lo, mid, hi: (mid, hi - lo, (hi - mid) + (lo - mid)))


def from_moments(values):
    return along(values, lambda m0, m1, m2: (m2 - m1, m0 - (m2 + m2), m2 + m1))


def dual_back(z0, z1, z2):
    both = z0 + z2
    return both - z1, z0, both + z1


def collide(f, solid, scale):
    m = moments(f)
    rho = m[0]
    inverse = 1.0 / rho
    jx, jy, jz = m[mi(1, 0, 0)], m[mi(0, 1, 0)], m[mi(0, 0, 1)]
    ux, uy, uz = jx * inverse, jy * inverse, jz * inverse
    xx, yy, zz = jx * ux, jy * uy, jz * uz
    third = rho * (1.0 / 3.0)
    ninth = rho * (1.0 / 9.0)
    e = [None] * 27
    e[mi(2, 0, 0)], e[mi(0, 2, 0)], e[mi(0, 0, 2)] = third + xx, third + yy, third + zz
    e[mi(1, 1, 0)], e[mi(1, 0, 1)], e[mi(0, 1, 1)] = jx * uy, jx * uz, jy * uz
    jx3, jy3, jz3 = jx * (1.0 / 3.0), jy * (1.0 / 3.0), jz * (1.0 / 3.0)
    e[mi(1, 2, 0)] = e[mi(1, 0, 2)] = jx3
    e[mi(2, 1, 0)] = e[mi(0, 1, 2)] = jy3
    e[mi(2, 0, 1)] = e[mi(0, 2, 1)] = jz3
    e[mi(2, 2, 0)] = ninth + (xx + yy) * (1.0 / 3.0)
    e[mi(2, 0, 2)] = ninth + (xx + zz) * (1.0 / 3.0)
    e[mi(0, 2, 2)] = ninth + (yy + zz) * (1.0 / 3.0)
    e[mi(2, 1, 1)] = e[mi(0, 1, 1)] * (1.0 / 3.0)
    e[mi(1, 2, 1)] = e[mi(1, 0, 1)] * (1.0 / 3.0)
    e[mi(1, 1, 2)] = e[mi(1, 1, 0)] * (1.0 / 3.0)
    e[mi(1, 2, 2)], e[mi(2, 1, 2)], e[mi(2, 2, 1)] = jx * (1.0 / 9.0), jy * (1.0 / 9.0), jz * (1.0 / 9.0)
    e[mi(2, 2, 2)] = (third + (xx + yy + zz)) * (1.0 / 9.0)
    z = []
    for i in range(27):
        if i in (0, 1, 3, 9):
            z.append(jnp.zeros_like(rho))
        else:
            z.append((m[i] if e[i] is None else m[i] - e[i]) * scale[i])
    h = from_moments(z)
    out = [jnp.where(solid, f[26 - q], f[q] - h[q]) for q in range(27)]
    return out, (ux, uy, uz)


def low_rank(z):
    def at(i, j, k):
        return z[mi(i, j, k)]

    third = 1.0 / 3.0
    top = at(2, 2, 2) * third
    d_xy, d_xz, d_yz = at(2, 2, 0) + top, at(2, 0, 2) + top, at(0, 2, 2) + top
    q_xx = at(2, 0, 0) + (at(2, 2, 0) + d_xz) * third
    q_yy = at(0, 2, 0) + (at(0, 2, 2) + d_xy) * third
    q_zz = at(0, 0, 2) + (at(2, 0, 2) + d_yz) * third
    base = at(0, 0, 0) + (q_xx + (at(0, 2, 0) + at(0, 0, 2) + at(0, 2, 2) * third)) * third
    b_x = at(1, 0, 0) + (at(1, 2, 0) + at(1, 0, 2) + at(1, 2, 2) * third) * third
    b_y = at(0, 1, 0) + (at(2, 1, 0) + at(0, 1, 2) + at(2, 1, 2) * third) * third
    b_z = at(0, 0, 1) + (at(2, 0, 1) + at(0, 2, 1) + at(2, 2, 1) * third) * third
    q_xy = at(1, 1, 0) + at(1, 1, 2) * third
    q_xz = at(1, 0, 1) + at(1, 2, 1) * third
    q_yz = at(0, 1, 1) + at(2, 1, 1) * third
    return base, (b_x, b_y, b_z), (q_xx, q_yy, q_zz, q_xy, q_xz, q_yz)


def form(coefficients, u):
    q_xx, q_yy, q_zz, q_xy, q_xz, q_yz = coefficients
    ux, uy, uz = u
    p_x = (q_xx + q_xx) * ux + q_xy * uy + q_xz * uz
    p_y = q_xy * ux + (q_yy + q_yy) * uy + q_yz * uz
    p_z = q_xz * ux + q_yz * uy + (q_zz + q_zz) * uz
    return p_x, p_y, p_z, (p_x * ux + p_y * uy + p_z * uz) * 0.5


def pull_back_parts(v, u, solid, scale):
    z = [y * s for y, s in zip(dual_moments(v), scale)]
    base, (b_x, b_y, b_z), coefficients = low_rank(z)
    p_x, p_y, p_z, quad = form(coefficients, u)
    z[0] = z[0] - (base - quad)
    z[mi(1, 0, 0)] = z[mi(1, 0, 0)] - (b_x + p_x)
    z[mi(0, 1, 0)] = z[mi(0, 1, 0)] - (b_y + p_y)
    z[mi(0, 0, 1)] = z[mi(0, 0, 1)] - (b_z + p_z)
    h = along(z, dual_back, (9, 3))
    for a in range(3):
        part = along(h[9 * a:9 * a + 9], dual_back, (1,))
        yield [jnp.where(solid, v[26 - q], v[q] - part[q - 9 * a]) for q in range(9 * a, 9 * a + 9)]


def pull_back(v, u, solid, scale):
    return sum(pull_back_parts(v, u, solid, scale), [])


def side_pull_back(groups, side, scale):
    def pass_(lo, mid, hi):
        return mid, hi - lo, (hi - mid) + (lo - mid)

    t = {a: along(values, pass_, (1, 3)) for a, values in groups.items()}
    if side in t:
        still, moved = t[0], t[side]
        first = moved if side == 1 else [-v for v in moved]
        second = [(v - m) - m for v, m in zip(moved, still)]
    else:
        moved = t[-side]
        still = [jnp.zeros_like(v) for v in moved]
        first = moved if side == -1 else [-v for v in moved]
        second = moved
    z = [y * s for y, s in zip(list(still) + list(first) + list(second), scale)]
    base, (b_x, b_y, b_z), coefficients = low_rank(z)
    z[0] = z[0] - base
    z[mi(1, 0, 0)] = z[mi(1, 0, 0)] - b_x
    z[mi(0, 1, 0)] = z[mi(0, 1, 0)] - b_y
    z[mi(0, 0, 1)] = z[mi(0, 0, 1)] - b_z
    h = [(z[i] + z[18 + i]) + z[9 + i] if side == 1 else (z[i] + z[18 + i]) - z[9 + i] for i in range(9)]
    h = along(h, dual_back, (1, 3))
    if side in groups:
        return [v - w for v, w in zip(groups[side], h)], coefficients
    return [-w for w in h], coefficients


def first_kernel(rows, rates_in, f_in, wall_in, cot_in, cot, scale_out, sums, speed, solid_out, packed,
                 raw_right,
                 rates, f, wall, sems):
    pairs = ((f_in, f), (rates_in, rates), (wall_in, wall), (cot_in, cot))
    copies = [pltpu.make_async_copy(source, target, sems.at[i]) for i, (source, target) in enumerate(pairs)]
    for copy in copies:
        copy.start()
    for copy in copies[:3]:
        copy.wait()
    for i in range(27):
        scale_out[i] = jnp.full((8, 128), rates[i] * (0.5 ** NNZ[i]), F32)
    scale = [rates[i] * (0.5 ** NNZ[i]) for i in range(27)]
    plane = lax.broadcasted_iota(jnp.int32, (8, 128), 0)
    boundary = (plane == 0) | (plane == 7)
    lane = lanes()
    table, _ = slots(rows)
    for x in range(rows):
        at = pl.ds(x, 8, stride=rows)
        solid = boundary | (wall[at, :] == 1)
        solid_out[x] = jnp.where(solid, 1.0, 0.0)
        out, u = collide([f[q, at, :] for q in range(27)], solid, scale)
        for k in range(3):
            speed[k, x] = u[k]
        for a in SIGNS:
            for b in SIGNS:
                low = turn(out[qi(a, b, -1)], -1, 0)
                high = turn(out[qi(a, b, 1)], 1, 0)
                i = 2 * (3 * (a + 1) + b + 1)
                sums[i, x] = out[qi(a, b, 0)] + (low + high)
                sums[i + 1, x] = high - low
    for copy in copies[3:]:
        copy.wait()
    raw_rows(rows, -1, cot, raw_right, 0)
    clear_end(raw_right, raw_height(-1))
    pieces = [jnp.zeros((8, 128), F32) for _ in range(3)]
    for key, (g, i, kind) in table.items():
        if key[0] == "v":
            block = cot[key[1], pl.ds(key[2], 8, stride=rows), :]
        elif key[0] == "w":
            block = solid_out[key[1]]
        else:
            block = sums[2 * (3 * (key[1] + 1) + key[2] + 1) + key[3], key[4]]
        mine = (lane == i) | (lane == i + 1)
        pieces[g] = jnp.where(mine, outgoing(block, i, kind), pieces[g])
    for g in range(3):
        packed[g] = pieces[g]


FULL = 9


def edge_rows(rows, side):
    near, far = (0, 1) if side == 1 else (rows - 1, rows - 2)
    keys = [(q, near) for q, c in enumerate(Q) if c[0] == side]
    keys += [(q, near) for q, c in enumerate(Q) if c[0] == 0]
    return keys + [(q, far) for q, c in enumerate(Q) if c[0] == side]


REDUCED = (1,)


def raw_count(side):
    return FULL if side in REDUCED else 27


def raw_at(k, gap):
    return 8 * k if k < FULL else 8 * FULL + gap + 6 * (k - FULL)


def raw_height(side):
    return raw_at(raw_count(side), 0)


def small_height(side):
    return 8 + 6 * (23 if side in REDUCED else 8)


def padded(count):
    return (count + 7) // 8 * 8


def raw_rows(rows, side, cot, message, gap):
    for k, (q, x) in enumerate(edge_rows(rows, side)[:raw_count(side)]):
        at = raw_at(k, gap)
        if k < FULL:
            message[at:at + 8] = cot[q, pl.ds(x, 8, stride=rows), :]
        else:
            message[at:at + 6] = cot[q, pl.ds(x + rows * (1 + Q[q][2]), 6, stride=rows), :]


def clear_end(message, count):
    if message.shape[0] > count:
        message[count:] = jnp.zeros((message.shape[0] - count, 128), F32)


def planes(ref, at):
    start = min(at - 1, ref.shape[0] - 8)
    return turn(ref[start:start + 8], 1 - (at - start), 0)


def sent_sums(rows):
    return [(-1, 0), (-1, 1), (0, 0), (0, rows - 1), (1, rows - 1), (1, rows - 2)]


def sums_over_y(a, x, sums, halo, table, lane):
    parts = {}
    for b in SIGNS:
        for s in range(2):
            i = 2 * (3 * (a + 1) + b + 1) + s
            g, at, kind = table["s", a, b, s, x]
            parts[b, s] = shift_y(sums[i, x], incoming(halo[g], at, kind, -b), -b, lane)
    return [(
        parts[0, 0][n] + (parts[-1, 0][n] + parts[1, 0][n]),
        parts[1, 0][n] - parts[-1, 0][n],
        parts[0, 1][n] + (parts[-1, 1][n] + parts[1, 1][n]),
    ) for n in range(2)]


def second_kernel(rows, scale_in, cot, sums, solid_in, from_left, from_right, to_left, to_right, sent, merged):
    lane = lanes()
    table, used = slots(rows)
    halo = []
    for g in range(3):
        takes_left = jnp.zeros((8, 128), jnp.bool_)
        for key, (h, i, kind) in table.items():
            if h == g and kind <= 0:
                takes_left = takes_left | (lane == i)
            if h == g and kind == -1:
                takes_left = takes_left | (lane == i + 1)
        halo.append(jnp.where(takes_left, from_left[g], from_right[g]))
        merged[g] = halo[g]

    t = {}
    for i, (a, x) in enumerate(sent_sums(rows)):
        t[a, x] = sums_over_y(a, x, sums, halo, table, lane)
        for n in range(2):
            for k in range(3):
                sent[i, 2 * k + n] = t[a, x][n][k]
    turned = {(g, c): turn(halo[g], -c, 0) for g in range(2) for c in SIGNS}
    for side, message in ((1, to_left), (-1, to_right)):
        near, far = (0, 1) if side == 1 else (rows - 1, rows - 2)
        with_raw = side == 1
        at = 8 * FULL if with_raw else 0
        items = raw_height(side) + 8 if with_raw else 8
        if with_raw:
            raw_rows(rows, side, cot, message, 8)
        clear_end(message, (raw_height(side) if with_raw else 0) + small_height(side))
        extra = []
        for n in range(2):
            row = list(t[-side, near][n])
            still, moved = t[0, near][n], t[-side, far][n]
            row += [still[0] + moved[0], moved[0] if side == -1 else -moved[0]]
            row += [still[1] + moved[1], still[2] + moved[2]]
            row.append(solid_in[near] if n == 0 else incoming(halo[table["w", near][0]], table["w", near][1], 0))
            extra.append(row)
        columns = halo[0]
        if side in REDUCED:
            groups = {0: [], side: []}
            for q, x in edge_rows(rows, side)[FULL:]:
                a, b, c = Q[q]
                main, beyond = gathered(rows, x - a, q, cot, turned, lane)
                groups[a].append(main)
                i = table["v", q, x][1]
                columns = jnp.where((lane == i) | (lane == i + 1), turn(beyond, i + 1, 1), columns)
            part, coefficients = side_pull_back(groups, side, [scale_in[i] for i in range(27)])
            extra[0] += list(part) + list(coefficients)
        for k, value in enumerate(extra[0]):
            message[items + 6 * k:items + 6 * k + 6] = value[1:7]
        for k in range(8):
            i = used + 2 * k
            columns = jnp.where((lane == i) | (lane == i + 1), turn(extra[1][k], i + 1, 1), columns)
        message[at:at + 8] = columns


def outer_rows(rows):
    return [x for x in range(-1, rows + 1) if not 0 < x < rows - 1]


def gathered(rows, x, q, cot, turned, lane, remote=None):
    table, _ = slots(rows)
    a, b, c = Q[q]
    source = x + a
    if 0 <= source < rows:
        main = turn(cot[q, pl.ds(source, 8, stride=rows), :], -c, 0)
        group, i, kind = table["v", q, source]
    else:
        load, group, i, kind = remote[q, source]
        main = load()
    outer = incoming(turned[group, c], i, kind, b)
    return shift_y(main, outer, b, lane)


def middle_kernel(rows, scale_in, cot, sums, solid_in, sent, merged, inner, known, own):
    scale = [scale_in[i] for i in range(27)]
    lane = lanes()
    table, _ = slots(rows)
    halo = [merged[g] for g in range(3)]
    t = {key: [[sent[i, 2 * k + n] for k in range(3)] for n in range(2)] for i, key in enumerate(sent_sums(rows))}
    for a in SIGNS:
        for x in range(rows):
            if (a, x) not in t:
                t[a, x] = sums_over_y(a, x, sums, halo, table, lane)
    for x in range(-1, rows + 1):
        for n in range(2):
            terms = [(a, t[a, x - a][n]) for a in SIGNS if 0 <= x - a < rows]
            along_x = jnp.zeros((8, 128), F32)
            for a, v in terms:
                if a:
                    along_x = along_x + v[0] if a == 1 else along_x - v[0]
            moments_here = [functools.reduce(jnp.add, [v[k] for _, v in terms]) for k in range(3)]
            for k, v in enumerate([moments_here[0], along_x] + moments_here[1:]):
                own[k, 2 * (x + 1) + n] = v
    turned = {(g, c): turn(merged[g], -c, 0) for g in range(2) for c in SIGNS}
    for x in range(1, rows - 1):
        v = [gathered(rows, x, q, cot, turned, lane) for q in range(27)]
        for n in range(2):
            total = [own[k, 2 * (x + 1) + n] for k in range(4)]
            inverse = 1.0 / total[0]
            if n == 0:
                wall = solid_in[x]
            else:
                g, i, kind = table["w", x]
                wall = incoming(merged[g], i, kind)
            out = pull_back([t[n] for t in v], [t * inverse for t in total[1:]], wall > 0.5, scale)
            for q in range(27):
                inner[q, 2 * (x - 1) + n] = out[q]
    for j, x in enumerate(outer_rows(rows)):
        for q in range(27):
            if 0 <= x + Q[q][0] < rows:
                known[q, 2 * j], known[q, 2 * j + 1] = gathered(rows, x, q, cot, turned, lane)


def outer_gradient(rows, side, scale, solid_in, own, merged, known, raw, gap, extra, columns_at, items_at, g1):
    lane = lanes()
    table, used = slots(rows)
    remote = {}
    def load(k, c):
        at = raw_at(k, gap)
        return turn(raw[at:at + 8], -c, 0) if k < FULL else planes(raw, at)

    for k, (q, x) in enumerate(edge_rows(rows, side)[:raw_count(side)]):
        _, i, kind = table["v", q, x]
        remote[q, x + side * rows] = (functools.partial(load, k, Q[q][2]), "far", i, kind)
    columns = extra[columns_at:columns_at + 8]
    turned = {("far", c): turn(columns, -c, 0) for c in SIGNS}
    plane = lax.broadcasted_iota(jnp.int32, (8, 128), 0)
    boundary = (plane == 0) | (plane == 7)
    near = rows - 1 if side == 1 else 0
    for j, x in enumerate(outer_rows(rows)):
        if x not in (near, near + side):
            continue
        v = []
        for q, (a, b, c) in enumerate(Q):
            if 0 <= x + a < rows:
                v.append((known[q, 2 * j], known[q, 2 * j + 1]))
            elif x == near or side not in REDUCED:
                v.append(gathered(rows, x, q, None, turned, lane, remote))
            else:
                v.append((None, incoming(columns, table["v", q, x + a - side * rows][1], 0)))
        for n in range(2):
            def got(k):
                return planes(extra, items_at + 6 * k) if n == 0 else incoming(columns, used + 2 * k, 0)

            total = [own[k, 2 * (x + 1) + n] for k in range(4)]
            if x == near:
                total = [total[0] + got(0), total[1] - got(0) if side == 1 else total[1] + got(0),
                         total[2] + got(1), total[3] + got(2)]
                if n == 0:
                    wall = solid_in[x]
                else:
                    g, i, kind = table["w", x]
                    wall = incoming(merged[g], i, kind)
            else:
                total = [total[k] + got(3 + k) for k in range(4)]
                wall = got(7)
            inverse = 1.0 / total[0]
            u = [t * inverse for t in total[1:]]
            solid = boundary | (wall > 0.5)
            if x != near and n == 0 and side in REDUCED:
                mine = [t[0] for t in v[9 * (1 - side):9 * (1 - side) + 9]]
                part, coefficients = side_pull_back({-side: mine}, side, scale)
                p_x, p_y, p_z, quad = form([m + got(17 + k) for k, m in enumerate(coefficients)], u)
                start = (p_x if side == 1 else -p_x) - quad
                along_y = {-1: start - p_y, 0: start, 1: start + p_y}
                for i in range(9):
                    b, c = i // 3 - 1, i % 3 - 1
                    rest = along_y[b] + p_z if c == 1 else along_y[b] - p_z if c == -1 else along_y[b]
                    value = (part[i] + got(8 + i)) + rest
                    g1[9 * (1 + side) + i, 2 * (j % 2)] = jnp.where(solid, mine[8 - i], value)
                continue
            g = pull_back([t[n] for t in v], u, solid, scale)
            for q in range(27):
                if 0 <= x - Q[q][0] < rows:
                    g1[q, 2 * (j % 2) + n] = g[q]


def pulled_row(rows, x, arrays, speed, solid_in, scale, lane):
    v = []
    for q, (a, b, c) in enumerate(Q):
        array, r = arrays(x + a)
        main = array[q, r]
        if b:
            main = shift_y(main, turn(array[q, r + 1], -b, 1), b, lane)[0]
        v.append(turn(main, -c, 0))
    return pull_back_parts(v, [speed[k, x] for k in range(3)], solid_in[x] > 0.5, scale)


def low_kernel(rows, scale_in, speed, solid_in, own, merged, inner, known, raw, extra, done, g1):
    scale = [scale_in[i] for i in range(27)]
    lane = lanes()
    outer_gradient(rows, -1, scale, solid_in, own, merged, known, raw, 0, extra, 0, 8, g1)

    def arrays(x):
        return (g1, 2 * (x + 1)) if x < 1 else (inner, 2 * (x - 1))

    for x in range(rows - 2):
        for a, part in enumerate(pulled_row(rows, x, arrays, speed, solid_in, scale, lane)):
            for i, value in enumerate(part):
                done[9 * a + i, x] = value


def last_kernel(rows, scale_in, speed, solid_in, own, merged, inner, known, done, from_high, out_hbm, high, out, sems):
    scale = [scale_in[i] for i in range(27)]
    lane = lanes()
    outer_gradient(rows, 1, scale, solid_in, own, merged, known, from_high, 8, from_high, 8 * FULL, raw_height(1) + 8, high)

    def arrays(x):
        return (inner, 2 * (x - 1)) if x < rows - 1 else (high, 2 * (x - rows + 1))

    late = {x: pulled_row(rows, x, arrays, speed, solid_in, scale, lane) for x in range(rows - 2, rows)}
    copies = []
    for a in range(3):
        for x in range(rows):
            part = next(late[x]) if x in late else [done[9 * a + i, x] for i in range(9)]
            for i, value in enumerate(part):
                out[9 * a + i, pl.ds(x, 8, stride=rows), :] = value
        part = pl.ds(9 * a, 9)
        copies.append(pltpu.make_async_copy(out.at[part], out_hbm.at[part], sems.at[a]))
        copies[a].start()
    for copy in copies:
        copy.wait()


def call(kernel, name, out_shapes, scratch, operands, space=pltpu.VMEM, work=0, out_space=pltpu.VMEM):
    return pl.pallas_call(
        kernel,
        out_shape=[jax.ShapeDtypeStruct(s, F32) for s in out_shapes],
        in_specs=[pl.BlockSpec(memory_space=space)] * len(operands),
        out_specs=[pl.BlockSpec(memory_space=out_space)] * len(out_shapes),
        scratch_shapes=scratch,
        compiler_params=pltpu.CompilerParams(vmem_limit_bytes=32 * 1024 * 1024),
        cost_estimate=pl.CostEstimate(flops=work, bytes_accessed=0 if work else 0, transcendentals=0) if work else None,
        name=name,
    )(*operands)


def ring(block, axis, step):
    size = lax.axis_size(axis)
    return lax.ppermute(block, axis, [(i, (i + step) % size) for i in range(size)])


def swap(block, axis, first):
    size = lax.axis_size(axis)
    route = []
    for i in range(first, size + first, 2):
        route += [(i % size, (i + 1) % size), ((i + 1) % size, i % size)]
    return lax.ppermute(block, axis, route)


def shards(checkpoint, rates, wall_mask, cotangent):
    planes, rows, width = checkpoint.shape[1:]
    f = checkpoint.reshape(27, planes * rows, width)
    cot = cotangent.reshape(27, planes * rows, width)
    wall = wall_mask.reshape(planes * rows, width)
    tile = (planes, width)
    lattice = (27, planes * rows, width)
    cot, scale, sums, speed, solid, packed, raw_right = call(
        functools.partial(first_kernel, rows), "collide",
        [lattice, (27,) + tile, (18, rows) + tile, (3, rows) + tile, (rows,) + tile, (3,) + tile,
         (padded(raw_height(-1)), width)],
        [pltpu.SMEM((27,), F32), pltpu.VMEM(lattice, F32), pltpu.VMEM(lattice[1:], jnp.int32),
         pltpu.SemaphoreType.DMA((4,))],
        tuple(pltpu.with_memory_space_constraint(v, pltpu.HBM) for v in (rates, f, wall, cot)), pltpu.HBM)
    raw_low = ring(raw_right, "gx", 1)
    across, inside = swap(packed, "gy", 1), swap(packed, "gy", 0)
    odd = lax.axis_index("gy") % 2 == 1
    from_left = jnp.where(odd, inside, across)
    from_right = jnp.where(odd, across, inside)
    to_left, small_right, sent, merged = call(
        functools.partial(second_kernel, rows), "pack",
        [(padded(raw_height(1) + small_height(1)), width), (padded(small_height(-1)), width), (6, 6) + tile, (3,) + tile], [],
        (scale, cot, sums, solid, from_left, from_right))
    small_low = ring(small_right, "gx", 1)
    from_high = ring(to_left, "gx", -1)
    inner, known, own = call(
        functools.partial(middle_kernel, rows), "inner_rows",
        [(27, 2 * rows - 4) + tile, (27, 8) + tile, (4, 2 * rows + 4) + tile], [],
        (scale, cot, sums, solid, sent, merged))
    (done,) = call(
        functools.partial(low_kernel, rows), "low_rows",
        [(27, rows - 2) + tile], [pltpu.VMEM((27, 4) + tile, F32)],
        (scale, speed, solid, own, merged, inner, known, raw_low, small_low), work=2000000000)
    (out,) = call(
        functools.partial(last_kernel, rows), "gradient",
        [lattice],
        [pltpu.VMEM((27, 4) + tile, F32), pltpu.VMEM(lattice, F32), pltpu.SemaphoreType.DMA((3,))],
        (scale, speed, solid, own, merged, inner, known, done, from_high), out_space=pltpu.HBM)
    return out.reshape(checkpoint.shape)


def solution(mesh):
    in_specs = (P(None, None, "gx", "gy"), P(), P(None, "gx", "gy"), P(None, None, "gx", "gy"))
    out_specs = P(None, None, "gx", "gy")
    return jax.shard_map(shards, mesh=mesh, in_specs=in_specs, out_specs=out_specs, check_vma=False)
```

```python
import functools
import jax
import jax.numpy as jnp
from jax import lax
from jax.experimental import pallas as pl
from jax.experimental.pallas import tpu as pltpu
from jax.sharding import PartitionSpec as P

F32 = jnp.float32
SIGNS = (-1, 0, 1)
Q = [(a, b, c) for a in SIGNS for b in SIGNS for c in SIGNS]


def qi(a, b, c):
    return 9 * (a + 1) + 3 * (b + 1) + (c + 1)


def mi(i, j, k):
    return 9 * i + 3 * j + k


NNZ = [(i > 0) + (j > 0) + (k > 0) for i in range(3) for j in range(3) for k in range(3)]


def layout(rows):
    quads, singles = [[], [], []], [[], [], []]
    for a in SIGNS:
        for c in SIGNS:
            for x in range(rows):
                left = (a >= 0 and x == 0) or (a == 1 and x == 1)
                right = (a <= 0 and x == rows - 1) or (a == -1 and x == rows - 2)
                g = 0 if left or right else 1
                quads[g].append((("v", qi(a, -1, c), x), ("v", qi(a, 1, c), x)))
                singles[g].append(("v", qi(a, 0, c), x))
    used = 4 * len(quads[0]) + 2 * len(singles[0])
    singles[1] += [("w", x) for x in range(rows)]
    for a in SIGNS:
        for s in range(2):
            for x in range(rows):
                quads[2].append((("s", a, 1, s, x), ("s", a, -1, s, x)))
                singles[2].append(("s", a, 0, s, x))
    room = 64 - 2 * len(quads[2])
    singles[0] += singles[2][room:]
    singles[2] = singles[2][:room]
    return quads, singles, used


def slots(rows):
    quads, singles, used = layout(rows)
    table = {}
    for g in range(3):
        for n, (low, high) in enumerate(quads[g]):
            table[low], table[high] = (g, 4 * n, -1), (g, 4 * n + 2, 1)
        for n, key in enumerate(singles[g]):
            table[key] = (g, 4 * len(quads[g]) + 2 * n, 0)
    return table, used


def turn(v, shift, axis):
    shift = shift % v.shape[axis]
    return v if shift == 0 else pltpu.roll(v, shift, axis)


def lanes():
    return lax.broadcasted_iota(jnp.int32, (8, 128), 1)


def incoming(packed, lane, kind, b=0):
    return turn(packed, {0: 127, 1: 0, -1: 126}[kind] - lane - b, 1)


def shift_y(main, rolled_outer, b, lane):
    if b == 0:
        return main, rolled_outer
    edge = lane == (127 if b == 1 else 0)
    rolled = turn(main, -b, 1)
    return jnp.where(edge, rolled_outer, rolled), jnp.where(edge, rolled, rolled_outer)


def along(values, pass_, steps=(1, 3, 9)):
    values = list(values)
    for step in steps:
        for start in range(len(values)):
            if (start // step) % 3 == 0:
                at = (start, start + step, start + 2 * step)
                for i, new in zip(at, pass_(*[values[j] for j in at])):
                    values[i] = new
    return values


def moments(values):
    def pass_(lo, mid, hi):
        both = lo + hi
        return both + mid, hi - lo, both
    return along(values, pass_)


def dual_moments(values):
    return along(values, lambda lo, mid, hi: (mid, hi - lo, (hi - mid) + (lo - mid)))


def from_moments(values):
    return along(values, lambda m0, m1, m2: (m2 - m1, m0 - (m2 + m2), m2 + m1))


def dual_back(z0, z1, z2):
    both = z0 + z2
    return both - z1, z0, both + z1


def collide(f, solid, scale):
    m = moments(f)
    rho = m[0]
    inverse = 1.0 / rho
    jx, jy, jz = m[mi(1, 0, 0)], m[mi(0, 1, 0)], m[mi(0, 0, 1)]
    ux, uy, uz = jx * inverse, jy * inverse, jz * inverse
    xx, yy, zz = jx * ux, jy * uy, jz * uz
    third = rho * (1.0 / 3.0)
    ninth = rho * (1.0 / 9.0)
    e = [None] * 27
    e[mi(2, 0, 0)], e[mi(0, 2, 0)], e[mi(0, 0, 2)] = third + xx, third + yy, third + zz
    e[mi(1, 1, 0)], e[mi(1, 0, 1)], e[mi(0, 1, 1)] = jx * uy, jx * uz, jy * uz
    jx3, jy3, jz3 = jx * (1.0 / 3.0), jy * (1.0 / 3.0), jz * (1.0 / 3.0)
    e[mi(1, 2, 0)] = e[mi(1, 0, 2)] = jx3
    e[mi(2, 1, 0)] = e[mi(0, 1, 2)] = jy3
    e[mi(2, 0, 1)] = e[mi(0, 2, 1)] = jz3
    e[mi(2, 2, 0)] = ninth + (xx + yy) * (1.0 / 3.0)
    e[mi(2, 0, 2)] = ninth + (xx + zz) * (1.0 / 3.0)
    e[mi(0, 2, 2)] = ninth + (yy + zz) * (1.0 / 3.0)
    e[mi(2, 1, 1)] = e[mi(0, 1, 1)] * (1.0 / 3.0)
    e[mi(1, 2, 1)] = e[mi(1, 0, 1)] * (1.0 / 3.0)
    e[mi(1, 1, 2)] = e[mi(1, 1, 0)] * (1.0 / 3.0)
    e[mi(1, 2, 2)], e[mi(2, 1, 2)], e[mi(2, 2, 1)] = jx * (1.0 / 9.0), jy * (1.0 / 9.0), jz * (1.0 / 9.0)
    e[mi(2, 2, 2)] = (third + (xx + yy + zz)) * (1.0 / 9.0)
    z = []
    for i in range(27):
        if i in (0, 1, 3, 9):
            z.append(jnp.zeros_like(rho))
        else:
            z.append((m[i] if e[i] is None else m[i] - e[i]) * scale[i])
    h = from_moments(z)
    out = [jnp.where(solid, f[26 - q], f[q] - h[q]) for q in range(27)]
    return out, (ux, uy, uz)


def low_rank(z):
    def at(i, j, k):
        return z[mi(i, j, k)]

    third = 1.0 / 3.0
    top = at(2, 2, 2) * third
    d_xy, d_xz, d_yz = at(2, 2, 0) + top, at(2, 0, 2) + top, at(0, 2, 2) + top
    q_xx = at(2, 0, 0) + (at(2, 2, 0) + d_xz) * third
    q_yy = at(0, 2, 0) + (at(0, 2, 2) + d_xy) * third
    q_zz = at(0, 0, 2) + (at(2, 0, 2) + d_yz) * third
    base = at(0, 0, 0) + (q_xx + (at(0, 2, 0) + at(0, 0, 2) + at(0, 2, 2) * third)) * third
    b_x = at(1, 0, 0) + (at(1, 2, 0) + at(1, 0, 2) + at(1, 2, 2) * third) * third
    b_y = at(0, 1, 0) + (at(2, 1, 0) + at(0, 1, 2) + at(2, 1, 2) * third) * third
    b_z = at(0, 0, 1) + (at(2, 0, 1) + at(0, 2, 1) + at(2, 2, 1) * third) * third
    q_xy = at(1, 1, 0) + at(1, 1, 2) * third
    q_xz = at(1, 0, 1) + at(1, 2, 1) * third
    q_yz = at(0, 1, 1) + at(2, 1, 1) * third
    return base, (b_x, b_y, b_z), (q_xx, q_yy, q_zz, q_xy, q_xz, q_yz)


def form(coefficients, u):
    q_xx, q_yy, q_zz, q_xy, q_xz, q_yz = coefficients
    ux, uy, uz = u
    p_x = (q_xx + q_xx) * ux + q_xy * uy + q_xz * uz
    p_y = q_xy * ux + (q_yy + q_yy) * uy + q_yz * uz
    p_z = q_xz * ux + q_yz * uy + (q_zz + q_zz) * uz
    return p_x, p_y, p_z, (p_x * ux + p_y * uy + p_z * uz) * 0.5


def pull_back_parts(v, u, solid, scale):
    z = [y * s for y, s in zip(dual_moments(v), scale)]
    base, (b_x, b_y, b_z), coefficients = low_rank(z)
    p_x, p_y, p_z, quad = form(coefficients, u)
    z[0] = z[0] - (base - quad)
    z[mi(1, 0, 0)] = z[mi(1, 0, 0)] - (b_x + p_x)
    z[mi(0, 1, 0)] = z[mi(0, 1, 0)] - (b_y + p_y)
    z[mi(0, 0, 1)] = z[mi(0, 0, 1)] - (b_z + p_z)
    h = along(z, dual_back, (9, 3))
    for a in range(3):
        part = along(h[9 * a:9 * a + 9], dual_back, (1,))
        yield [jnp.where(solid, v[26 - q], v[q] - part[q - 9 * a]) for q in range(9 * a, 9 * a + 9)]


def pull_back(v, u, solid, scale):
    return sum(pull_back_parts(v, u, solid, scale), [])


def side_pull_back(groups, side, scale):
    def pass_(lo, mid, hi):
        return mid, hi - lo, (hi - mid) + (lo - mid)

    t = {a: along(values, pass_, (1, 3)) for a, values in groups.items()}
    if side in t:
        still, moved = t[0], t[side]
        first = moved if side == 1 else [-v for v in moved]
        second = [(v - m) - m for v, m in zip(moved, still)]
    else:
        moved = t[-side]
        still = [jnp.zeros_like(v) for v in moved]
        first = moved if side == -1 else [-v for v in moved]
        second = moved
    z = [y * s for y, s in zip(list(still) + list(first) + list(second), scale)]
    base, (b_x, b_y, b_z), coefficients = low_rank(z)
    z[0] = z[0] - base
    z[mi(1, 0, 0)] = z[mi(1, 0, 0)] - b_x
    z[mi(0, 1, 0)] = z[mi(0, 1, 0)] - b_y
    z[mi(0, 0, 1)] = z[mi(0, 0, 1)] - b_z
    h = [(z[i] + z[18 + i]) + z[9 + i] if side == 1 else (z[i] + z[18 + i]) - z[9 + i] for i in range(9)]
    h = along(h, dual_back, (1, 3))
    if side in groups:
        return [v - w for v, w in zip(groups[side], h)], coefficients
    return [-w for w in h], coefficients


def first_kernel(rows, rates_in, f_in, wall_in, cot_in, cot, scale_out, sums, speed, solid_out, packed,
                 raw_right,
                 rates, f, wall, sems):
    pairs = ((f_in, f), (rates_in, rates), (wall_in, wall), (cot_in, cot))
    copies = [pltpu.make_async_copy(source, target, sems.at[i]) for i, (source, target) in enumerate(pairs)]
    for copy in copies:
        copy.start()
    for copy in copies[:3]:
        copy.wait()
    for i in range(27):
        scale_out[i] = jnp.full((8, 128), rates[i] * (0.5 ** NNZ[i]), F32)
    scale = [rates[i] * (0.5 ** NNZ[i]) for i in range(27)]
    plane = lax.broadcasted_iota(jnp.int32, (8, 128), 0)
    boundary = (plane == 0) | (plane == 7)
    lane = lanes()
    table, _ = slots(rows)
    for x in range(rows):
        at = pl.ds(x, 8, stride=rows)
        solid = boundary | (wall[at, :] == 1)
        solid_out[x] = jnp.where(solid, 1.0, 0.0)
        out, u = collide([f[q, at, :] for q in range(27)], solid, scale)
        for k in range(3):
            speed[k, x] = u[k]
        for a in SIGNS:
            for b in SIGNS:
                low = turn(out[qi(a, b, -1)], -1, 0)
                high = turn(out[qi(a, b, 1)], 1, 0)
                i = 2 * (3 * (a + 1) + b + 1)
                sums[i, x] = out[qi(a, b, 0)] + (low + high)
                sums[i + 1, x] = high - low
    for copy in copies[3:]:
        copy.wait()
    raw_rows(rows, -1, cot, raw_right, 0)
    clear_end(raw_right, raw_height(-1))
    def block(key):
        if key[0] == "v":
            return cot[key[1], pl.ds(key[2], 8, stride=rows), :]
        if key[0] == "w":
            return solid_out[key[1]]
        return sums[2 * (3 * (key[1] + 1) + key[2] + 1) + key[3], key[4]]

    quads, singles, _ = layout(rows)
    by_two, by_four = lane >> 1, lane >> 2
    high_lanes = lane >= 64
    for g in range(3):
        piece = jnp.zeros((8, 128), F32)
        for n, (low, high) in enumerate(quads[g]):
            both = jnp.where(high_lanes, block(low), block(high))
            piece = jnp.where(by_four == n, turn(both, 4 * n + 2, 1), piece)
        for n, key in enumerate(singles[g]):
            i = 4 * len(quads[g]) + 2 * n
            piece = jnp.where(by_two == i // 2, turn(block(key), i + 1, 1), piece)
        packed[g] = piece


FULL = 9


def edge_rows(rows, side):
    near, far = (0, 1) if side == 1 else (rows - 1, rows - 2)
    keys = [(q, near) for q, c in enumerate(Q) if c[0] == side]
    keys += [(q, near) for q, c in enumerate(Q) if c[0] == 0]
    return keys + [(q, far) for q, c in enumerate(Q) if c[0] == side]


REDUCED = (1,)


def raw_count(side):
    return FULL if side in REDUCED else 27


def raw_at(k, gap):
    return 8 * k if k < FULL else 8 * FULL + gap + 6 * (k - FULL)


def raw_height(side):
    return raw_at(raw_count(side), 0)


def small_height(side):
    return 8 + 6 * (23 if side in REDUCED else 8)


def padded(count):
    return (count + 7) // 8 * 8


def raw_rows(rows, side, cot, message, gap):
    for k, (q, x) in enumerate(edge_rows(rows, side)[:raw_count(side)]):
        at = raw_at(k, gap)
        if k < FULL:
            message[at:at + 8] = cot[q, pl.ds(x, 8, stride=rows), :]
        else:
            message[at:at + 6] = cot[q, pl.ds(x + rows * (1 + Q[q][2]), 6, stride=rows), :]


def clear_end(message, count):
    if message.shape[0] > count:
        message[count:] = jnp.zeros((message.shape[0] - count, 128), F32)


def planes(ref, at):
    start = min(at - 1, ref.shape[0] - 8)
    return turn(ref[start:start + 8], 1 - (at - start), 0)


def sent_sums(rows):
    return [(-1, 0), (-1, 1), (0, 0), (0, rows - 1), (1, rows - 1), (1, rows - 2)]


def sums_over_y(a, x, sums, halo, table, lane):
    parts = {}
    for b in SIGNS:
        for s in range(2):
            i = 2 * (3 * (a + 1) + b + 1) + s
            g, at, kind = table["s", a, b, s, x]
            parts[b, s] = shift_y(sums[i, x], incoming(halo[g], at, kind, -b), -b, lane)
    return [(
        parts[0, 0][n] + (parts[-1, 0][n] + parts[1, 0][n]),
        parts[1, 0][n] - parts[-1, 0][n],
        parts[0, 1][n] + (parts[-1, 1][n] + parts[1, 1][n]),
    ) for n in range(2)]


def second_kernel(rows, scale_in, cot, sums, solid_in, from_left, from_right, to_left, to_right, sent, merged):
    lane = lanes()
    table, used = slots(rows)
    by_two = lane >> 1
    halo = []
    for g in range(3):
        end = 4 * len(layout(rows)[0][g])
        takes_left = ((lane < end) & ((lane & 2) == 0)) | ((lane >= end) & ((lane & 1) == 0))
        halo.append(jnp.where(takes_left, from_left[g], from_right[g]))
        merged[g] = halo[g]

    t = {}
    for i, (a, x) in enumerate(sent_sums(rows)):
        t[a, x] = sums_over_y(a, x, sums, halo, table, lane)
        for n in range(2):
            for k in range(3):
                sent[i, 2 * k + n] = t[a, x][n][k]
    turned = {(g, c): turn(halo[g], -c, 0) for g in range(2) for c in SIGNS}
    for side, message in ((1, to_left), (-1, to_right)):
        near, far = (0, 1) if side == 1 else (rows - 1, rows - 2)
        with_raw = side == 1
        at = 8 * FULL if with_raw else 0
        items = raw_height(side) + 8 if with_raw else 8
        if with_raw:
            raw_rows(rows, side, cot, message, 8)
        clear_end(message, (raw_height(side) if with_raw else 0) + small_height(side))
        extra = []
        for n in range(2):
            row = list(t[-side, near][n])
            still, moved = t[0, near][n], t[-side, far][n]
            row += [still[0] + moved[0], moved[0] if side == -1 else -moved[0]]
            row += [still[1] + moved[1], still[2] + moved[2]]
            row.append(solid_in[near] if n == 0 else incoming(halo[table["w", near][0]], table["w", near][1], 0))
            extra.append(row)
        columns = halo[0]
        if side in REDUCED:
            groups = {0: [], side: []}
            for q, x in edge_rows(rows, side)[FULL:]:
                a, b, c = Q[q]
                main, beyond = gathered(rows, x - a, q, cot, turned, lane)
                groups[a].append(main)
                i = table["v", q, x][1]
                columns = jnp.where(by_two == i // 2, turn(beyond, i + 1, 1), columns)
            part, coefficients = side_pull_back(groups, side, [scale_in[i] for i in range(27)])
            extra[0] += list(part) + list(coefficients)
        for k, value in enumerate(extra[0]):
            message[items + 6 * k:items + 6 * k + 6] = value[1:7]
        for k in range(8):
            i = used + 2 * k
            columns = jnp.where(by_two == i // 2, turn(extra[1][k], i + 1, 1), columns)
        message[at:at + 8] = columns


def outer_rows(rows):
    return [x for x in range(-1, rows + 1) if not 0 < x < rows - 1]


def gathered(rows, x, q, cot, turned, lane, remote=None):
    table, _ = slots(rows)
    a, b, c = Q[q]
    source = x + a
    if 0 <= source < rows:
        main = turn(cot[q, pl.ds(source, 8, stride=rows), :], -c, 0)
        group, i, kind = table["v", q, source]
    else:
        load, group, i, kind = remote[q, source]
        main = load()
    outer = incoming(turned[group, c], i, kind, b)
    return shift_y(main, outer, b, lane)


def middle_kernel(rows, scale_in, cot, sums, solid_in, sent, merged, inner, known, own):
    scale = [scale_in[i] for i in range(27)]
    lane = lanes()
    table, _ = slots(rows)
    halo = [merged[g] for g in range(3)]
    t = {key: [[sent[i, 2 * k + n] for k in range(3)] for n in range(2)] for i, key in enumerate(sent_sums(rows))}
    for a in SIGNS:
        for x in range(rows):
            if (a, x) not in t:
                t[a, x] = sums_over_y(a, x, sums, halo, table, lane)
    for x in range(-1, rows + 1):
        for n in range(2):
            terms = [(a, t[a, x - a][n]) for a in SIGNS if 0 <= x - a < rows]
            along_x = jnp.zeros((8, 128), F32)
            for a, v in terms:
                if a:
                    along_x = along_x + v[0] if a == 1 else along_x - v[0]
            moments_here = [functools.reduce(jnp.add, [v[k] for _, v in terms]) for k in range(3)]
            for k, v in enumerate([moments_here[0], along_x] + moments_here[1:]):
                own[k, 2 * (x + 1) + n] = v
    turned = {(g, c): turn(merged[g], -c, 0) for g in range(2) for c in SIGNS}
    for x in range(1, rows - 1):
        v = [gathered(rows, x, q, cot, turned, lane) for q in range(27)]
        for n in range(2):
            total = [own[k, 2 * (x + 1) + n] for k in range(4)]
            inverse = 1.0 / total[0]
            if n == 0:
                wall = solid_in[x]
            else:
                g, i, kind = table["w", x]
                wall = incoming(merged[g], i, kind)
            out = pull_back([t[n] for t in v], [t * inverse for t in total[1:]], wall > 0.5, scale)
            for q in range(27):
                inner[q, 2 * (x - 1) + n] = out[q]
    for j, x in enumerate(outer_rows(rows)):
        for q in range(27):
            if 0 <= x + Q[q][0] < rows:
                known[q, 2 * j], known[q, 2 * j + 1] = gathered(rows, x, q, cot, turned, lane)


def outer_gradient(rows, side, scale, solid_in, own, merged, known, raw, gap, extra, columns_at, items_at, g1):
    lane = lanes()
    table, used = slots(rows)
    remote = {}
    def load(k, c):
        at = raw_at(k, gap)
        return turn(raw[at:at + 8], -c, 0) if k < FULL else planes(raw, at)

    for k, (q, x) in enumerate(edge_rows(rows, side)[:raw_count(side)]):
        _, i, kind = table["v", q, x]
        remote[q, x + side * rows] = (functools.partial(load, k, Q[q][2]), "far", i, kind)
    columns = extra[columns_at:columns_at + 8]
    turned = {("far", c): turn(columns, -c, 0) for c in SIGNS}
    plane = lax.broadcasted_iota(jnp.int32, (8, 128), 0)
    boundary = (plane == 0) | (plane == 7)
    near = rows - 1 if side == 1 else 0
    for j, x in enumerate(outer_rows(rows)):
        if x not in (near, near + side):
            continue
        v = []
        for q, (a, b, c) in enumerate(Q):
            if 0 <= x + a < rows:
                v.append((known[q, 2 * j], known[q, 2 * j + 1]))
            elif x == near or side not in REDUCED:
                v.append(gathered(rows, x, q, None, turned, lane, remote))
            else:
                v.append((None, incoming(columns, table["v", q, x + a - side * rows][1], 0)))
        for n in range(2):
            def got(k):
                return planes(extra, items_at + 6 * k) if n == 0 else incoming(columns, used + 2 * k, 0)

            total = [own[k, 2 * (x + 1) + n] for k in range(4)]
            if x == near:
                total = [total[0] + got(0), total[1] - got(0) if side == 1 else total[1] + got(0),
                         total[2] + got(1), total[3] + got(2)]
                if n == 0:
                    wall = solid_in[x]
                else:
                    g, i, kind = table["w", x]
                    wall = incoming(merged[g], i, kind)
            else:
                total = [total[k] + got(3 + k) for k in range(4)]
                wall = got(7)
            inverse = 1.0 / total[0]
            u = [t * inverse for t in total[1:]]
            solid = boundary | (wall > 0.5)
            if x != near and n == 0 and side in REDUCED:
                mine = [t[0] for t in v[9 * (1 - side):9 * (1 - side) + 9]]
                part, coefficients = side_pull_back({-side: mine}, side, scale)
                p_x, p_y, p_z, quad = form([m + got(17 + k) for k, m in enumerate(coefficients)], u)
                start = (p_x if side == 1 else -p_x) - quad
                along_y = {-1: start - p_y, 0: start, 1: start + p_y}
                for i in range(9):
                    b, c = i // 3 - 1, i % 3 - 1
                    rest = along_y[b] + p_z if c == 1 else along_y[b] - p_z if c == -1 else along_y[b]
                    value = (part[i] + got(8 + i)) + rest
                    g1[9 * (1 + side) + i, 2 * (j % 2)] = jnp.where(solid, mine[8 - i], value)
                continue
            g = pull_back([t[n] for t in v], u, solid, scale)
            for q in range(27):
                if 0 <= x - Q[q][0] < rows:
                    g1[q, 2 * (j % 2) + n] = g[q]


def pulled_row(rows, x, arrays, speed, solid_in, scale, lane):
    v = []
    for q, (a, b, c) in enumerate(Q):
        array, r = arrays(x + a)
        main = array[q, r]
        if b:
            main = shift_y(main, turn(array[q, r + 1], -b, 1), b, lane)[0]
        v.append(turn(main, -c, 0))
    return pull_back_parts(v, [speed[k, x] for k in range(3)], solid_in[x] > 0.5, scale)


def low_kernel(rows, scale_in, speed, solid_in, own, merged, inner, known, raw, extra, done, g1):
    scale = [scale_in[i] for i in range(27)]
    lane = lanes()
    outer_gradient(rows, -1, scale, solid_in, own, merged, known, raw, 0, extra, 0, 8, g1)

    def arrays(x):
        return (g1, 2 * (x + 1)) if x < 1 else (inner, 2 * (x - 1))

    for x in range(rows - 2):
        for a, part in enumerate(pulled_row(rows, x, arrays, speed, solid_in, scale, lane)):
            for i, value in enumerate(part):
                done[9 * a + i, x] = value


def last_kernel(rows, scale_in, speed, solid_in, own, merged, inner, known, done, from_high, out_hbm, high, out, sems):
    scale = [scale_in[i] for i in range(27)]
    lane = lanes()
    outer_gradient(rows, 1, scale, solid_in, own, merged, known, from_high, 8, from_high, 8 * FULL, raw_height(1) + 8, high)

    def arrays(x):
        return (inner, 2 * (x - 1)) if x < rows - 1 else (high, 2 * (x - rows + 1))

    late = {x: pulled_row(rows, x, arrays, speed, solid_in, scale, lane) for x in range(rows - 2, rows)}
    copies = []
    for a in range(3):
        for x in range(rows):
            part = next(late[x]) if x in late else [done[9 * a + i, x] for i in range(9)]
            for i, value in enumerate(part):
                out[9 * a + i, pl.ds(x, 8, stride=rows), :] = value
        part = pl.ds(9 * a, 9)
        copies.append(pltpu.make_async_copy(out.at[part], out_hbm.at[part], sems.at[a]))
        copies[a].start()
    for copy in copies:
        copy.wait()


def call(kernel, name, out_shapes, scratch, operands, space=pltpu.VMEM, work=0, out_space=pltpu.VMEM):
    return pl.pallas_call(
        kernel,
        out_shape=[jax.ShapeDtypeStruct(s, F32) for s in out_shapes],
        in_specs=[pl.BlockSpec(memory_space=space)] * len(operands),
        out_specs=[pl.BlockSpec(memory_space=out_space)] * len(out_shapes),
        scratch_shapes=scratch,
        compiler_params=pltpu.CompilerParams(vmem_limit_bytes=32 * 1024 * 1024),
        cost_estimate=pl.CostEstimate(flops=work, bytes_accessed=0 if work else 0, transcendentals=0) if work else None,
        name=name,
    )(*operands)


def ring(block, axis, step):
    size = lax.axis_size(axis)
    return lax.ppermute(block, axis, [(i, (i + step) % size) for i in range(size)])


def swap(block, axis, first):
    size = lax.axis_size(axis)
    route = []
    for i in range(first, size + first, 2):
        route += [(i % size, (i + 1) % size), ((i + 1) % size, i % size)]
    return lax.ppermute(block, axis, route)


def shards(checkpoint, rates, wall_mask, cotangent):
    planes, rows, width = checkpoint.shape[1:]
    f = checkpoint.reshape(27, planes * rows, width)
    cot = cotangent.reshape(27, planes * rows, width)
    wall = wall_mask.reshape(planes * rows, width)
    tile = (planes, width)
    lattice = (27, planes * rows, width)
    cot, scale, sums, speed, solid, packed, raw_right = call(
        functools.partial(first_kernel, rows), "collide",
        [lattice, (27,) + tile, (18, rows) + tile, (3, rows) + tile, (rows,) + tile, (3,) + tile,
         (padded(raw_height(-1)), width)],
        [pltpu.SMEM((27,), F32), pltpu.VMEM(lattice, F32), pltpu.VMEM(lattice[1:], jnp.int32),
         pltpu.SemaphoreType.DMA((4,))],
        tuple(pltpu.with_memory_space_constraint(v, pltpu.HBM) for v in (rates, f, wall, cot)), pltpu.HBM)
    raw_low = ring(raw_right, "gx", 1)
    across, inside = swap(packed, "gy", 1), swap(packed, "gy", 0)
    odd = lax.axis_index("gy") % 2 == 1
    from_left = jnp.where(odd, inside, across)
    from_right = jnp.where(odd, across, inside)
    to_left, small_right, sent, merged = call(
        functools.partial(second_kernel, rows), "pack",
        [(padded(raw_height(1) + small_height(1)), width), (padded(small_height(-1)), width), (6, 6) + tile, (3,) + tile], [],
        (scale, cot, sums, solid, from_left, from_right))
    small_low = ring(small_right, "gx", 1)
    from_high = ring(to_left, "gx", -1)
    inner, known, own = call(
        functools.partial(middle_kernel, rows), "inner_rows",
        [(27, 2 * rows - 4) + tile, (27, 8) + tile, (4, 2 * rows + 4) + tile], [],
        (scale, cot, sums, solid, sent, merged))
    (done,) = call(
        functools.partial(low_kernel, rows), "low_rows",
        [(27, rows - 2) + tile], [pltpu.VMEM((27, 4) + tile, F32)],
        (scale, speed, solid, own, merged, inner, known, raw_low, small_low), work=2000000000)
    (out,) = call(
        functools.partial(last_kernel, rows), "gradient",
        [lattice],
        [pltpu.VMEM((27, 4) + tile, F32), pltpu.VMEM(lattice, F32), pltpu.SemaphoreType.DMA((3,))],
        (scale, speed, solid, own, merged, inner, known, done, from_high), out_space=pltpu.HBM)
    return out.reshape(checkpoint.shape)


def solution(mesh):
    in_specs = (P(None, None, "gx", "gy"), P(), P(None, "gx", "gy"), P(None, None, "gx", "gy"))
    out_specs = P(None, None, "gx", "gy")
    return jax.shard_map(shards, mesh=mesh, in_specs=in_specs, out_specs=out_specs, check_vma=False)
```

```python
import functools
import jax
import jax.numpy as jnp
from jax import lax
from jax.experimental import pallas as pl
from jax.experimental.pallas import tpu as pltpu
from jax.sharding import PartitionSpec as P

F32 = jnp.float32
SIGNS = (-1, 0, 1)
Q = [(a, b, c) for a in SIGNS for b in SIGNS for c in SIGNS]


def qi(a, b, c):
    return 9 * (a + 1) + 3 * (b + 1) + (c + 1)


def mi(i, j, k):
    return 9 * i + 3 * j + k


NNZ = [(i > 0) + (j > 0) + (k > 0) for i in range(3) for j in range(3) for k in range(3)]


def layout(rows):
    quads, singles = [[], [], []], [[], [], []]
    for a in SIGNS:
        for c in SIGNS:
            for x in range(rows):
                left = (a >= 0 and x == 0) or (a == 1 and x == 1)
                right = (a <= 0 and x == rows - 1) or (a == -1 and x == rows - 2)
                g = 0 if left or right else 1
                quads[g].append((("v", qi(a, -1, c), x), ("v", qi(a, 1, c), x)))
                singles[g].append(("v", qi(a, 0, c), x))
    used = 4 * len(quads[0]) + 2 * len(singles[0])
    singles[1] += [("w", x) for x in range(rows)]
    for a in SIGNS:
        for s in range(2):
            for x in range(rows):
                quads[2].append((("s", a, 1, s, x), ("s", a, -1, s, x)))
                singles[2].append(("s", a, 0, s, x))
    room = 64 - 2 * len(quads[2])
    singles[0] += singles[2][room:]
    singles[2] = singles[2][:room]
    return quads, singles, used


def slots(rows):
    quads, singles, used = layout(rows)
    table = {}
    for g in range(3):
        for n, (low, high) in enumerate(quads[g]):
            table[low], table[high] = (g, 4 * n, -1), (g, 4 * n + 2, 1)
        for n, key in enumerate(singles[g]):
            table[key] = (g, 4 * len(quads[g]) + 2 * n, 0)
    return table, used


def turn(v, shift, axis):
    shift = shift % v.shape[axis]
    return v if shift == 0 else pltpu.roll(v, shift, axis)


def lanes():
    return lax.broadcasted_iota(jnp.int32, (8, 128), 1)


def incoming(packed, lane, kind, b=0):
    return turn(packed, {0: 127, 1: 0, -1: 126}[kind] - lane - b, 1)


def shift_y(main, rolled_outer, b, lane):
    if b == 0:
        return main, rolled_outer
    edge = lane == (127 if b == 1 else 0)
    rolled = turn(main, -b, 1)
    return jnp.where(edge, rolled_outer, rolled), jnp.where(edge, rolled, rolled_outer)


def along(values, pass_, steps=(1, 3, 9)):
    values = list(values)
    for step in steps:
        for start in range(len(values)):
            if (start // step) % 3 == 0:
                at = (start, start + step, start + 2 * step)
                for i, new in zip(at, pass_(*[values[j] for j in at])):
                    values[i] = new
    return values


def moments(values):
    def pass_(lo, mid, hi):
        both = lo + hi
        return both + mid, hi - lo, both
    return along(values, pass_)


def dual_moments(values):
    return along(values, lambda lo, mid, hi: (mid, hi - lo, (hi - mid) + (lo - mid)))


def from_moments(values):
    return along(values, lambda m0, m1, m2: (m2 - m1, m0 - (m2 + m2), m2 + m1))


def dual_back(z0, z1, z2):
    both = z0 + z2
    return both - z1, z0, both + z1


def collide(f, solid, scale):
    m = moments(f)
    rho = m[0]
    inverse = 1.0 / rho
    jx, jy, jz = m[mi(1, 0, 0)], m[mi(0, 1, 0)], m[mi(0, 0, 1)]
    ux, uy, uz = jx * inverse, jy * inverse, jz * inverse
    xx, yy, zz = jx * ux, jy * uy, jz * uz
    third = rho * (1.0 / 3.0)
    ninth = rho * (1.0 / 9.0)
    e = [None] * 27
    e[mi(2, 0, 0)], e[mi(0, 2, 0)], e[mi(0, 0, 2)] = third + xx, third + yy, third + zz
    e[mi(1, 1, 0)], e[mi(1, 0, 1)], e[mi(0, 1, 1)] = jx * uy, jx * uz, jy * uz
    jx3, jy3, jz3 = jx * (1.0 / 3.0), jy * (1.0 / 3.0), jz * (1.0 / 3.0)
    e[mi(1, 2, 0)] = e[mi(1, 0, 2)] = jx3
    e[mi(2, 1, 0)] = e[mi(0, 1, 2)] = jy3
    e[mi(2, 0, 1)] = e[mi(0, 2, 1)] = jz3
    e[mi(2, 2, 0)] = ninth + (xx + yy) * (1.0 / 3.0)
    e[mi(2, 0, 2)] = ninth + (xx + zz) * (1.0 / 3.0)
    e[mi(0, 2, 2)] = ninth + (yy + zz) * (1.0 / 3.0)
    e[mi(2, 1, 1)] = e[mi(0, 1, 1)] * (1.0 / 3.0)
    e[mi(1, 2, 1)] = e[mi(1, 0, 1)] * (1.0 / 3.0)
    e[mi(1, 1, 2)] = e[mi(1, 1, 0)] * (1.0 / 3.0)
    e[mi(1, 2, 2)], e[mi(2, 1, 2)], e[mi(2, 2, 1)] = jx * (1.0 / 9.0), jy * (1.0 / 9.0), jz * (1.0 / 9.0)
    e[mi(2, 2, 2)] = (third + (xx + yy + zz)) * (1.0 / 9.0)
    z = []
    for i in range(27):
        if i in (0, 1, 3, 9):
            z.append(jnp.zeros_like(rho))
        else:
            z.append((m[i] if e[i] is None else m[i] - e[i]) * scale[i])
    h = from_moments(z)
    out = [jnp.where(solid, f[26 - q], f[q] - h[q]) for q in range(27)]
    return out, (ux, uy, uz)


def low_rank(z):
    def at(i, j, k):
        return z[mi(i, j, k)]

    third = 1.0 / 3.0
    top = at(2, 2, 2) * third
    d_xy, d_xz, d_yz = at(2, 2, 0) + top, at(2, 0, 2) + top, at(0, 2, 2) + top
    q_xx = at(2, 0, 0) + (at(2, 2, 0) + d_xz) * third
    q_yy = at(0, 2, 0) + (at(0, 2, 2) + d_xy) * third
    q_zz = at(0, 0, 2) + (at(2, 0, 2) + d_yz) * third
    base = at(0, 0, 0) + (q_xx + (at(0, 2, 0) + at(0, 0, 2) + at(0, 2, 2) * third)) * third
    b_x = at(1, 0, 0) + (at(1, 2, 0) + at(1, 0, 2) + at(1, 2, 2) * third) * third
    b_y = at(0, 1, 0) + (at(2, 1, 0) + at(0, 1, 2) + at(2, 1, 2) * third) * third
    b_z = at(0, 0, 1) + (at(2, 0, 1) + at(0, 2, 1) + at(2, 2, 1) * third) * third
    q_xy = at(1, 1, 0) + at(1, 1, 2) * third
    q_xz = at(1, 0, 1) + at(1, 2, 1) * third
    q_yz = at(0, 1, 1) + at(2, 1, 1) * third
    return base, (b_x, b_y, b_z), (q_xx, q_yy, q_zz, q_xy, q_xz, q_yz)


def form(coefficients, u):
    q_xx, q_yy, q_zz, q_xy, q_xz, q_yz = coefficients
    ux, uy, uz = u
    p_x = (q_xx + q_xx) * ux + q_xy * uy + q_xz * uz
    p_y = q_xy * ux + (q_yy + q_yy) * uy + q_yz * uz
    p_z = q_xz * ux + q_yz * uy + (q_zz + q_zz) * uz
    return p_x, p_y, p_z, (p_x * ux + p_y * uy + p_z * uz) * 0.5


def pull_back_parts(v, u, solid, scale):
    z = [y * s for y, s in zip(dual_moments(v), scale)]
    base, (b_x, b_y, b_z), coefficients = low_rank(z)
    p_x, p_y, p_z, quad = form(coefficients, u)
    z[0] = z[0] - (base - quad)
    z[mi(1, 0, 0)] = z[mi(1, 0, 0)] - (b_x + p_x)
    z[mi(0, 1, 0)] = z[mi(0, 1, 0)] - (b_y + p_y)
    z[mi(0, 0, 1)] = z[mi(0, 0, 1)] - (b_z + p_z)
    h = along(z, dual_back, (9, 3))
    for a in range(3):
        part = along(h[9 * a:9 * a + 9], dual_back, (1,))
        yield [jnp.where(solid, v[26 - q], v[q] - part[q - 9 * a]) for q in range(9 * a, 9 * a + 9)]


def pull_back(v, u, solid, scale):
    return sum(pull_back_parts(v, u, solid, scale), [])


def side_pull_back(groups, side, scale):
    def pass_(lo, mid, hi):
        return mid, hi - lo, (hi - mid) + (lo - mid)

    t = {a: along(values, pass_, (1, 3)) for a, values in groups.items()}
    if side in t:
        still, moved = t[0], t[side]
        first = moved if side == 1 else [-v for v in moved]
        second = [(v - m) - m for v, m in zip(moved, still)]
    else:
        moved = t[-side]
        still = [jnp.zeros_like(v) for v in moved]
        first = moved if side == -1 else [-v for v in moved]
        second = moved
    z = [y * s for y, s in zip(list(still) + list(first) + list(second), scale)]
    base, (b_x, b_y, b_z), coefficients = low_rank(z)
    z[0] = z[0] - base
    z[mi(1, 0, 0)] = z[mi(1, 0, 0)] - b_x
    z[mi(0, 1, 0)] = z[mi(0, 1, 0)] - b_y
    z[mi(0, 0, 1)] = z[mi(0, 0, 1)] - b_z
    h = [(z[i] + z[18 + i]) + z[9 + i] if side == 1 else (z[i] + z[18 + i]) - z[9 + i] for i in range(9)]
    h = along(h, dual_back, (1, 3))
    if side in groups:
        return [v - w for v, w in zip(groups[side], h)], coefficients
    return [-w for w in h], coefficients


def first_kernel(rows, rates_in, f_in, wall_in, cot_in, cot, scale_out, sums, speed, solid_out, packed,
                 raw_right,
                 rates, f, wall, sems):
    pairs = ((f_in, f), (rates_in, rates), (wall_in, wall), (cot_in, cot))
    copies = [pltpu.make_async_copy(source, target, sems.at[i]) for i, (source, target) in enumerate(pairs)]
    for copy in copies:
        copy.start()
    for copy in copies[:3]:
        copy.wait()
    for i in range(27):
        scale_out[i] = jnp.full((8, 128), rates[i] * (0.5 ** NNZ[i]), F32)
    scale = [rates[i] * (0.5 ** NNZ[i]) for i in range(27)]
    plane = lax.broadcasted_iota(jnp.int32, (8, 128), 0)
    boundary = (plane == 0) | (plane == 7)
    lane = lanes()
    table, _ = slots(rows)
    for x in range(rows):
        at = pl.ds(x, 8, stride=rows)
        solid = boundary | (wall[at, :] == 1)
        solid_out[x] = jnp.where(solid, 1.0, 0.0)
        out, u = collide([f[q, at, :] for q in range(27)], solid, scale)
        for k in range(3):
            speed[k, x] = u[k]
        for a in SIGNS:
            for b in SIGNS:
                low = turn(out[qi(a, b, -1)], -1, 0)
                high = turn(out[qi(a, b, 1)], 1, 0)
                i = 2 * (3 * (a + 1) + b + 1)
                sums[i, x] = out[qi(a, b, 0)] + (low + high)
                sums[i + 1, x] = high - low
    for copy in copies[3:]:
        copy.wait()
    raw_rows(rows, -1, cot, raw_right, 0)
    clear_end(raw_right, raw_height(-1))
    def block(key):
        if key[0] == "v":
            return cot[key[1], pl.ds(key[2], 8, stride=rows), :]
        if key[0] == "w":
            return solid_out[key[1]]
        return sums[2 * (3 * (key[1] + 1) + key[2] + 1) + key[3], key[4]]

    quads, singles, _ = layout(rows)
    by_two, by_four = lane >> 1, lane >> 2
    high_lanes = lane >= 64
    for g in range(3):
        piece = jnp.zeros((8, 128), F32)
        for n, (low, high) in enumerate(quads[g]):
            both = jnp.where(high_lanes, block(low), block(high))
            piece = jnp.where(by_four == n, turn(both, 4 * n + 2, 1), piece)
        for n, key in enumerate(singles[g]):
            i = 4 * len(quads[g]) + 2 * n
            piece = jnp.where(by_two == i // 2, turn(block(key), i + 1, 1), piece)
        packed[g] = piece


FULL = 9


def edge_rows(rows, side):
    near, far = (0, 1) if side == 1 else (rows - 1, rows - 2)
    keys = [(q, near) for q, c in enumerate(Q) if c[0] == side]
    keys += [(q, near) for q, c in enumerate(Q) if c[0] == 0]
    return keys + [(q, far) for q, c in enumerate(Q) if c[0] == side]


REDUCED = (1, -1)


def raw_count(side):
    return FULL if side in REDUCED else 27


def raw_at(k, gap):
    return 8 * k if k < FULL else 8 * FULL + gap + 6 * (k - FULL)


def raw_height(side):
    return raw_at(raw_count(side), 0)


def small_height(side):
    return 8 + 6 * (23 if side in REDUCED else 8)


def padded(count):
    return (count + 7) // 8 * 8


def raw_rows(rows, side, cot, message, gap):
    for k, (q, x) in enumerate(edge_rows(rows, side)[:raw_count(side)]):
        at = raw_at(k, gap)
        if k < FULL:
            message[at:at + 8] = cot[q, pl.ds(x, 8, stride=rows), :]
        else:
            message[at:at + 6] = cot[q, pl.ds(x + rows * (1 + Q[q][2]), 6, stride=rows), :]


def clear_end(message, count):
    if message.shape[0] > count:
        message[count:] = jnp.zeros((message.shape[0] - count, 128), F32)


def planes(ref, at):
    start = min(at - 1, ref.shape[0] - 8)
    return turn(ref[start:start + 8], 1 - (at - start), 0)


def sent_sums(rows):
    return [(-1, 0), (-1, 1), (0, 0), (0, rows - 1), (1, rows - 1), (1, rows - 2)]


def sums_over_y(a, x, sums, halo, table, lane):
    parts = {}
    for b in SIGNS:
        for s in range(2):
            i = 2 * (3 * (a + 1) + b + 1) + s
            g, at, kind = table["s", a, b, s, x]
            parts[b, s] = shift_y(sums[i, x], incoming(halo[g], at, kind, -b), -b, lane)
    return [(
        parts[0, 0][n] + (parts[-1, 0][n] + parts[1, 0][n]),
        parts[1, 0][n] - parts[-1, 0][n],
        parts[0, 1][n] + (parts[-1, 1][n] + parts[1, 1][n]),
    ) for n in range(2)]


def second_kernel(rows, scale_in, cot, sums, solid_in, from_left, from_right, to_left, to_right, sent, merged):
    lane = lanes()
    table, used = slots(rows)
    by_two = lane >> 1
    halo = []
    for g in range(3):
        end = 4 * len(layout(rows)[0][g])
        takes_left = ((lane < end) & ((lane & 2) == 0)) | ((lane >= end) & ((lane & 1) == 0))
        halo.append(jnp.where(takes_left, from_left[g], from_right[g]))
        merged[g] = halo[g]

    t = {}
    for i, (a, x) in enumerate(sent_sums(rows)):
        t[a, x] = sums_over_y(a, x, sums, halo, table, lane)
        for n in range(2):
            for k in range(3):
                sent[i, 2 * k + n] = t[a, x][n][k]
    turned = {(g, c): turn(halo[g], -c, 0) for g in range(2) for c in SIGNS}
    keys = sent_sums(rows)

    def both(a, x, n):
        return [sent[keys.index((a, x)), 2 * k + n] for k in range(3)]

    def one_side(side, message):
        near, far = (0, 1) if side == 1 else (rows - 1, rows - 2)
        with_raw = side == 1
        at = 8 * FULL if with_raw else 0
        items = raw_height(side) + 8 if with_raw else 8
        if with_raw:
            raw_rows(rows, side, cot, message, 8)
        clear_end(message, (raw_height(side) if with_raw else 0) + small_height(side))
        extra = []
        for n in range(2):
            row = both(-side, near, n)
            still, moved = both(0, near, n), both(-side, far, n)
            row += [still[0] + moved[0], moved[0] if side == -1 else -moved[0]]
            row += [still[1] + moved[1], still[2] + moved[2]]
            row.append(solid_in[near] if n == 0 else incoming(halo[table["w", near][0]], table["w", near][1], 0))
            extra.append(row)
        columns = halo[0]
        if side in REDUCED:
            groups = {0: [], side: []}
            for q, x in edge_rows(rows, side)[FULL:]:
                a, b, c = Q[q]
                main, beyond = gathered(rows, x - a, q, cot, turned, lane)
                groups[a].append(main)
                i = table["v", q, x][1]
                columns = jnp.where(by_two == i // 2, turn(beyond, i + 1, 1), columns)
            part, coefficients = side_pull_back(groups, side, [scale_in[i] for i in range(27)])
            extra[0] += list(part) + list(coefficients)
        for k, value in enumerate(extra[0]):
            message[items + 6 * k:items + 6 * k + 6] = value[1:7]
        for k in range(8):
            i = used + 2 * k
            columns = jnp.where(by_two == i // 2, turn(extra[1][k], i + 1, 1), columns)
        message[at:at + 8] = columns

    one_side(-1, to_right)
    pl.when(lax.axis_index("gx") >= 0)(functools.partial(one_side, 1, to_left))


def outer_rows(rows):
    return [x for x in range(-1, rows + 1) if not 0 < x < rows - 1]


def gathered(rows, x, q, cot, turned, lane, remote=None):
    table, _ = slots(rows)
    a, b, c = Q[q]
    source = x + a
    if 0 <= source < rows:
        main = turn(cot[q, pl.ds(source, 8, stride=rows), :], -c, 0)
        group, i, kind = table["v", q, source]
    else:
        load, group, i, kind = remote[q, source]
        main = load()
    outer = incoming(turned[group, c], i, kind, b)
    return shift_y(main, outer, b, lane)


def middle_kernel(rows, scale_in, cot, sums, solid_in, sent, merged, inner, known, own):
    scale = [scale_in[i] for i in range(27)]
    lane = lanes()
    table, _ = slots(rows)
    halo = [merged[g] for g in range(3)]
    t = {key: [[sent[i, 2 * k + n] for k in range(3)] for n in range(2)] for i, key in enumerate(sent_sums(rows))}
    for a in SIGNS:
        for x in range(rows):
            if (a, x) not in t:
                t[a, x] = sums_over_y(a, x, sums, halo, table, lane)
    for x in range(-1, rows + 1):
        for n in range(2):
            terms = [(a, t[a, x - a][n]) for a in SIGNS if 0 <= x - a < rows]
            along_x = jnp.zeros((8, 128), F32)
            for a, v in terms:
                if a:
                    along_x = along_x + v[0] if a == 1 else along_x - v[0]
            moments_here = [functools.reduce(jnp.add, [v[k] for _, v in terms]) for k in range(3)]
            for k, v in enumerate([moments_here[0], along_x] + moments_here[1:]):
                own[k, 2 * (x + 1) + n] = v
    turned = {(g, c): turn(merged[g], -c, 0) for g in range(2) for c in SIGNS}
    for x in range(1, rows - 1):
        v = [gathered(rows, x, q, cot, turned, lane) for q in range(27)]
        for n in range(2):
            total = [own[k, 2 * (x + 1) + n] for k in range(4)]
            inverse = 1.0 / total[0]
            if n == 0:
                wall = solid_in[x]
            else:
                g, i, kind = table["w", x]
                wall = incoming(merged[g], i, kind)
            out = pull_back([t[n] for t in v], [t * inverse for t in total[1:]], wall > 0.5, scale)
            for q in range(27):
                inner[q, 2 * (x - 1) + n] = out[q]
    for j, x in enumerate(outer_rows(rows)):
        for q in range(27):
            if 0 <= x + Q[q][0] < rows:
                known[q, 2 * j], known[q, 2 * j + 1] = gathered(rows, x, q, cot, turned, lane)


def outer_gradient(rows, side, scale, solid_in, own, merged, known, raw, gap, extra, columns_at, items_at, g1):
    lane = lanes()
    table, used = slots(rows)
    remote = {}
    def load(k, c):
        at = raw_at(k, gap)
        return turn(raw[at:at + 8], -c, 0) if k < FULL else planes(raw, at)

    for k, (q, x) in enumerate(edge_rows(rows, side)[:raw_count(side)]):
        _, i, kind = table["v", q, x]
        remote[q, x + side * rows] = (functools.partial(load, k, Q[q][2]), "far", i, kind)
    columns = extra[columns_at:columns_at + 8]
    turned = {("far", c): turn(columns, -c, 0) for c in SIGNS}
    plane = lax.broadcasted_iota(jnp.int32, (8, 128), 0)
    boundary = (plane == 0) | (plane == 7)
    near = rows - 1 if side == 1 else 0
    for j, x in enumerate(outer_rows(rows)):
        if x not in (near, near + side):
            continue
        v = []
        for q, (a, b, c) in enumerate(Q):
            if 0 <= x + a < rows:
                v.append((known[q, 2 * j], known[q, 2 * j + 1]))
            elif x == near or side not in REDUCED:
                v.append(gathered(rows, x, q, None, turned, lane, remote))
            else:
                v.append((None, incoming(columns, table["v", q, x + a - side * rows][1], 0)))
        for n in range(2):
            def got(k):
                return planes(extra, items_at + 6 * k) if n == 0 else incoming(columns, used + 2 * k, 0)

            total = [own[k, 2 * (x + 1) + n] for k in range(4)]
            if x == near:
                total = [total[0] + got(0), total[1] - got(0) if side == 1 else total[1] + got(0),
                         total[2] + got(1), total[3] + got(2)]
                if n == 0:
                    wall = solid_in[x]
                else:
                    g, i, kind = table["w", x]
                    wall = incoming(merged[g], i, kind)
            else:
                total = [total[k] + got(3 + k) for k in range(4)]
                wall = got(7)
            inverse = 1.0 / total[0]
            u = [t * inverse for t in total[1:]]
            solid = boundary | (wall > 0.5)
            if x != near and n == 0 and side in REDUCED:
                mine = [t[0] for t in v[9 * (1 - side):9 * (1 - side) + 9]]
                part, coefficients = side_pull_back({-side: mine}, side, scale)
                p_x, p_y, p_z, quad = form([m + got(17 + k) for k, m in enumerate(coefficients)], u)
                start = (p_x if side == 1 else -p_x) - quad
                along_y = {-1: start - p_y, 0: start, 1: start + p_y}
                for i in range(9):
                    b, c = i // 3 - 1, i % 3 - 1
                    rest = along_y[b] + p_z if c == 1 else along_y[b] - p_z if c == -1 else along_y[b]
                    value = (part[i] + got(8 + i)) + rest
                    g1[9 * (1 + side) + i, 2 * (j % 2)] = jnp.where(solid, mine[8 - i], value)
                continue
            g = pull_back([t[n] for t in v], u, solid, scale)
            for q in range(27):
                if 0 <= x - Q[q][0] < rows:
                    g1[q, 2 * (j % 2) + n] = g[q]


def pulled_row(rows, x, arrays, speed, solid_in, scale, lane):
    v = []
    for q, (a, b, c) in enumerate(Q):
        array, r = arrays(x + a)
        main = array[q, r]
        if b:
            main = shift_y(main, turn(array[q, r + 1], -b, 1), b, lane)[0]
        v.append(turn(main, -c, 0))
    return pull_back_parts(v, [speed[k, x] for k in range(3)], solid_in[x] > 0.5, scale)


def low_kernel(rows, scale_in, speed, solid_in, own, merged, inner, known, raw, extra, done, g1):
    scale = [scale_in[i] for i in range(27)]
    lane = lanes()
    outer_gradient(rows, -1, scale, solid_in, own, merged, known, raw, 0, extra, 0, 8, g1)

    def arrays(x):
        return (g1, 2 * (x + 1)) if x < 1 else (inner, 2 * (x - 1))

    for x in range(rows - 2):
        for a, part in enumerate(pulled_row(rows, x, arrays, speed, solid_in, scale, lane)):
            for i, value in enumerate(part):
                done[9 * a + i, x] = value


def last_kernel(rows, scale_in, speed, solid_in, own, merged, inner, known, done, from_high, out_hbm, high, out, sems):
    scale = [scale_in[i] for i in range(27)]
    lane = lanes()
    outer_gradient(rows, 1, scale, solid_in, own, merged, known, from_high, 8, from_high, 8 * FULL, raw_height(1) + 8, high)

    def arrays(x):
        return (inner, 2 * (x - 1)) if x < rows - 1 else (high, 2 * (x - rows + 1))

    late = {x: pulled_row(rows, x, arrays, speed, solid_in, scale, lane) for x in range(rows - 2, rows)}
    copies = []
    for a in range(3):
        for x in range(rows):
            part = next(late[x]) if x in late else [done[9 * a + i, x] for i in range(9)]
            for i, value in enumerate(part):
                out[9 * a + i, pl.ds(x, 8, stride=rows), :] = value
        part = pl.ds(9 * a, 9)
        copies.append(pltpu.make_async_copy(out.at[part], out_hbm.at[part], sems.at[a]))
        copies[a].start()
    for copy in copies:
        copy.wait()


def call(kernel, name, out_shapes, scratch, operands, space=pltpu.VMEM, work=0, out_space=pltpu.VMEM):
    return pl.pallas_call(
        kernel,
        out_shape=[jax.ShapeDtypeStruct(s, F32) for s in out_shapes],
        in_specs=[pl.BlockSpec(memory_space=space)] * len(operands),
        out_specs=[pl.BlockSpec(memory_space=out_space)] * len(out_shapes),
        scratch_shapes=scratch,
        compiler_params=pltpu.CompilerParams(vmem_limit_bytes=32 * 1024 * 1024),
        cost_estimate=pl.CostEstimate(flops=work, bytes_accessed=0 if work else 0, transcendentals=0) if work else None,
        name=name,
    )(*operands)


def ring(block, axis, step):
    size = lax.axis_size(axis)
    return lax.ppermute(block, axis, [(i, (i + step) % size) for i in range(size)])


def swap(block, axis, first):
    size = lax.axis_size(axis)
    route = []
    for i in range(first, size + first, 2):
        route += [(i % size, (i + 1) % size), ((i + 1) % size, i % size)]
    return lax.ppermute(block, axis, route)


def shards(checkpoint, rates, wall_mask, cotangent):
    planes, rows, width = checkpoint.shape[1:]
    f = checkpoint.reshape(27, planes * rows, width)
    cot = cotangent.reshape(27, planes * rows, width)
    wall = wall_mask.reshape(planes * rows, width)
    tile = (planes, width)
    lattice = (27, planes * rows, width)
    cot, scale, sums, speed, solid, packed, raw_right = call(
        functools.partial(first_kernel, rows), "collide",
        [lattice, (27,) + tile, (18, rows) + tile, (3, rows) + tile, (rows,) + tile, (3,) + tile,
         (padded(raw_height(-1)), width)],
        [pltpu.SMEM((27,), F32), pltpu.VMEM(lattice, F32), pltpu.VMEM(lattice[1:], jnp.int32),
         pltpu.SemaphoreType.DMA((4,))],
        tuple(pltpu.with_memory_space_constraint(v, pltpu.HBM) for v in (rates, f, wall, cot)), pltpu.HBM)
    raw_low = ring(raw_right, "gx", 1)
    across, inside = swap(packed, "gy", 1), swap(packed, "gy", 0)
    odd = lax.axis_index("gy") % 2 == 1
    from_left = jnp.where(odd, inside, across)
    from_right = jnp.where(odd, across, inside)
    to_left, small_right, sent, merged = call(
        functools.partial(second_kernel, rows), "pack",
        [(padded(raw_height(1) + small_height(1)), width), (padded(small_height(-1)), width), (6, 6) + tile, (3,) + tile], [],
        (scale, cot, sums, solid, from_left, from_right))
    small_low = ring(small_right, "gx", 1)
    from_high = ring(to_left, "gx", -1)
    inner, known, own = call(
        functools.partial(middle_kernel, rows), "inner_rows",
        [(27, 2 * rows - 4) + tile, (27, 8) + tile, (4, 2 * rows + 4) + tile], [],
        (scale, cot, sums, solid, sent, merged))
    def hold(source, target):
        target[...] = source[...]

    (raw_low,) = call(hold, "near_rows", [(padded(raw_height(-1)), width)], [], (raw_low,), work=1000000000)
    (done,) = call(
        functools.partial(low_kernel, rows), "low_rows",
        [(27, rows - 2) + tile], [pltpu.VMEM((27, 4) + tile, F32)],
        (scale, speed, solid, own, merged, inner, known, raw_low, small_low), work=2000000000)
    (out,) = call(
        functools.partial(last_kernel, rows), "gradient",
        [lattice],
        [pltpu.VMEM((27, 4) + tile, F32), pltpu.VMEM(lattice, F32), pltpu.SemaphoreType.DMA((3,))],
        (scale, speed, solid, own, merged, inner, known, done, from_high), out_space=pltpu.HBM)
    return out.reshape(checkpoint.shape)


def solution(mesh):
    in_specs = (P(None, None, "gx", "gy"), P(), P(None, "gx", "gy"), P(None, None, "gx", "gy"))
    out_specs = P(None, None, "gx", "gy")
    return jax.shard_map(shards, mesh=mesh, in_specs=in_specs, out_specs=out_specs, check_vma=False)
```

```python
import functools
import jax
import jax.numpy as jnp
from jax import lax
from jax.experimental import pallas as pl
from jax.experimental.pallas import tpu as pltpu
from jax.sharding import PartitionSpec as P

F32 = jnp.float32
SIGNS = (-1, 0, 1)
Q = [(a, b, c) for a in SIGNS for b in SIGNS for c in SIGNS]


def qi(a, b, c):
    return 9 * (a + 1) + 3 * (b + 1) + (c + 1)


def mi(i, j, k):
    return 9 * i + 3 * j + k


NNZ = [(i > 0) + (j > 0) + (k > 0) for i in range(3) for j in range(3) for k in range(3)]


def layout(rows):
    quads, singles = [[], [], []], [[], [], []]
    for a in SIGNS:
        for c in SIGNS:
            for x in range(rows):
                left = (a >= 0 and x == 0) or (a == 1 and x == 1)
                right = (a <= 0 and x == rows - 1) or (a == -1 and x == rows - 2)
                g = 0 if left or right else 1
                quads[g].append((("v", qi(a, -1, c), x), ("v", qi(a, 1, c), x)))
                singles[g].append(("v", qi(a, 0, c), x))
    used = 4 * len(quads[0]) + 2 * len(singles[0])
    singles[1] += [("w", x) for x in range(rows)]
    for a in SIGNS:
        for s in range(2):
            for x in range(rows):
                quads[2].append((("s", a, 1, s, x), ("s", a, -1, s, x)))
                singles[2].append(("s", a, 0, s, x))
    room = 64 - 2 * len(quads[2])
    singles[0] += singles[2][room:]
    singles[2] = singles[2][:room]
    return quads, singles, used


def slots(rows):
    quads, singles, used = layout(rows)
    table = {}
    for g in range(3):
        for n, (low, high) in enumerate(quads[g]):
            table[low], table[high] = (g, 4 * n, -1), (g, 4 * n + 2, 1)
        for n, key in enumerate(singles[g]):
            table[key] = (g, 4 * len(quads[g]) + 2 * n, 0)
    return table, used


def turn(v, shift, axis):
    shift = shift % v.shape[axis]
    return v if shift == 0 else pltpu.roll(v, shift, axis)


def region(body):
    pl.when(lax.axis_index("gx") >= 0)(body)


def lanes():
    return lax.broadcasted_iota(jnp.int32, (8, 128), 1)


def incoming(packed, lane, kind, b=0):
    return turn(packed, {0: 127, 1: 0, -1: 126}[kind] - lane - b, 1)


def shift_y(main, rolled_outer, b, lane):
    if b == 0:
        return main, rolled_outer
    edge = lane == (127 if b == 1 else 0)
    rolled = turn(main, -b, 1)
    return jnp.where(edge, rolled_outer, rolled), jnp.where(edge, rolled, rolled_outer)


def along(values, pass_, steps=(1, 3, 9)):
    values = list(values)
    for step in steps:
        for start in range(len(values)):
            if (start // step) % 3 == 0:
                at = (start, start + step, start + 2 * step)
                for i, new in zip(at, pass_(*[values[j] for j in at])):
                    values[i] = new
    return values


def moments(values):
    def pass_(lo, mid, hi):
        both = lo + hi
        return both + mid, hi - lo, both
    return along(values, pass_)


def dual_moments(values):
    return along(values, lambda lo, mid, hi: (mid, hi - lo, (hi - mid) + (lo - mid)))


def from_moments(values):
    return along(values, lambda m0, m1, m2: (m2 - m1, m0 - (m2 + m2), m2 + m1))


def dual_back(z0, z1, z2):
    both = z0 + z2
    return both - z1, z0, both + z1


def collide(f, solid, scale):
    m = moments(f)
    rho = m[0]
    inverse = 1.0 / rho
    jx, jy, jz = m[mi(1, 0, 0)], m[mi(0, 1, 0)], m[mi(0, 0, 1)]
    ux, uy, uz = jx * inverse, jy * inverse, jz * inverse
    xx, yy, zz = jx * ux, jy * uy, jz * uz
    third = rho * (1.0 / 3.0)
    ninth = rho * (1.0 / 9.0)
    e = [None] * 27
    e[mi(2, 0, 0)], e[mi(0, 2, 0)], e[mi(0, 0, 2)] = third + xx, third + yy, third + zz
    e[mi(1, 1, 0)], e[mi(1, 0, 1)], e[mi(0, 1, 1)] = jx * uy, jx * uz, jy * uz
    jx3, jy3, jz3 = jx * (1.0 / 3.0), jy * (1.0 / 3.0), jz * (1.0 / 3.0)
    e[mi(1, 2, 0)] = e[mi(1, 0, 2)] = jx3
    e[mi(2, 1, 0)] = e[mi(0, 1, 2)] = jy3
    e[mi(2, 0, 1)] = e[mi(0, 2, 1)] = jz3
    e[mi(2, 2, 0)] = ninth + (xx + yy) * (1.0 / 3.0)
    e[mi(2, 0, 2)] = ninth + (xx + zz) * (1.0 / 3.0)
    e[mi(0, 2, 2)] = ninth + (yy + zz) * (1.0 / 3.0)
    e[mi(2, 1, 1)] = e[mi(0, 1, 1)] * (1.0 / 3.0)
    e[mi(1, 2, 1)] = e[mi(1, 0, 1)] * (1.0 / 3.0)
    e[mi(1, 1, 2)] = e[mi(1, 1, 0)] * (1.0 / 3.0)
    e[mi(1, 2, 2)], e[mi(2, 1, 2)], e[mi(2, 2, 1)] = jx * (1.0 / 9.0), jy * (1.0 / 9.0), jz * (1.0 / 9.0)
    e[mi(2, 2, 2)] = (third + (xx + yy + zz)) * (1.0 / 9.0)
    z = []
    for i in range(27):
        if i in (0, 1, 3, 9):
            z.append(jnp.zeros_like(rho))
        else:
            z.append((m[i] if e[i] is None else m[i] - e[i]) * scale[i])
    h = from_moments(z)
    out = [jnp.where(solid, f[26 - q], f[q] - h[q]) for q in range(27)]
    return out, (ux, uy, uz)


def low_rank(z):
    def at(i, j, k):
        return z[mi(i, j, k)]

    third = 1.0 / 3.0
    top = at(2, 2, 2) * third
    d_xy, d_xz, d_yz = at(2, 2, 0) + top, at(2, 0, 2) + top, at(0, 2, 2) + top
    q_xx = at(2, 0, 0) + (at(2, 2, 0) + d_xz) * third
    q_yy = at(0, 2, 0) + (at(0, 2, 2) + d_xy) * third
    q_zz = at(0, 0, 2) + (at(2, 0, 2) + d_yz) * third
    base = at(0, 0, 0) + (q_xx + (at(0, 2, 0) + at(0, 0, 2) + at(0, 2, 2) * third)) * third
    b_x = at(1, 0, 0) + (at(1, 2, 0) + at(1, 0, 2) + at(1, 2, 2) * third) * third
    b_y = at(0, 1, 0) + (at(2, 1, 0) + at(0, 1, 2) + at(2, 1, 2) * third) * third
    b_z = at(0, 0, 1) + (at(2, 0, 1) + at(0, 2, 1) + at(2, 2, 1) * third) * third
    q_xy = at(1, 1, 0) + at(1, 1, 2) * third
    q_xz = at(1, 0, 1) + at(1, 2, 1) * third
    q_yz = at(0, 1, 1) + at(2, 1, 1) * third
    return base, (b_x, b_y, b_z), (q_xx, q_yy, q_zz, q_xy, q_xz, q_yz)


def form(coefficients, u):
    q_xx, q_yy, q_zz, q_xy, q_xz, q_yz = coefficients
    ux, uy, uz = u
    p_x = (q_xx + q_xx) * ux + q_xy * uy + q_xz * uz
    p_y = q_xy * ux + (q_yy + q_yy) * uy + q_yz * uz
    p_z = q_xz * ux + q_yz * uy + (q_zz + q_zz) * uz
    return p_x, p_y, p_z, (p_x * ux + p_y * uy + p_z * uz) * 0.5


def pull_back_parts(v, u, solid, scale):
    z = [y * s for y, s in zip(dual_moments(v), scale)]
    base, (b_x, b_y, b_z), coefficients = low_rank(z)
    p_x, p_y, p_z, quad = form(coefficients, u)
    z[0] = z[0] - (base - quad)
    z[mi(1, 0, 0)] = z[mi(1, 0, 0)] - (b_x + p_x)
    z[mi(0, 1, 0)] = z[mi(0, 1, 0)] - (b_y + p_y)
    z[mi(0, 0, 1)] = z[mi(0, 0, 1)] - (b_z + p_z)
    h = along(z, dual_back, (9, 3))
    for a in range(3):
        part = along(h[9 * a:9 * a + 9], dual_back, (1,))
        yield [jnp.where(solid, v[26 - q], v[q] - part[q - 9 * a]) for q in range(9 * a, 9 * a + 9)]


def pull_back(v, u, solid, scale):
    return sum(pull_back_parts(v, u, solid, scale), [])


def side_pull_back(groups, side, scale):
    def pass_(lo, mid, hi):
        return mid, hi - lo, (hi - mid) + (lo - mid)

    t = {a: along(values, pass_, (1, 3)) for a, values in groups.items()}
    if side in t:
        still, moved = t[0], t[side]
        first = moved if side == 1 else [-v for v in moved]
        second = [(v - m) - m for v, m in zip(moved, still)]
    else:
        moved = t[-side]
        still = [jnp.zeros_like(v) for v in moved]
        first = moved if side == -1 else [-v for v in moved]
        second = moved
    z = [y * s for y, s in zip(list(still) + list(first) + list(second), scale)]
    base, (b_x, b_y, b_z), coefficients = low_rank(z)
    z[0] = z[0] - base
    z[mi(1, 0, 0)] = z[mi(1, 0, 0)] - b_x
    z[mi(0, 1, 0)] = z[mi(0, 1, 0)] - b_y
    z[mi(0, 0, 1)] = z[mi(0, 0, 1)] - b_z
    h = [(z[i] + z[18 + i]) + z[9 + i] if side == 1 else (z[i] + z[18 + i]) - z[9 + i] for i in range(9)]
    h = along(h, dual_back, (1, 3))
    if side in groups:
        return [v - w for v, w in zip(groups[side], h)], coefficients
    return [-w for w in h], coefficients


def first_kernel(rows, rates_in, f_in, wall_in, cot_in, cot, scale_out, sums, speed, solid_out, packed,
                 raw_right,
                 rates, f, wall, sems):
    pairs = ((f_in, f), (rates_in, rates), (wall_in, wall), (cot_in, cot))
    copies = [pltpu.make_async_copy(source, target, sems.at[i]) for i, (source, target) in enumerate(pairs)]
    for copy in copies:
        copy.start()
    for copy in copies[:3]:
        copy.wait()
    for i in range(27):
        scale_out[i] = jnp.full((8, 128), rates[i] * (0.5 ** NNZ[i]), F32)
    scale = [rates[i] * (0.5 ** NNZ[i]) for i in range(27)]
    plane = lax.broadcasted_iota(jnp.int32, (8, 128), 0)
    boundary = (plane == 0) | (plane == 7)
    lane = lanes()
    table, _ = slots(rows)
    for x in range(rows):
        at = pl.ds(x, 8, stride=rows)
        solid = boundary | (wall[at, :] == 1)
        solid_out[x] = jnp.where(solid, 1.0, 0.0)
        out, u = collide([f[q, at, :] for q in range(27)], solid, scale)
        for k in range(3):
            speed[k, x] = u[k]
        for a in SIGNS:
            for b in SIGNS:
                low = turn(out[qi(a, b, -1)], -1, 0)
                high = turn(out[qi(a, b, 1)], 1, 0)
                i = 2 * (3 * (a + 1) + b + 1)
                sums[i, x] = out[qi(a, b, 0)] + (low + high)
                sums[i + 1, x] = high - low
    for copy in copies[3:]:
        copy.wait()
    raw_rows(rows, -1, cot, raw_right, 0)
    clear_end(raw_right, raw_height(-1))
    def block(key):
        if key[0] == "v":
            return cot[key[1], pl.ds(key[2], 8, stride=rows), :]
        if key[0] == "w":
            return solid_out[key[1]]
        return sums[2 * (3 * (key[1] + 1) + key[2] + 1) + key[3], key[4]]

    quads, singles, _ = layout(rows)
    by_two, by_four = lane >> 1, lane >> 2
    high_lanes = lane >= 64
    def pack(g):
        piece = jnp.zeros((8, 128), F32)
        for n, (low, high) in enumerate(quads[g]):
            both = jnp.where(high_lanes, block(low), block(high))
            piece = jnp.where(by_four == n, turn(both, 4 * n + 2, 1), piece)
        for n, key in enumerate(singles[g]):
            i = 4 * len(quads[g]) + 2 * n
            piece = jnp.where(by_two == i // 2, turn(block(key), i + 1, 1), piece)
        packed[g] = piece

    for g in range(3):
        region(functools.partial(pack, g))


FULL = 9


def edge_rows(rows, side):
    near, far = (0, 1) if side == 1 else (rows - 1, rows - 2)
    keys = [(q, near) for q, c in enumerate(Q) if c[0] == side]
    keys += [(q, near) for q, c in enumerate(Q) if c[0] == 0]
    return keys + [(q, far) for q, c in enumerate(Q) if c[0] == side]


REDUCED = (1,)


def raw_count(side):
    return FULL if side in REDUCED else 27


def raw_at(k, gap):
    return 8 * k if k < FULL else 8 * FULL + gap + 6 * (k - FULL)


def raw_height(side):
    return raw_at(raw_count(side), 0)


def small_height(side):
    return 8 + 6 * (23 if side in REDUCED else 8)


def padded(count):
    return (count + 7) // 8 * 8


def raw_rows(rows, side, cot, message, gap):
    for k, (q, x) in enumerate(edge_rows(rows, side)[:raw_count(side)]):
        at = raw_at(k, gap)
        if k < FULL:
            message[at:at + 8] = cot[q, pl.ds(x, 8, stride=rows), :]
        else:
            message[at:at + 6] = cot[q, pl.ds(x + rows * (1 + Q[q][2]), 6, stride=rows), :]


def clear_end(message, count):
    if message.shape[0] > count:
        message[count:] = jnp.zeros((message.shape[0] - count, 128), F32)


def planes(ref, at):
    start = min(at - 1, ref.shape[0] - 8)
    return turn(ref[start:start + 8], 1 - (at - start), 0)


def sent_sums(rows):
    return [(-1, 0), (-1, 1), (0, 0), (0, rows - 1), (1, rows - 1), (1, rows - 2)]


def sums_over_y(a, x, sums, halo, table, lane):
    parts = {}
    for b in SIGNS:
        for s in range(2):
            i = 2 * (3 * (a + 1) + b + 1) + s
            g, at, kind = table["s", a, b, s, x]
            parts[b, s] = shift_y(sums[i, x], incoming(halo[g], at, kind, -b), -b, lane)
    return [(
        parts[0, 0][n] + (parts[-1, 0][n] + parts[1, 0][n]),
        parts[1, 0][n] - parts[-1, 0][n],
        parts[0, 1][n] + (parts[-1, 1][n] + parts[1, 1][n]),
    ) for n in range(2)]


def second_kernel(rows, scale_in, cot, sums, solid_in, from_left, from_right, to_left, to_right, sent, merged):
    lane = lanes()
    table, used = slots(rows)
    by_two = lane >> 1
    halo = []
    for g in range(3):
        end = 4 * len(layout(rows)[0][g])
        takes_left = ((lane < end) & ((lane & 2) == 0)) | ((lane >= end) & ((lane & 1) == 0))
        halo.append(jnp.where(takes_left, from_left[g], from_right[g]))
        merged[g] = halo[g]

    t = {}
    for i, (a, x) in enumerate(sent_sums(rows)):
        t[a, x] = sums_over_y(a, x, sums, halo, table, lane)
        for n in range(2):
            for k in range(3):
                sent[i, 2 * k + n] = t[a, x][n][k]
    turned = {(g, c): turn(halo[g], -c, 0) for g in range(2) for c in SIGNS}
    for side, message in ((1, to_left), (-1, to_right)):
        near, far = (0, 1) if side == 1 else (rows - 1, rows - 2)
        with_raw = side == 1
        at = 8 * FULL if with_raw else 0
        items = raw_height(side) + 8 if with_raw else 8
        if with_raw:
            raw_rows(rows, side, cot, message, 8)
        clear_end(message, (raw_height(side) if with_raw else 0) + small_height(side))
        extra = []
        for n in range(2):
            row = list(t[-side, near][n])
            still, moved = t[0, near][n], t[-side, far][n]
            row += [still[0] + moved[0], moved[0] if side == -1 else -moved[0]]
            row += [still[1] + moved[1], still[2] + moved[2]]
            row.append(solid_in[near] if n == 0 else incoming(halo[table["w", near][0]], table["w", near][1], 0))
            extra.append(row)
        columns = halo[0]
        if side in REDUCED:
            groups = {0: [], side: []}
            for q, x in edge_rows(rows, side)[FULL:]:
                a, b, c = Q[q]
                main, beyond = gathered(rows, x - a, q, cot, turned, lane)
                groups[a].append(main)
                i = table["v", q, x][1]
                columns = jnp.where(by_two == i // 2, turn(beyond, i + 1, 1), columns)
            part, coefficients = side_pull_back(groups, side, [scale_in[i] for i in range(27)])
            extra[0] += list(part) + list(coefficients)
        for k, value in enumerate(extra[0]):
            message[items + 6 * k:items + 6 * k + 6] = value[1:7]
        for k in range(8):
            i = used + 2 * k
            columns = jnp.where(by_two == i // 2, turn(extra[1][k], i + 1, 1), columns)
        message[at:at + 8] = columns


def outer_rows(rows):
    return [x for x in range(-1, rows + 1) if not 0 < x < rows - 1]


def gathered(rows, x, q, cot, turned, lane, remote=None):
    table, _ = slots(rows)
    a, b, c = Q[q]
    source = x + a
    if 0 <= source < rows:
        main = turn(cot[q, pl.ds(source, 8, stride=rows), :], -c, 0)
        group, i, kind = table["v", q, source]
    else:
        load, group, i, kind = remote[q, source]
        main = load()
    outer = incoming(turned[group, c], i, kind, b)
    return shift_y(main, outer, b, lane)


def middle_kernel(rows, scale_in, cot, sums, solid_in, sent, merged, inner, known, own):
    scale = [scale_in[i] for i in range(27)]
    lane = lanes()
    table, _ = slots(rows)
    halo = [merged[g] for g in range(3)]
    t = {key: [[sent[i, 2 * k + n] for k in range(3)] for n in range(2)] for i, key in enumerate(sent_sums(rows))}
    for a in SIGNS:
        for x in range(rows):
            if (a, x) not in t:
                t[a, x] = sums_over_y(a, x, sums, halo, table, lane)
    for x in range(-1, rows + 1):
        for n in range(2):
            terms = [(a, t[a, x - a][n]) for a in SIGNS if 0 <= x - a < rows]
            along_x = jnp.zeros((8, 128), F32)
            for a, v in terms:
                if a:
                    along_x = along_x + v[0] if a == 1 else along_x - v[0]
            moments_here = [functools.reduce(jnp.add, [v[k] for _, v in terms]) for k in range(3)]
            for k, v in enumerate([moments_here[0], along_x] + moments_here[1:]):
                own[k, 2 * (x + 1) + n] = v
    turned = {(g, c): turn(merged[g], -c, 0) for g in range(2) for c in SIGNS}
    for x in range(1, rows - 1):
        v = [gathered(rows, x, q, cot, turned, lane) for q in range(27)]
        for n in range(2):
            total = [own[k, 2 * (x + 1) + n] for k in range(4)]
            inverse = 1.0 / total[0]
            if n == 0:
                wall = solid_in[x]
            else:
                g, i, kind = table["w", x]
                wall = incoming(merged[g], i, kind)
            out = pull_back([t[n] for t in v], [t * inverse for t in total[1:]], wall > 0.5, scale)
            for q in range(27):
                inner[q, 2 * (x - 1) + n] = out[q]
    for j, x in enumerate(outer_rows(rows)):
        for q in range(27):
            if 0 <= x + Q[q][0] < rows:
                known[q, 2 * j], known[q, 2 * j + 1] = gathered(rows, x, q, cot, turned, lane)


def outer_gradient(rows, side, scale, solid_in, own, merged, known, raw, gap, extra, columns_at, items_at, g1):
    lane = lanes()
    table, used = slots(rows)
    remote = {}
    def load(k, c):
        at = raw_at(k, gap)
        return turn(raw[at:at + 8], -c, 0) if k < FULL else planes(raw, at)

    for k, (q, x) in enumerate(edge_rows(rows, side)[:raw_count(side)]):
        _, i, kind = table["v", q, x]
        remote[q, x + side * rows] = (functools.partial(load, k, Q[q][2]), "far", i, kind)
    columns = extra[columns_at:columns_at + 8]
    turned = {("far", c): turn(columns, -c, 0) for c in SIGNS}
    plane = lax.broadcasted_iota(jnp.int32, (8, 128), 0)
    boundary = (plane == 0) | (plane == 7)
    near = rows - 1 if side == 1 else 0
    for j, x in enumerate(outer_rows(rows)):
        if x not in (near, near + side):
            continue
        v = []
        for q, (a, b, c) in enumerate(Q):
            if 0 <= x + a < rows:
                v.append((known[q, 2 * j], known[q, 2 * j + 1]))
            elif x == near or side not in REDUCED:
                v.append(gathered(rows, x, q, None, turned, lane, remote))
            else:
                v.append((None, incoming(columns, table["v", q, x + a - side * rows][1], 0)))
        for n in range(2):
            def got(k):
                return planes(extra, items_at + 6 * k) if n == 0 else incoming(columns, used + 2 * k, 0)

            total = [own[k, 2 * (x + 1) + n] for k in range(4)]
            if x == near:
                total = [total[0] + got(0), total[1] - got(0) if side == 1 else total[1] + got(0),
                         total[2] + got(1), total[3] + got(2)]
                if n == 0:
                    wall = solid_in[x]
                else:
                    g, i, kind = table["w", x]
                    wall = incoming(merged[g], i, kind)
            else:
                total = [total[k] + got(3 + k) for k in range(4)]
                wall = got(7)
            inverse = 1.0 / total[0]
            u = [t * inverse for t in total[1:]]
            solid = boundary | (wall > 0.5)
            if x != near and n == 0 and side in REDUCED:
                mine = [t[0] for t in v[9 * (1 - side):9 * (1 - side) + 9]]
                part, coefficients = side_pull_back({-side: mine}, side, scale)
                p_x, p_y, p_z, quad = form([m + got(17 + k) for k, m in enumerate(coefficients)], u)
                start = (p_x if side == 1 else -p_x) - quad
                along_y = {-1: start - p_y, 0: start, 1: start + p_y}
                for i in range(9):
                    b, c = i // 3 - 1, i % 3 - 1
                    rest = along_y[b] + p_z if c == 1 else along_y[b] - p_z if c == -1 else along_y[b]
                    value = (part[i] + got(8 + i)) + rest
                    g1[9 * (1 + side) + i, 2 * (j % 2)] = jnp.where(solid, mine[8 - i], value)
                continue
            g = pull_back([t[n] for t in v], u, solid, scale)
            for q in range(27):
                if 0 <= x - Q[q][0] < rows:
                    g1[q, 2 * (j % 2) + n] = g[q]


def pulled(rows, x, q, arrays, lane):
    a, b, c = Q[q]
    array, r = arrays(x + a)
    main = array[q, r]
    if b:
        main = shift_y(main, turn(array[q, r + 1], -b, 1), b, lane)[0]
    return turn(main, -c, 0)


def early_keys(rows):
    return [(q, x) for x in range(rows - 2, rows) for q in range(27) if 0 < x + Q[q][0] < rows - 1]


def low_kernel(rows, scale_in, speed, solid_in, own, merged, inner, known, raw, extra, done, ready, g1):
    scale = [scale_in[i] for i in range(27)]
    lane = lanes()
    outer_gradient(rows, -1, scale, solid_in, own, merged, known, raw, 0, extra, 0, 8, g1)

    def arrays(x):
        return (g1, 2 * (x + 1)) if x < 1 else (inner, 2 * (x - 1))

    for x in range(rows - 2):
        v = [pulled(rows, x, q, arrays, lane) for q in range(27)]
        for q, value in enumerate(pull_back(v, [speed[k, x] for k in range(3)], solid_in[x] > 0.5, scale)):
            done[q, x] = value
    for i, (q, x) in enumerate(early_keys(rows)):
        ready[i] = pulled(rows, x, q, arrays, lane)


def last_kernel(rows, scale_in, speed, solid_in, own, merged, known, done, ready, from_high, out_hbm, high, out, sems):
    scale = [scale_in[i] for i in range(27)]
    lane = lanes()
    outer_gradient(rows, 1, scale, solid_in, own, merged, known, from_high, 8, from_high, 8 * FULL, raw_height(1) + 8, high)

    def arrays(x):
        return high, 2 * (x - rows + 1)

    keys = early_keys(rows)
    late = {}
    for x in range(rows - 2, rows):
        v = [ready[keys.index((q, x))] if (q, x) in keys else pulled(rows, x, q, arrays, lane) for q in range(27)]
        late[x] = pull_back_parts(v, [speed[k, x] for k in range(3)], solid_in[x] > 0.5, scale)
    copies = []
    for a in range(3):
        for x in range(rows):
            part = next(late[x]) if x in late else [done[9 * a + i, x] for i in range(9)]
            for i, value in enumerate(part):
                out[9 * a + i, pl.ds(x, 8, stride=rows), :] = value
        part = pl.ds(9 * a, 9)
        copies.append(pltpu.make_async_copy(out.at[part], out_hbm.at[part], sems.at[a]))
        copies[a].start()
    for copy in copies:
        copy.wait()


def call(kernel, name, out_shapes, scratch, operands, space=pltpu.VMEM, work=0, out_space=pltpu.VMEM):
    return pl.pallas_call(
        kernel,
        out_shape=[jax.ShapeDtypeStruct(s, F32) for s in out_shapes],
        in_specs=[pl.BlockSpec(memory_space=space)] * len(operands),
        out_specs=[pl.BlockSpec(memory_space=out_space)] * len(out_shapes),
        scratch_shapes=scratch,
        compiler_params=pltpu.CompilerParams(vmem_limit_bytes=32 * 1024 * 1024),
        cost_estimate=pl.CostEstimate(flops=work, bytes_accessed=0 if work else 0, transcendentals=0) if work else None,
        name=name,
    )(*operands)


def ring(block, axis, step):
    size = lax.axis_size(axis)
    return lax.ppermute(block, axis, [(i, (i + step) % size) for i in range(size)])


def swap(block, axis, first):
    size = lax.axis_size(axis)
    route = []
    for i in range(first, size + first, 2):
        route += [(i % size, (i + 1) % size), ((i + 1) % size, i % size)]
    return lax.ppermute(block, axis, route)


def shards(checkpoint, rates, wall_mask, cotangent):
    planes, rows, width = checkpoint.shape[1:]
    f = checkpoint.reshape(27, planes * rows, width)
    cot = cotangent.reshape(27, planes * rows, width)
    wall = wall_mask.reshape(planes * rows, width)
    tile = (planes, width)
    lattice = (27, planes * rows, width)
    cot, scale, sums, speed, solid, packed, raw_right = call(
        functools.partial(first_kernel, rows), "collide",
        [lattice, (27,) + tile, (18, rows) + tile, (3, rows) + tile, (rows,) + tile, (3,) + tile,
         (padded(raw_height(-1)), width)],
        [pltpu.SMEM((27,), F32), pltpu.VMEM(lattice, F32), pltpu.VMEM(lattice[1:], jnp.int32),
         pltpu.SemaphoreType.DMA((4,))],
        tuple(pltpu.with_memory_space_constraint(v, pltpu.HBM) for v in (rates, f, wall, cot)), pltpu.HBM)
    raw_low = ring(raw_right, "gx", 1)
    across, inside = swap(packed, "gy", 1), swap(packed, "gy", 0)
    odd = lax.axis_index("gy") % 2 == 1
    from_left = jnp.where(odd, inside, across)
    from_right = jnp.where(odd, across, inside)
    to_left, small_right, sent, merged = call(
        functools.partial(second_kernel, rows), "pack",
        [(padded(raw_height(1) + small_height(1)), width), (padded(small_height(-1)), width), (6, 6) + tile, (3,) + tile], [],
        (scale, cot, sums, solid, from_left, from_right))
    small_low = ring(small_right, "gx", 1)
    from_high = ring(to_left, "gx", -1)
    inner, known, own = call(
        functools.partial(middle_kernel, rows), "inner_rows",
        [(27, 2 * rows - 4) + tile, (27, 8) + tile, (4, 2 * rows + 4) + tile], [],
        (scale, cot, sums, solid, sent, merged))
    done, ready = call(
        functools.partial(low_kernel, rows), "low_rows",
        [(27, rows - 2) + tile, (len(early_keys(rows)),) + tile], [pltpu.VMEM((27, 4) + tile, F32)],
        (scale, speed, solid, own, merged, inner, known, raw_low, small_low), work=2000000000)
    (out,) = call(
        functools.partial(last_kernel, rows), "gradient",
        [lattice],
        [pltpu.VMEM((27, 4) + tile, F32), pltpu.VMEM(lattice, F32), pltpu.SemaphoreType.DMA((3,))],
        (scale, speed, solid, own, merged, known, done, ready, from_high), out_space=pltpu.HBM)
    return out.reshape(checkpoint.shape)


def solution(mesh):
    in_specs = (P(None, None, "gx", "gy"), P(), P(None, "gx", "gy"), P(None, None, "gx", "gy"))
    out_specs = P(None, None, "gx", "gy")
    return jax.shard_map(shards, mesh=mesh, in_specs=in_specs, out_specs=out_specs, check_vma=False)
```

```python
import functools
import jax
import jax.numpy as jnp
from jax import lax
from jax.experimental import pallas as pl
from jax.experimental.pallas import tpu as pltpu
from jax.sharding import PartitionSpec as P

F32 = jnp.float32
SIGNS = (-1, 0, 1)
Q = [(a, b, c) for a in SIGNS for b in SIGNS for c in SIGNS]


def qi(a, b, c):
    return 9 * (a + 1) + 3 * (b + 1) + (c + 1)


def mi(i, j, k):
    return 9 * i + 3 * j + k


NNZ = [(i > 0) + (j > 0) + (k > 0) for i in range(3) for j in range(3) for k in range(3)]


def layout(rows):
    quads, singles = [[], [], []], [[], [], []]
    for a in SIGNS:
        for c in SIGNS:
            for x in range(rows):
                left = (a >= 0 and x == 0) or (a == 1 and x == 1)
                right = (a <= 0 and x == rows - 1) or (a == -1 and x == rows - 2)
                g = 0 if left or right else 1
                quads[g].append((("v", qi(a, -1, c), x), ("v", qi(a, 1, c), x)))
                singles[g].append(("v", qi(a, 0, c), x))
    used = 4 * len(quads[0]) + 2 * len(singles[0])
    singles[1] += [("w", x) for x in range(rows)]
    for a in SIGNS:
        for s in range(2):
            for x in range(rows):
                quads[2].append((("s", a, 1, s, x), ("s", a, -1, s, x)))
                singles[2].append(("s", a, 0, s, x))
    room = 64 - 2 * len(quads[2])
    singles[0] += singles[2][room:]
    singles[2] = singles[2][:room]
    return quads, singles, used


def slots(rows):
    quads, singles, used = layout(rows)
    table = {}
    for g in range(3):
        for n, (low, high) in enumerate(quads[g]):
            table[low], table[high] = (g, 4 * n, -1), (g, 4 * n + 2, 1)
        for n, key in enumerate(singles[g]):
            table[key] = (g, 4 * len(quads[g]) + 2 * n, 0)
    return table, used


def turn(v, shift, axis):
    shift = shift % v.shape[axis]
    return v if shift == 0 else pltpu.roll(v, shift, axis)


def lanes():
    return lax.broadcasted_iota(jnp.int32, (8, 128), 1)


def incoming(packed, lane, kind, b=0):
    return turn(packed, {0: 127, 1: 0, -1: 126}[kind] - lane - b, 1)


def shift_y(main, rolled_outer, b, lane):
    if b == 0:
        return main, rolled_outer
    edge = lane == (127 if b == 1 else 0)
    rolled = turn(main, -b, 1)
    return jnp.where(edge, rolled_outer, rolled), jnp.where(edge, rolled, rolled_outer)


def along(values, pass_, steps=(1, 3, 9)):
    values = list(values)
    for step in steps:
        for start in range(len(values)):
            if (start // step) % 3 == 0:
                at = (start, start + step, start + 2 * step)
                for i, new in zip(at, pass_(*[values[j] for j in at])):
                    values[i] = new
    return values


def moments(values):
    def pass_(lo, mid, hi):
        both = lo + hi
        return both + mid, hi - lo, both
    return along(values, pass_)


def dual_moments(values):
    return along(values, lambda lo, mid, hi: (mid, hi - lo, (hi - mid) + (lo - mid)))


def from_moments(values):
    return along(values, lambda m0, m1, m2: (m2 - m1, m0 - (m2 + m2), m2 + m1))


def dual_back(z0, z1, z2):
    both = z0 + z2
    return both - z1, z0, both + z1


def collide(f, solid, scale):
    m = moments(f)
    rho = m[0]
    inverse = 1.0 / rho
    jx, jy, jz = m[mi(1, 0, 0)], m[mi(0, 1, 0)], m[mi(0, 0, 1)]
    ux, uy, uz = jx * inverse, jy * inverse, jz * inverse
    xx, yy, zz = jx * ux, jy * uy, jz * uz
    third = rho * (1.0 / 3.0)
    ninth = rho * (1.0 / 9.0)
    e = [None] * 27
    e[mi(2, 0, 0)], e[mi(0, 2, 0)], e[mi(0, 0, 2)] = third + xx, third + yy, third + zz
    e[mi(1, 1, 0)], e[mi(1, 0, 1)], e[mi(0, 1, 1)] = jx * uy, jx * uz, jy * uz
    jx3, jy3, jz3 = jx * (1.0 / 3.0), jy * (1.0 / 3.0), jz * (1.0 / 3.0)
    e[mi(1, 2, 0)] = e[mi(1, 0, 2)] = jx3
    e[mi(2, 1, 0)] = e[mi(0, 1, 2)] = jy3
    e[mi(2, 0, 1)] = e[mi(0, 2, 1)] = jz3
    e[mi(2, 2, 0)] = ninth + (xx + yy) * (1.0 / 3.0)
    e[mi(2, 0, 2)] = ninth + (xx + zz) * (1.0 / 3.0)
    e[mi(0, 2, 2)] = ninth + (yy + zz) * (1.0 / 3.0)
    e[mi(2, 1, 1)] = e[mi(0, 1, 1)] * (1.0 / 3.0)
    e[mi(1, 2, 1)] = e[mi(1, 0, 1)] * (1.0 / 3.0)
    e[mi(1, 1, 2)] = e[mi(1, 1, 0)] * (1.0 / 3.0)
    e[mi(1, 2, 2)], e[mi(2, 1, 2)], e[mi(2, 2, 1)] = jx * (1.0 / 9.0), jy * (1.0 / 9.0), jz * (1.0 / 9.0)
    e[mi(2, 2, 2)] = (third + (xx + yy + zz)) * (1.0 / 9.0)
    z = []
    for i in range(27):
        if i in (0, 1, 3, 9):
            z.append(jnp.zeros_like(rho))
        else:
            z.append((m[i] if e[i] is None else m[i] - e[i]) * scale[i])
    h = from_moments(z)
    out = [jnp.where(solid, f[26 - q], f[q] - h[q]) for q in range(27)]
    return out, (ux, uy, uz)


def low_rank(z):
    def at(i, j, k):
        return z[mi(i, j, k)]

    third = 1.0 / 3.0
    top = at(2, 2, 2) * third
    d_xy, d_xz, d_yz = at(2, 2, 0) + top, at(2, 0, 2) + top, at(0, 2, 2) + top
    q_xx = at(2, 0, 0) + (at(2, 2, 0) + d_xz) * third
    q_yy = at(0, 2, 0) + (at(0, 2, 2) + d_xy) * third
    q_zz = at(0, 0, 2) + (at(2, 0, 2) + d_yz) * third
    base = at(0, 0, 0) + (q_xx + (at(0, 2, 0) + at(0, 0, 2) + at(0, 2, 2) * third)) * third
    b_x = at(1, 0, 0) + (at(1, 2, 0) + at(1, 0, 2) + at(1, 2, 2) * third) * third
    b_y = at(0, 1, 0) + (at(2, 1, 0) + at(0, 1, 2) + at(2, 1, 2) * third) * third
    b_z = at(0, 0, 1) + (at(2, 0, 1) + at(0, 2, 1) + at(2, 2, 1) * third) * third
    q_xy = at(1, 1, 0) + at(1, 1, 2) * third
    q_xz = at(1, 0, 1) + at(1, 2, 1) * third
    q_yz = at(0, 1, 1) + at(2, 1, 1) * third
    return base, (b_x, b_y, b_z), (q_xx, q_yy, q_zz, q_xy, q_xz, q_yz)


def form(coefficients, u):
    q_xx, q_yy, q_zz, q_xy, q_xz, q_yz = coefficients
    ux, uy, uz = u
    p_x = (q_xx + q_xx) * ux + q_xy * uy + q_xz * uz
    p_y = q_xy * ux + (q_yy + q_yy) * uy + q_yz * uz
    p_z = q_xz * ux + q_yz * uy + (q_zz + q_zz) * uz
    return p_x, p_y, p_z, (p_x * ux + p_y * uy + p_z * uz) * 0.5


def pull_back_parts(v, u, solid, scale):
    z = [y * s for y, s in zip(dual_moments(v), scale)]
    base, (b_x, b_y, b_z), coefficients = low_rank(z)
    p_x, p_y, p_z, quad = form(coefficients, u)
    z[0] = z[0] - (base - quad)
    z[mi(1, 0, 0)] = z[mi(1, 0, 0)] - (b_x + p_x)
    z[mi(0, 1, 0)] = z[mi(0, 1, 0)] - (b_y + p_y)
    z[mi(0, 0, 1)] = z[mi(0, 0, 1)] - (b_z + p_z)
    h = along(z, dual_back, (9, 3))
    for a in range(3):
        part = along(h[9 * a:9 * a + 9], dual_back, (1,))
        yield [jnp.where(solid, v[26 - q], v[q] - part[q - 9 * a]) for q in range(9 * a, 9 * a + 9)]


def pull_back(v, u, solid, scale):
    return sum(pull_back_parts(v, u, solid, scale), [])


def side_pull_back(groups, side, scale):
    def pass_(lo, mid, hi):
        return mid, hi - lo, (hi - mid) + (lo - mid)

    t = {a: along(values, pass_, (1, 3)) for a, values in groups.items()}
    if side in t:
        still, moved = t[0], t[side]
        first = moved if side == 1 else [-v for v in moved]
        second = [(v - m) - m for v, m in zip(moved, still)]
    else:
        moved = t[-side]
        still = [jnp.zeros_like(v) for v in moved]
        first = moved if side == -1 else [-v for v in moved]
        second = moved
    z = [y * s for y, s in zip(list(still) + list(first) + list(second), scale)]
    base, (b_x, b_y, b_z), coefficients = low_rank(z)
    z[0] = z[0] - base
    z[mi(1, 0, 0)] = z[mi(1, 0, 0)] - b_x
    z[mi(0, 1, 0)] = z[mi(0, 1, 0)] - b_y
    z[mi(0, 0, 1)] = z[mi(0, 0, 1)] - b_z
    h = [(z[i] + z[18 + i]) + z[9 + i] if side == 1 else (z[i] + z[18 + i]) - z[9 + i] for i in range(9)]
    h = along(h, dual_back, (1, 3))
    if side in groups:
        return [v - w for v, w in zip(groups[side], h)], coefficients
    return [-w for w in h], coefficients


def first_kernel(rows, rates_in, f_in, wall_in, cot_in, cot, scale_out, sums, speed, solid_out, packed,
                 raw_right,
                 rates, f, wall, sems):
    pairs = ((f_in, f), (rates_in, rates), (wall_in, wall), (cot_in, cot))
    copies = [pltpu.make_async_copy(source, target, sems.at[i]) for i, (source, target) in enumerate(pairs)]
    for copy in copies:
        copy.start()
    for copy in copies[:3]:
        copy.wait()
    for i in range(27):
        scale_out[i] = jnp.full((8, 128), rates[i] * (0.5 ** NNZ[i]), F32)
    scale = [rates[i] * (0.5 ** NNZ[i]) for i in range(27)]
    plane = lax.broadcasted_iota(jnp.int32, (8, 128), 0)
    boundary = (plane == 0) | (plane == 7)
    lane = lanes()
    table, _ = slots(rows)
    for x in range(rows):
        at = pl.ds(x, 8, stride=rows)
        solid = boundary | (wall[at, :] == 1)
        solid_out[x] = jnp.where(solid, 1.0, 0.0)
        out, u = collide([f[q, at, :] for q in range(27)], solid, scale)
        for k in range(3):
            speed[k, x] = u[k]
        for a in SIGNS:
            for b in SIGNS:
                low = turn(out[qi(a, b, -1)], -1, 0)
                high = turn(out[qi(a, b, 1)], 1, 0)
                i = 2 * (3 * (a + 1) + b + 1)
                sums[i, x] = out[qi(a, b, 0)] + (low + high)
                sums[i + 1, x] = high - low
    for copy in copies[3:]:
        copy.wait()
    raw_rows(rows, -1, cot, raw_right, 0)
    clear_end(raw_right, raw_height(-1))
    def block(key):
        if key[0] == "v":
            return cot[key[1], pl.ds(key[2], 8, stride=rows), :]
        if key[0] == "w":
            return solid_out[key[1]]
        return sums[2 * (3 * (key[1] + 1) + key[2] + 1) + key[3], key[4]]

    quads, singles, _ = layout(rows)
    by_two, by_four = lane >> 1, lane >> 2
    high_lanes = lane >= 64
    for g in range(3):
        piece = jnp.zeros((8, 128), F32)
        for n, (low, high) in enumerate(quads[g]):
            both = jnp.where(high_lanes, block(low), block(high))
            piece = jnp.where(by_four == n, turn(both, 4 * n + 2, 1), piece)
        for n, key in enumerate(singles[g]):
            i = 4 * len(quads[g]) + 2 * n
            piece = jnp.where(by_two == i // 2, turn(block(key), i + 1, 1), piece)
        packed[g] = piece


FULL = 9


def edge_rows(rows, side):
    near, far = (0, 1) if side == 1 else (rows - 1, rows - 2)
    keys = [(q, near) for q, c in enumerate(Q) if c[0] == side]
    keys += [(q, near) for q, c in enumerate(Q) if c[0] == 0]
    return keys + [(q, far) for q, c in enumerate(Q) if c[0] == side]


REDUCED = (-1,)


def raw_count(side):
    return FULL if side in REDUCED else 27


def raw_at(k, gap):
    return 8 * k if k < FULL else 8 * FULL + gap + 6 * (k - FULL)


def raw_height(side):
    return raw_at(raw_count(side), 0)


def small_height(side):
    return 8 + 6 * (23 if side in REDUCED else 8)


def padded(count):
    return (count + 7) // 8 * 8


def raw_rows(rows, side, cot, message, gap):
    for k, (q, x) in enumerate(edge_rows(rows, side)[:raw_count(side)]):
        at = raw_at(k, gap)
        if k < FULL:
            message[at:at + 8] = cot[q, pl.ds(x, 8, stride=rows), :]
        else:
            message[at:at + 6] = cot[q, pl.ds(x + rows * (1 + Q[q][2]), 6, stride=rows), :]


def clear_end(message, count):
    if message.shape[0] > count:
        message[count:] = jnp.zeros((message.shape[0] - count, 128), F32)


def planes(ref, at):
    start = min(at - 1, ref.shape[0] - 8)
    return turn(ref[start:start + 8], 1 - (at - start), 0)


def sent_sums(rows):
    return [(-1, 0), (-1, 1), (0, 0), (0, rows - 1), (1, rows - 1), (1, rows - 2)]


def sums_over_y(a, x, sums, halo, table, lane):
    parts = {}
    for b in SIGNS:
        for s in range(2):
            i = 2 * (3 * (a + 1) + b + 1) + s
            g, at, kind = table["s", a, b, s, x]
            parts[b, s] = shift_y(sums[i, x], incoming(halo[g], at, kind, -b), -b, lane)
    return [(
        parts[0, 0][n] + (parts[-1, 0][n] + parts[1, 0][n]),
        parts[1, 0][n] - parts[-1, 0][n],
        parts[0, 1][n] + (parts[-1, 1][n] + parts[1, 1][n]),
    ) for n in range(2)]


def second_kernel(rows, scale_in, cot, sums, solid_in, from_left, from_right, to_left, to_right, sent, merged):
    lane = lanes()
    table, used = slots(rows)
    by_two = lane >> 1
    halo = []
    for g in range(3):
        end = 4 * len(layout(rows)[0][g])
        takes_left = ((lane < end) & ((lane & 2) == 0)) | ((lane >= end) & ((lane & 1) == 0))
        halo.append(jnp.where(takes_left, from_left[g], from_right[g]))
        merged[g] = halo[g]

    t = {}
    for i, (a, x) in enumerate(sent_sums(rows)):
        t[a, x] = sums_over_y(a, x, sums, halo, table, lane)
        for n in range(2):
            for k in range(3):
                sent[i, 2 * k + n] = t[a, x][n][k]
    turned = {(g, c): turn(halo[g], -c, 0) for g in range(2) for c in SIGNS}
    for side, message in ((1, to_left), (-1, to_right)):
        near, far = (0, 1) if side == 1 else (rows - 1, rows - 2)
        with_raw = side == 1
        at = 8 * FULL if with_raw else 0
        items = raw_height(side) + 8 if with_raw else 8
        if with_raw:
            raw_rows(rows, side, cot, message, 8)
        clear_end(message, (raw_height(side) if with_raw else 0) + small_height(side))
        extra = []
        for n in range(2):
            row = list(t[-side, near][n])
            still, moved = t[0, near][n], t[-side, far][n]
            row += [still[0] + moved[0], moved[0] if side == -1 else -moved[0]]
            row += [still[1] + moved[1], still[2] + moved[2]]
            row.append(solid_in[near] if n == 0 else incoming(halo[table["w", near][0]], table["w", near][1], 0))
            extra.append(row)
        columns = halo[0]
        if side in REDUCED:
            groups = {0: [], side: []}
            for q, x in edge_rows(rows, side)[FULL:]:
                a, b, c = Q[q]
                main, beyond = gathered(rows, x - a, q, cot, turned, lane)
                groups[a].append(main)
                i = table["v", q, x][1]
                columns = jnp.where(by_two == i // 2, turn(beyond, i + 1, 1), columns)
            part, coefficients = side_pull_back(groups, side, [scale_in[i] for i in range(27)])
            extra[0] += list(part) + list(coefficients)
        for k, value in enumerate(extra[0]):
            message[items + 6 * k:items + 6 * k + 6] = value[1:7]
        for k in range(8):
            i = used + 2 * k
            columns = jnp.where(by_two == i // 2, turn(extra[1][k], i + 1, 1), columns)
        message[at:at + 8] = columns


def outer_rows(rows):
    return [x for x in range(-1, rows + 1) if not 0 < x < rows - 1]


def gathered(rows, x, q, cot, turned, lane, remote=None):
    table, _ = slots(rows)
    a, b, c = Q[q]
    source = x + a
    if 0 <= source < rows:
        main = turn(cot[q, pl.ds(source, 8, stride=rows), :], -c, 0)
        group, i, kind = table["v", q, source]
    else:
        load, group, i, kind = remote[q, source]
        main = load()
    outer = incoming(turned[group, c], i, kind, b)
    return shift_y(main, outer, b, lane)


def middle_kernel(rows, scale_in, cot, sums, solid_in, sent, merged, inner, known, own):
    scale = [scale_in[i] for i in range(27)]
    lane = lanes()
    table, _ = slots(rows)
    halo = [merged[g] for g in range(3)]
    t = {key: [[sent[i, 2 * k + n] for k in range(3)] for n in range(2)] for i, key in enumerate(sent_sums(rows))}
    for a in SIGNS:
        for x in range(rows):
            if (a, x) not in t:
                t[a, x] = sums_over_y(a, x, sums, halo, table, lane)
    for x in range(-1, rows + 1):
        for n in range(2):
            terms = [(a, t[a, x - a][n]) for a in SIGNS if 0 <= x - a < rows]
            along_x = jnp.zeros((8, 128), F32)
            for a, v in terms:
                if a:
                    along_x = along_x + v[0] if a == 1 else along_x - v[0]
            moments_here = [functools.reduce(jnp.add, [v[k] for _, v in terms]) for k in range(3)]
            for k, v in enumerate([moments_here[0], along_x] + moments_here[1:]):
                own[k, 2 * (x + 1) + n] = v
    turned = {(g, c): turn(merged[g], -c, 0) for g in range(2) for c in SIGNS}
    for x in range(1, rows - 1):
        v = [gathered(rows, x, q, cot, turned, lane) for q in range(27)]
        for n in range(2):
            total = [own[k, 2 * (x + 1) + n] for k in range(4)]
            inverse = 1.0 / total[0]
            if n == 0:
                wall = solid_in[x]
            else:
                g, i, kind = table["w", x]
                wall = incoming(merged[g], i, kind)
            out = pull_back([t[n] for t in v], [t * inverse for t in total[1:]], wall > 0.5, scale)
            for q in range(27):
                inner[q, 2 * (x - 1) + n] = out[q]
    for j, x in enumerate(outer_rows(rows)):
        for q in range(27):
            if 0 <= x + Q[q][0] < rows:
                known[q, 2 * j], known[q, 2 * j + 1] = gathered(rows, x, q, cot, turned, lane)


def outer_gradient(rows, side, scale, solid_in, own, merged, known, raw, gap, extra, columns_at, items_at, g1):
    lane = lanes()
    table, used = slots(rows)
    remote = {}
    def load(k, c):
        at = raw_at(k, gap)
        return turn(raw[at:at + 8], -c, 0) if k < FULL else planes(raw, at)

    for k, (q, x) in enumerate(edge_rows(rows, side)[:raw_count(side)]):
        _, i, kind = table["v", q, x]
        remote[q, x + side * rows] = (functools.partial(load, k, Q[q][2]), "far", i, kind)
    columns = extra[columns_at:columns_at + 8]
    turned = {("far", c): turn(columns, -c, 0) for c in SIGNS}
    plane = lax.broadcasted_iota(jnp.int32, (8, 128), 0)
    boundary = (plane == 0) | (plane == 7)
    near = rows - 1 if side == 1 else 0
    for j, x in enumerate(outer_rows(rows)):
        if x not in (near, near + side):
            continue
        v = []
        for q, (a, b, c) in enumerate(Q):
            if 0 <= x + a < rows:
                v.append((known[q, 2 * j], known[q, 2 * j + 1]))
            elif x == near or side not in REDUCED:
                v.append(gathered(rows, x, q, None, turned, lane, remote))
            else:
                v.append((None, incoming(columns, table["v", q, x + a - side * rows][1], 0)))
        for n in range(2):
            def got(k):
                return planes(extra, items_at + 6 * k) if n == 0 else incoming(columns, used + 2 * k, 0)

            total = [own[k, 2 * (x + 1) + n] for k in range(4)]
            if x == near:
                total = [total[0] + got(0), total[1] - got(0) if side == 1 else total[1] + got(0),
                         total[2] + got(1), total[3] + got(2)]
                if n == 0:
                    wall = solid_in[x]
                else:
                    g, i, kind = table["w", x]
                    wall = incoming(merged[g], i, kind)
            else:
                total = [total[k] + got(3 + k) for k in range(4)]
                wall = got(7)
            inverse = 1.0 / total[0]
            u = [t * inverse for t in total[1:]]
            solid = boundary | (wall > 0.5)
            if x != near and n == 0 and side in REDUCED:
                mine = [t[0] for t in v[9 * (1 - side):9 * (1 - side) + 9]]
                part, coefficients = side_pull_back({-side: mine}, side, scale)
                p_x, p_y, p_z, quad = form([m + got(17 + k) for k, m in enumerate(coefficients)], u)
                start = (p_x if side == 1 else -p_x) - quad
                along_y = {-1: start - p_y, 0: start, 1: start + p_y}
                for i in range(9):
                    b, c = i // 3 - 1, i % 3 - 1
                    rest = along_y[b] + p_z if c == 1 else along_y[b] - p_z if c == -1 else along_y[b]
                    value = (part[i] + got(8 + i)) + rest
                    g1[9 * (1 + side) + i, 2 * (j % 2)] = jnp.where(solid, mine[8 - i], value)
                continue
            g = pull_back([t[n] for t in v], u, solid, scale)
            for q in range(27):
                if 0 <= x - Q[q][0] < rows:
                    g1[q, 2 * (j % 2) + n] = g[q]


def pulled_row(rows, x, arrays, speed, solid_in, scale, lane):
    v = []
    for q, (a, b, c) in enumerate(Q):
        array, r = arrays(x + a)
        main = array[q, r]
        if b:
            main = shift_y(main, turn(array[q, r + 1], -b, 1), b, lane)[0]
        v.append(turn(main, -c, 0))
    return pull_back_parts(v, [speed[k, x] for k in range(3)], solid_in[x] > 0.5, scale)


def low_kernel(rows, scale_in, speed, solid_in, own, merged, inner, known, raw, extra, done, g1):
    scale = [scale_in[i] for i in range(27)]
    lane = lanes()
    outer_gradient(rows, -1, scale, solid_in, own, merged, known, raw, 0, extra, 0, 8, g1)

    def arrays(x):
        return (g1, 2 * (x + 1)) if x < 1 else (inner, 2 * (x - 1))

    for x in range(rows - 2):
        for a, part in enumerate(pulled_row(rows, x, arrays, speed, solid_in, scale, lane)):
            for i, value in enumerate(part):
                done[9 * a + i, x] = value


def last_kernel(rows, scale_in, speed, solid_in, own, merged, inner, known, done, from_high, out_hbm, high, out, sems):
    scale = [scale_in[i] for i in range(27)]
    lane = lanes()
    outer_gradient(rows, 1, scale, solid_in, own, merged, known, from_high, 8, from_high, 8 * FULL, raw_height(1) + 8, high)

    def arrays(x):
        return (inner, 2 * (x - 1)) if x < rows - 1 else (high, 2 * (x - rows + 1))

    late = {x: pulled_row(rows, x, arrays, speed, solid_in, scale, lane) for x in range(rows - 2, rows)}
    copies = []
    for a in range(3):
        for x in range(rows):
            part = next(late[x]) if x in late else [done[9 * a + i, x] for i in range(9)]
            for i, value in enumerate(part):
                out[9 * a + i, pl.ds(x, 8, stride=rows), :] = value
        part = pl.ds(9 * a, 9)
        copies.append(pltpu.make_async_copy(out.at[part], out_hbm.at[part], sems.at[a]))
        copies[a].start()
    for copy in copies:
        copy.wait()


def call(kernel, name, out_shapes, scratch, operands, space=pltpu.VMEM, work=0, out_space=pltpu.VMEM):
    return pl.pallas_call(
        kernel,
        out_shape=[jax.ShapeDtypeStruct(s, F32) for s in out_shapes],
        in_specs=[pl.BlockSpec(memory_space=space)] * len(operands),
        out_specs=[pl.BlockSpec(memory_space=out_space)] * len(out_shapes),
        scratch_shapes=scratch,
        compiler_params=pltpu.CompilerParams(vmem_limit_bytes=32 * 1024 * 1024),
        cost_estimate=pl.CostEstimate(flops=work, bytes_accessed=0 if work else 0, transcendentals=0) if work else None,
        name=name,
    )(*operands)


def ring(block, axis, step):
    size = lax.axis_size(axis)
    return lax.ppermute(block, axis, [(i, (i + step) % size) for i in range(size)])


def swap(block, axis, first):
    size = lax.axis_size(axis)
    route = []
    for i in range(first, size + first, 2):
        route += [(i % size, (i + 1) % size), ((i + 1) % size, i % size)]
    return lax.ppermute(block, axis, route)


def shards(checkpoint, rates, wall_mask, cotangent):
    planes, rows, width = checkpoint.shape[1:]
    f = checkpoint.reshape(27, planes * rows, width)
    cot = cotangent.reshape(27, planes * rows, width)
    wall = wall_mask.reshape(planes * rows, width)
    tile = (planes, width)
    lattice = (27, planes * rows, width)
    cot, scale, sums, speed, solid, packed, raw_right = call(
        functools.partial(first_kernel, rows), "collide",
        [lattice, (27,) + tile, (18, rows) + tile, (3, rows) + tile, (rows,) + tile, (3,) + tile,
         (padded(raw_height(-1)), width)],
        [pltpu.SMEM((27,), F32), pltpu.VMEM(lattice, F32), pltpu.VMEM(lattice[1:], jnp.int32),
         pltpu.SemaphoreType.DMA((4,))],
        tuple(pltpu.with_memory_space_constraint(v, pltpu.HBM) for v in (rates, f, wall, cot)), pltpu.HBM)
    raw_low = ring(raw_right, "gx", 1)
    across, inside = swap(packed, "gy", 1), swap(packed, "gy", 0)
    odd = lax.axis_index("gy") % 2 == 1
    from_left = jnp.where(odd, inside, across)
    from_right = jnp.where(odd, across, inside)
    to_left, small_right, sent, merged = call(
        functools.partial(second_kernel, rows), "pack",
        [(padded(raw_height(1) + small_height(1)), width), (padded(small_height(-1)), width), (6, 6) + tile, (3,) + tile], [],
        (scale, cot, sums, solid, from_left, from_right))
    small_low = ring(small_right, "gx", 1)
    from_high = ring(to_left, "gx", -1)
    inner, known, own = call(
        functools.partial(middle_kernel, rows), "inner_rows",
        [(27, 2 * rows - 4) + tile, (27, 8) + tile, (4, 2 * rows + 4) + tile], [],
        (scale, cot, sums, solid, sent, merged))
    def hold(source, target):
        target[...] = source[...]

    (raw_low,) = call(hold, "hold", [(padded(raw_height(-1)), width)], [], (raw_low,), work=1000000000)
    (done,) = call(
        functools.partial(low_kernel, rows), "low_rows",
        [(27, rows - 2) + tile], [pltpu.VMEM((27, 4) + tile, F32)],
        (scale, speed, solid, own, merged, inner, known, raw_low, small_low), work=2000000000)
    (out,) = call(
        functools.partial(last_kernel, rows), "gradient",
        [lattice],
        [pltpu.VMEM((27, 4) + tile, F32), pltpu.VMEM(lattice, F32), pltpu.SemaphoreType.DMA((3,))],
        (scale, speed, solid, own, merged, inner, known, done, from_high), out_space=pltpu.HBM)
    return out.reshape(checkpoint.shape)


def solution(mesh):
    in_specs = (P(None, None, "gx", "gy"), P(), P(None, "gx", "gy"), P(None, None, "gx", "gy"))
    out_specs = P(None, None, "gx", "gy")
    return jax.shard_map(shards, mesh=mesh, in_specs=in_specs, out_specs=out_specs, check_vma=False)
```
